32 devices in a mesh: grp: 2 (over y), blk: 4 (over z), rhs: 2 (over x), sub: 2 (over core).
Axes of the slice: x: 2, y: 2, z: 4, core: 2. Of those that a mesh axis runs over, the one named last changes fastest.
Arguments:
- x_panels: bfloat16 [32, 128, 2, 128], P(('grp', 'blk', 'sub'), None, None, 'rhs'), parts along dimension 0, may hold values from -6 to 6
- leaf_basis: bfloat16 [16, 32, 64, 2, 128], P(('blk', 'sub'), 'rhs'), may hold values from -0.375 to 0.375
- leaf_count: int32 [16], P(('blk', 'sub')), may hold values from 1 to 32, as said below
- parent_map: int32 [64], P('rhs'), may hold values from 0 to 15
- up_transfer: bfloat16 [8, 64, 64, 256], P(('blk', 'sub'), 'rhs'), may hold values from -0.375 to 0.375
- mid_perm: int32 [8], replicated, may hold values from 0 to 7, each once
- down_transfer: bfloat16 [4, 2, 32, 2, 64, 256], P(None, 'rhs', ('blk', 'sub')), may hold values from -0.375 to 0.375
- row_basis: bfloat16 [2, 32, 2, 4, 128, 128], P('rhs', ('blk', 'sub')), may hold values from -0.25 to 0.25
Outputs:
- field_out: bfloat16 [4, 32, 2, 128, 2, 128], P(('grp', 'rhs'), ('blk', 'sub')), parts along dimension 0
The draws below stay inside these ranges and needn't reach their ends.
There are 2 independent parts, one for each index of `grp`. The reference program is written for one: setup_inputs(seed, part) draws one part's arguments, and reference() takes and returns one part's arrays. A program takes and returns all parts, laid end to end along the dimension named above; an argument that names none is the same for every part. Nothing has to cross between parts.
Inputs may be any that keep to these rules, and one draw needn't show every extreme that they name: Level-0 directions d >= leaf_count[b] of leaf box b are padding and contribute nothing; in every draw some box has all 32 directions live and some box has one. Level-1 direction j draws from level-0 direction (j // 32) * 16 + parent_map[j]. `mid_perm`: A permutation of the 8 level-1 column groups; entries 2q and 2q + 1 are the children of level-2 column group q.
All inputs are finite; a program needn't handle non-finite values.
Results may differ from the reference program's by a relative error of at most 0.0064.
Values may be sent and summed in bfloat16 or wider, within the bound.
No kernel may reach another device: no remote copies, remote signals or barrier semaphores. Data moves between devices by JAX's collectives and lax.ppermute only.
A program may use at most 64 MiB of HBM per device.

```python
import jax
import jax.numpy as jnp
from jax import lax

RANK = 64
LEAF = 128
NRHS = 128
DIRL = 16
NB = 16
NB1 = 8
NB2 = 4
DGRP = 2
DIR0 = 32
DIR1 = 64


def draw_leaf_count(key, part):
    key = jax.random.fold_in(key, 11)
    first, second = jax.random.split(key, 2)
    counts = jax.random.randint(first, (NB,), 1, DIR0 + 1)
    order = jax.random.permutation(second, NB)
    counts = counts.at[order[0]].set(DIR0)
    counts = counts.at[order[1]].set(1)
    return counts.astype(jnp.int32)


def plant(values, key, low, largest):
    dims = values.shape
    place = [jax.random.randint(jax.random.fold_in(key, axis), (), 0, dims[axis]) for axis in range(len(dims))]
    values = values.at[tuple(place)].set(low)
    longest = dims.index(max(dims))
    place[longest] = (place[longest] + 1) % dims[longest]
    return values.at[tuple(place)].set(largest)


def block_scale(key, extent, shards, least, top_value):
    loudness = 1.0
    for dim, blocks in shards:
        steps = jax.random.uniform(jax.random.fold_in(jax.random.fold_in(key, 6), dim), (blocks,), jnp.float32, least / len(shards), top_value / len(shards))
        loudness = loudness * jnp.repeat(jnp.exp(steps), extent[dim] // blocks).reshape((-1,) + (1,) * (len(extent) - 1 - dim))
    return loudness


def noise(key, shape, deviation, reach, cuts=(), kind=jnp.bfloat16):
    values = deviation * jax.random.normal(key, shape, jnp.float32)
    if cuts:
        values = values * block_scale(key, shape, cuts, -0.22, 0.18)
    return jnp.clip(values, -reach, reach).astype(kind)


def setup_inputs(seed: int = 0, part: int = 0) -> dict:
    streams_of = jax.random.split(jax.random.key(seed), 9)
    part_splits = jax.random.split(jax.random.fold_in(streams_of[8], part), 9)
    x_panels = noise(part_splits[0], (NB, LEAF, 2, NRHS), 1.0, 6.0, ((0, 8), (3, 2)))
    leaf_basis = noise(streams_of[1], (NB, DIR0, RANK, 2, LEAF), (2 * LEAF) ** -0.5, 0.375, ((0, 8), (1, 2)))
    leaf_count = draw_leaf_count(jax.random.fold_in(streams_of[8], 71), part)
    parent_map = plant(jax.random.randint(streams_of[3], (DIR1,), 0, DIRL), jax.random.fold_in(streams_of[3], 1), 0, DIRL - 1).astype(jnp.int32)
    up_transfer = noise(streams_of[4], (NB1, DIR1, RANK, 4 * RANK), (4 * RANK) ** -0.5, 0.375, ((0, 8), (1, 2)))
    mid_perm = jax.random.permutation(streams_of[5], NB1).astype(jnp.int32)
    down_transfer = noise(streams_of[6], (NB2, DGRP, 2 * DIRL, 2, RANK, 4 * RANK), (4 * RANK) ** -0.5, 0.375, ((1, 2), (2, 8)))
    row_basis = noise(streams_of[7], (DGRP, 2 * DIRL, 2, NB2, LEAF, 2 * RANK), (NB2 * 2 * RANK) ** -0.5, 0.25, ((0, 2), (1, 8)))
    return dict(x_panels=x_panels, leaf_basis=leaf_basis, leaf_count=leaf_count, parent_map=parent_map, up_transfer=up_transfer, mid_perm=mid_perm, down_transfer=down_transfer, row_basis=row_basis)


def twisted(values):
    real_part = values[..., 0, :]
    imag_part = values[..., 1, :]
    turned = jnp.stack([-imag_part, real_part], axis=-2)
    return jnp.stack([values, turned], axis=-4)


def reference(x_panels, leaf_basis, leaf_count, parent_map, up_transfer, mid_perm, down_transfer, row_basis):
    group_of = jnp.arange(DIR1, dtype=jnp.int32) // (2 * DIRL)
    parents = (group_of * DIRL + parent_map).astype(jnp.int32)
    x_pairs = x_panels.reshape(NB1, 2, LEAF, 2, NRHS)
    basis_pairs = leaf_basis.reshape(NB1, 2, DIR0, RANK, 2 * LEAF)
    count_pairs = leaf_count.reshape(NB1, 2)

    def lower(items):
        x_pair, basis_pair, count_pair, transfer = items
        spread = twisted(x_pair).reshape(2, 2 * LEAF, 2 * NRHS)
        coeffs = jnp.einsum('sdmk,skn->sdmn', basis_pair.astype(jnp.float32), spread.astype(jnp.float32))
        live = jnp.arange(DIR0, dtype=jnp.int32)[None, :] < count_pair[:, None]
        coeffs = jnp.where(live[:, :, None, None], coeffs, jnp.zeros_like(coeffs)).astype(jnp.bfloat16)
        coeffs = coeffs.reshape(2, DIR0, RANK, 2, NRHS)
        chosen = jnp.take(coeffs, parents, axis=1)
        spread_up = jnp.transpose(twisted(chosen), (1, 0, 2, 3, 4, 5)).reshape(DIR1, 4 * RANK, 2 * NRHS)
        merged = jnp.einsum('jmx,jxn->jmn', transfer.astype(jnp.float32), spread_up.astype(jnp.float32))
        return merged.astype(jnp.bfloat16).reshape(DIR1, RANK, 2, NRHS)

    middle = lax.map(lower, (x_pairs, basis_pairs, count_pairs, up_transfer))
    ordered = jnp.take(middle, mid_perm, axis=0).reshape(NB2, 2, DIR1, RANK, 2, NRHS)
    down_dirs = jnp.moveaxis(down_transfer.reshape(NB2, DIR1, 2, RANK, 4 * RANK), 1, 0)
    row_dirs = row_basis.reshape(DIR1, 2, NB2, LEAF, 2 * RANK)

    def upper(items):
        position, down_block, row_block = items
        column = lax.dynamic_index_in_dim(ordered, position, axis=2, keepdims=False)
        spread = twisted(column).reshape(NB2, 4 * RANK, 2 * NRHS)
        coarse = jnp.einsum('qtmx,qxn->qtmn', down_block.astype(jnp.float32), spread.astype(jnp.float32))
        coarse = coarse.astype(jnp.bfloat16).reshape(NB2, 2, RANK, 2, NRHS)
        spread_row = twisted(coarse).reshape(NB2, 2, 2 * RANK, 2 * NRHS)
        result = jnp.einsum('tqlx,qtxn->tln', row_block.astype(jnp.float32), spread_row.astype(jnp.float32))
        return result.astype(jnp.bfloat16).reshape(2, LEAF, 2, NRHS)

    outputs = lax.map(upper, (jnp.arange(DIR1, dtype=jnp.int32), down_dirs, row_dirs))
    return outputs.reshape(DGRP, 2 * DIRL, 2, LEAF, 2, NRHS)
```

```python
import functools

import jax
import jax.numpy as jnp
from jax import lax
from jax.experimental import pallas as pl
from jax.experimental.pallas import tpu as pltpu
from jax.sharding import PartitionSpec as P

NRHS = 128
HALF = 64
F32 = jnp.float32
BF16 = jnp.bfloat16


def turn(values):
    lane = lax.broadcasted_iota(jnp.int32, values.shape, 1)
    rolled = pltpu.roll(values, HALF, 1)
    return jnp.where(lane < HALF, -rolled, rolled)


def lower_kernel(count_ref, parent_ref, x_ref, basis_ref, up_ref, out_ref, g_ref, leaf_ref):
    boxes, dirs, rows, _ = basis_ref.shape
    rank = rows // 2
    pairs, dirs_up = up_ref.shape[0], up_ref.shape[1]
    dests, _, local, _, _ = out_ref.shape
    first = lax.axis_index("rhs") * dirs
    for b in range(boxes):
        x = x_ref[b]
        spread = jnp.concatenate([x, -x[HALF:], x[:HALF]], axis=0)
        for d in range(dirs):
            slot = b * dirs + d
            g = lax.dot_general(
                basis_ref[b, d], spread, (((1,), (1,)), ((), ())), preferred_element_type=F32
            )
            g_ref[slot, 0] = g[:, :NRHS]
            g_ref[slot, 1] = g[:, NRHS:]
            even = pl.ds(0, rank, stride=2)
            odd = pl.ds(1, rank, stride=2)
            plain = g_ref[slot, 0, even, :] + g_ref[slot, 1, odd, :]
            turned = g_ref[slot, 1, even, :] - g_ref[slot, 0, odd, :]
            live = first + d < count_ref[b]
            plain = jnp.where(live, plain, jnp.zeros_like(plain)).astype(BF16)
            turned = jnp.where(live, turned, jnp.zeros_like(turned)).astype(BF16)
            base = (b % 2) * 2 * rank
            leaf_ref[b // 2, d, base : base + rank, :] = plain
            leaf_ref[b // 2, d, base + rank : base + 2 * rank, :] = turned
    for p in range(pairs):
        for j in range(dirs_up):
            mid = jnp.dot(
                up_ref[p, j], leaf_ref[p, parent_ref[j]], preferred_element_type=F32
            )
            out_ref[j // local, p, j % local] = mid.astype(BF16)


def lower(count, parents, x, basis, up, dests):
    boxes, dirs, rows, _ = basis.shape
    pairs, dirs_up, rank, _ = up.shape
    smem = pl.BlockSpec(memory_space=pltpu.SMEM)
    vmem = pl.BlockSpec(memory_space=pltpu.VMEM)
    return pl.pallas_call(
        lower_kernel,
        out_shape=jax.ShapeDtypeStruct((dests, pairs, dirs_up // dests, rank, NRHS), BF16),
        in_specs=[smem, smem, vmem, vmem, vmem],
        out_specs=vmem,
        scratch_shapes=[
            pltpu.VMEM((boxes * dirs, 2, rows, NRHS), F32),
            pltpu.VMEM((pairs, dirs, 4 * rank, NRHS), BF16),
        ],
        compiler_params=pltpu.CompilerParams(vmem_limit_bytes=32 * 1024 * 1024),
        cost_estimate=pl.CostEstimate(
            flops=400_000_000, bytes_accessed=2_800_000, transcendentals=0
        ),
        name="lower",
    )(count, parents, x, basis, up)


def upper_half(perm_ref, mid_ref, down_ref, row_ref, h):
    groups = down_ref.shape[0]
    rank = mid_ref.shape[2]
    tops = ([], [])
    for q in range(groups):
        parts = []
        for s in range(2):
            mid = mid_ref[perm_ref[2 * q + s], h]
            parts += [mid, turn(mid.astype(F32)).astype(BF16)]
        top = jnp.dot(
            down_ref[q, h], jnp.concatenate(parts, axis=0), preferred_element_type=F32
        )
        for t in range(2):
            piece = top[t * rank : (t + 1) * rank]
            tops[t].extend([piece.astype(BF16), turn(piece).astype(BF16)])
    results = []
    for t in range(2):
        rows = jnp.concatenate([row_ref[h, t, q] for q in range(groups)], axis=1)
        results.append(
            jnp.dot(rows, jnp.concatenate(tops[t], axis=0), preferred_element_type=F32)
        )
    return results


def upper_first_kernel(perm_ref, mid_ref, down_ref, row_ref, out_ref):
    for h in range(out_ref.shape[0]):
        results = upper_half(perm_ref, mid_ref, down_ref, row_ref, h)
        for t in range(2):
            out_ref[h, t] = results[t].astype(BF16)


def upper_last_kernel(own_first, perm_ref, mid_ref, down_ref, row_ref, held_ref, out_ref, mix_ref):
    leaf = held_ref.shape[2]
    if own_first:
        swap = lax.axis_index("rhs") == 1
    for h in range(out_ref.shape[0]):
        results = upper_half(perm_ref, mid_ref, down_ref, row_ref, h)
        for t in range(2):
            low = held_ref[h, t].astype(F32)
            high = results[t]
            if own_first:
                low, high = jnp.where(swap, high, low), jnp.where(swap, low, high)
            lane = lax.broadcasted_iota(jnp.int32, low.shape, 1)
            left = lane < HALF
            real = jnp.where(left, low, pltpu.roll(high, HALF, 1))
            imag = jnp.where(left, pltpu.roll(low, HALF, 1), high)
            mix_ref[h, t, pl.ds(0, leaf, stride=2), :] = real
            mix_ref[h, t, pl.ds(1, leaf, stride=2), :] = imag
            out_ref[h, t] = mix_ref[h, t].astype(BF16)


def upper(perm, mid, down, row, held, own_first):
    groups, local, _, _ = down.shape
    leaf = row.shape[3]
    smem = pl.BlockSpec(memory_space=pltpu.SMEM)
    vmem = pl.BlockSpec(memory_space=pltpu.VMEM)
    params = dict(
        out_specs=vmem,
        compiler_params=pltpu.CompilerParams(vmem_limit_bytes=32 * 1024 * 1024),
        cost_estimate=pl.CostEstimate(
            flops=400_000_000, bytes_accessed=2_800_000, transcendentals=0
        ),
    )
    if held is None:
        return pl.pallas_call(
            upper_first_kernel,
            out_shape=jax.ShapeDtypeStruct((local, 2, leaf, NRHS), BF16),
            in_specs=[smem, vmem, vmem, vmem],
            name="upper_first",
            **params,
        )(perm, mid, down, row)
    return pl.pallas_call(
        functools.partial(upper_last_kernel, own_first),
        out_shape=jax.ShapeDtypeStruct((local, 2, 2 * leaf, NRHS), BF16),
        in_specs=[smem, vmem, vmem, vmem, vmem],
        scratch_shapes=[pltpu.VMEM((local, 2, 2 * leaf, NRHS), F32)],
        name="upper_last",
        **params,
    )(perm, mid, down, row, held)


def on_device(
    dests, x_panels, leaf_basis, leaf_count, parent_map, up_transfer, mid_perm, down_transfer, row_basis
):
    boxes, directions, rank, _, leaf = leaf_basis.shape
    basis = leaf_basis.reshape(boxes, directions, rank * 2, leaf)
    groups, _, local = down_transfer.shape[:3]
    down = down_transfer.reshape(groups, local, 2 * rank, 4 * rank)
    row = row_basis.reshape(local, 2, groups, leaf, 2 * rank)
    flipped = jnp.transpose(x_panels, (0, 2, 3, 1))
    own_first = flipped.shape[2] == HALF
    if own_first:
        other = lax.ppermute(flipped, "rhs", [(0, 1), (1, 0)])
        halves = [flipped, other]
    else:
        whole = lax.all_gather(flipped, "rhs", axis=2, tiled=True)
        halves = [whole[:, :, :HALF], whole[:, :, HALF:]]
    arrived = []
    for half in halves:
        x = half.reshape(boxes, 2 * HALF, leaf)
        mid = lower(leaf_count, parent_map, x, basis, up_transfer, dests)
        moved = lax.all_to_all(mid, ("blk", "sub"), split_axis=0, concat_axis=0, tiled=True)
        arrived.append(moved.reshape(-1, local, rank, NRHS))
    held = upper(mid_perm, arrived[0], down, row, None, own_first)
    result = upper(mid_perm, arrived[1], down, row, held, own_first)
    return result.reshape(1, local, 2, leaf, 2, NRHS)


def solution(mesh):
    dests = mesh.shape["blk"] * mesh.shape["sub"]
    return jax.shard_map(
        functools.partial(on_device, dests),
        mesh=mesh,
        in_specs=(
            P(("grp", "blk", "sub"), None, None, "rhs"),
            P(("blk", "sub"), "rhs", None, None, None),
            P(("blk", "sub")),
            P("rhs"),
            P(("blk", "sub"), "rhs", None, None),
            P(),
            P(None, "rhs", ("blk", "sub"), None, None, None),
            P("rhs", ("blk", "sub"), None, None, None, None),
        ),
        out_specs=P(("grp", "rhs"), ("blk", "sub"), None, None, None, None),
        check_vma=False,
    )
```

```python
import functools

import jax
import jax.numpy as jnp
from jax import lax
from jax.experimental import pallas as pl
from jax.experimental.pallas import tpu as pltpu
from jax.sharding import PartitionSpec as P

NRHS = 128
HALF = 64
F32 = jnp.float32
BF16 = jnp.bfloat16


def turn(values):
    lane = lax.broadcasted_iota(jnp.int32, values.shape, 1)
    rolled = pltpu.roll(values, HALF, 1)
    return jnp.where(lane < HALF, -rolled, rolled)


def lower_body(me, order, count_ref, parent_ref, x_ref, basis_ref, up_ref, outs, g_ref, leaf_ref, ready):
    boxes, dirs, rows, _ = basis_ref.shape
    rank = rows // 2
    pairs = up_ref.shape[0]
    local = outs[0].shape[1]
    first = lax.axis_index("rhs") * dirs
    even = pl.ds(0, rank, stride=2)
    odd = pl.ds(1, rank, stride=2)
    ready("start")
    for b in range(boxes):
        ready(b)
        x = x_ref[b]
        spread = jnp.concatenate([x, -x[HALF:], x[:HALF]], axis=0)
        for d in range(dirs):
            slot = b * dirs + d
            g = lax.dot_general(
                basis_ref[b, d], spread, (((1,), (1,)), ((), ())), preferred_element_type=F32
            )
            g_ref[slot, 0] = g[:, :NRHS]
            g_ref[slot, 1] = g[:, NRHS:]
            plain = g_ref[slot, 0, even, :] + g_ref[slot, 1, odd, :]
            turned = g_ref[slot, 1, even, :] - g_ref[slot, 0, odd, :]
            live = first + d < count_ref[b]
            plain = jnp.where(live, plain, jnp.zeros_like(plain)).astype(BF16)
            turned = jnp.where(live, turned, jnp.zeros_like(turned)).astype(BF16)
            base = (b % 2) * 2 * rank
            leaf_ref[b // 2, d, base : base + rank, :] = plain
            leaf_ref[b // 2, d, base + rank : base + 2 * rank, :] = turned
    ready("up")
    for out_ref, k in zip(outs, order):
        dest = jnp.bitwise_xor(me, k)
        for p in range(pairs):
            for h in range(local):
                j = dest * local + h
                mid = jnp.dot(
                    up_ref[p, j], leaf_ref[p, parent_ref[j]], preferred_element_type=F32
                )
                out_ref[p, h] = mid.astype(BF16)


def position():
    return lax.axis_index("blk") * lax.axis_size("sub") + lax.axis_index("sub")


def lower_cold_kernel(order, count_hbm, parent_hbm, x_hbm, basis_hbm, up_hbm, *refs):
    n = len(order)
    outs = refs[:n]
    g_ref, leaf_ref, count_ref, parent_ref, x_ref, basis_ref, up_ref, sems = refs[n:]
    boxes = basis_ref.shape[0]
    copies = {
        "x": pltpu.make_async_copy(x_hbm, x_ref, sems.at[0]),
        "count": pltpu.make_async_copy(count_hbm, count_ref, sems.at[1]),
        "parent": pltpu.make_async_copy(parent_hbm, parent_ref, sems.at[2]),
        "up": pltpu.make_async_copy(up_hbm, up_ref, sems.at[3]),
    }
    for b in range(boxes):
        copies[b] = pltpu.make_async_copy(basis_hbm.at[b], basis_ref.at[b], sems.at[4 + b])
    for name in ["x", 0, "count"] + list(range(1, boxes)) + ["up", "parent"]:
        copies[name].start()

    def ready(name):
        for other in {"start": ["x", "count"], "up": ["up", "parent"]}.get(name, [name]):
            copies[other].wait()

    lower_body(
        position(), order, count_ref, parent_ref, x_ref, basis_ref, up_ref, outs, g_ref, leaf_ref, ready
    )


def lower_warm_kernel(order, count_ref, parent_ref, x_ref, basis_ref, up_ref, *refs):
    n = len(order)
    outs = refs[:n]
    g_ref, leaf_ref = refs[n:]
    lower_body(
        position(), order, count_ref, parent_ref, x_ref, basis_ref, up_ref, outs, g_ref, leaf_ref, lambda name: None
    )


def lower(order, cold, count, parents, x, basis, up):
    boxes, dirs, rows, leaf = basis.shape
    pairs, dirs_up, rank, _ = up.shape
    smem = pl.BlockSpec(memory_space=pltpu.SMEM)
    vmem = pl.BlockSpec(memory_space=pltpu.VMEM)
    hbm = pl.BlockSpec(memory_space=pltpu.HBM)
    scratch = [
        pltpu.VMEM((boxes * dirs, 2, rows, NRHS), F32),
        pltpu.VMEM((pairs, dirs, 4 * rank, NRHS), BF16),
    ]
    if cold:
        scratch += [
            pltpu.SMEM(count.shape, jnp.int32),
            pltpu.SMEM(parents.shape, jnp.int32),
            pltpu.VMEM(x.shape, BF16),
            pltpu.VMEM(basis.shape, BF16),
            pltpu.VMEM(up.shape, BF16),
            pltpu.SemaphoreType.DMA((4 + boxes,)),
        ]
    block = jax.ShapeDtypeStruct((pairs, dirs_up // len(order), rank, NRHS), BF16)
    return pl.pallas_call(
        functools.partial(lower_cold_kernel if cold else lower_warm_kernel, order),
        out_shape=[block] * len(order),
        in_specs=[hbm] * 5 if cold else [smem, smem, vmem, vmem, vmem],
        out_specs=[vmem] * len(order),
        scratch_shapes=scratch,
        compiler_params=pltpu.CompilerParams(vmem_limit_bytes=32 * 1024 * 1024),
        cost_estimate=pl.CostEstimate(
            flops=400_000_000, bytes_accessed=2_800_000, transcendentals=0
        ),
        name="lower_cold" if cold else "lower_warm",
    )(count, parents, x, basis, up)


def gather_mids(order, mids, spread_ref):
    me = position()
    pairs, local, rank, _ = mids[0].shape
    for mid_ref, k in zip(mids, order):
        source = jnp.bitwise_xor(me, k)
        for p in range(pairs):
            for h in range(local):
                mid = mid_ref[p, h]
                spread_ref[source * pairs + p, h, :rank] = mid
                spread_ref[source * pairs + p, h, rank:] = turn(mid.astype(F32)).astype(BF16)


def upper_half(perm_ref, spread_ref, down_ref, row_ref, h):
    groups = down_ref.shape[0]
    rank = spread_ref.shape[2] // 2
    tops = ([], [])
    for q in range(groups):
        parts = [spread_ref[perm_ref[2 * q + s], h] for s in range(2)]
        top = jnp.dot(
            down_ref[q, h], jnp.concatenate(parts, axis=0), preferred_element_type=F32
        )
        for t in range(2):
            piece = top[t * rank : (t + 1) * rank]
            tops[t].extend([piece.astype(BF16), turn(piece).astype(BF16)])
    results = []
    for t in range(2):
        rows = jnp.concatenate([row_ref[h, t, q] for q in range(groups)], axis=1)
        results.append(
            jnp.dot(rows, jnp.concatenate(tops[t], axis=0), preferred_element_type=F32)
        )
    return results


def upper_first_kernel(order, perm_ref, down_ref, row_ref, *refs):
    n = len(order)
    mids, out_ref, spread_ref = refs[:n], refs[n], refs[n + 1]
    gather_mids(order, mids, spread_ref)
    for h in range(out_ref.shape[0]):
        results = upper_half(perm_ref, spread_ref, down_ref, row_ref, h)
        for t in range(2):
            out_ref[h, t] = results[t].astype(BF16)


def upper_last_kernel(order, own_first, perm_ref, down_ref, row_ref, held_ref, *refs):
    n = len(order)
    mids, out_ref, spread_ref, mix_ref = refs[:n], refs[n], refs[n + 1], refs[n + 2]
    leaf = held_ref.shape[2]
    gather_mids(order, mids, spread_ref)
    if own_first:
        swap = lax.axis_index("rhs") == 1
    for h in range(out_ref.shape[0]):
        results = upper_half(perm_ref, spread_ref, down_ref, row_ref, h)
        for t in range(2):
            low = held_ref[h, t].astype(F32)
            high = results[t]
            if own_first:
                low, high = jnp.where(swap, high, low), jnp.where(swap, low, high)
            lane = lax.broadcasted_iota(jnp.int32, low.shape, 1)
            left = lane < HALF
            real = jnp.where(left, low, pltpu.roll(high, HALF, 1))
            imag = jnp.where(left, pltpu.roll(low, HALF, 1), high)
            mix_ref[h, t, pl.ds(0, leaf, stride=2), :] = real
            mix_ref[h, t, pl.ds(1, leaf, stride=2), :] = imag
            out_ref[h, t] = mix_ref[h, t].astype(BF16)


def upper(order, perm, mids, down, row, held, own_first):
    groups, local, _, width = down.shape
    leaf = row.shape[3]
    smem = pl.BlockSpec(memory_space=pltpu.SMEM)
    vmem = pl.BlockSpec(memory_space=pltpu.VMEM)
    params = dict(
        out_specs=vmem,
        compiler_params=pltpu.CompilerParams(vmem_limit_bytes=32 * 1024 * 1024),
        cost_estimate=pl.CostEstimate(
            flops=400_000_000, bytes_accessed=2_800_000, transcendentals=0
        ),
    )
    spread = pltpu.VMEM((2 * groups, local, width // 2, NRHS), BF16)
    n = len(mids)
    if held is None:
        return pl.pallas_call(
            functools.partial(upper_first_kernel, order),
            out_shape=jax.ShapeDtypeStruct((local, 2, leaf, NRHS), BF16),
            in_specs=[smem] + [vmem] * (2 + n),
            scratch_shapes=[spread],
            name="upper_first",
            **params,
        )(perm, down, row, *mids)
    return pl.pallas_call(
        functools.partial(upper_last_kernel, order, own_first),
        out_shape=jax.ShapeDtypeStruct((local, 2, 2 * leaf, NRHS), BF16),
        in_specs=[smem] + [vmem] * (3 + n),
        scratch_shapes=[spread, pltpu.VMEM((local, 2, 2 * leaf, NRHS), F32)],
        name="upper_last",
        **params,
    )(perm, down, row, held, *mids)


def on_device(
    dests, x_panels, leaf_basis, leaf_count, parent_map, up_transfer, mid_perm, down_transfer, row_basis
):
    boxes, directions, rank, _, leaf = leaf_basis.shape
    basis = leaf_basis.reshape(boxes, directions, rank * 2, leaf)
    groups, _, local = down_transfer.shape[:3]
    down = down_transfer.reshape(groups, local, 2 * rank, 4 * rank)
    row = row_basis.reshape(local, 2, groups, leaf, 2 * rank)
    flipped = jnp.transpose(x_panels, (0, 2, 3, 1))
    own_first = flipped.shape[2] == HALF
    order = tuple(range(dests - 1, -1, -1))
    if own_first:
        halves = [flipped, lax.ppermute(flipped, "rhs", [(0, 1), (1, 0)])]
    else:
        whole = lax.all_gather(flipped, "rhs", axis=2, tiled=True)
        halves = [whole[:, :, :HALF], whole[:, :, HALF:]]
    arrived = []
    for i, half in enumerate(halves):
        x = half.reshape(boxes, 2 * HALF, leaf)
        mids = lower(order, i == 0, leaf_count, parent_map, x, basis, up_transfer)
        if i == 0:
            mids, halves[1] = lax.optimization_barrier((mids, halves[1]))
        moved = []
        for mid, k in zip(mids, order):
            if k:
                pairs = [(m, m ^ k) for m in range(dests)]
                mid = lax.ppermute(mid, ("blk", "sub"), pairs)
            moved.append(mid)
        arrived.append(moved)
    held = upper(order, mid_perm, arrived[0], down, row, None, own_first)
    result = upper(order, mid_perm, arrived[1], down, row, held, own_first)
    return result.reshape(1, local, 2, leaf, 2, NRHS)


def solution(mesh):
    dests = mesh.shape["blk"] * mesh.shape["sub"]
    return jax.shard_map(
        functools.partial(on_device, dests),
        mesh=mesh,
        in_specs=(
            P(("grp", "blk", "sub"), None, None, "rhs"),
            P(("blk", "sub"), "rhs", None, None, None),
            P(("blk", "sub")),
            P("rhs"),
            P(("blk", "sub"), "rhs", None, None),
            P(),
            P(None, "rhs", ("blk", "sub"), None, None, None),
            P("rhs", ("blk", "sub"), None, None, None, None),
        ),
        out_specs=P(("grp", "rhs"), ("blk", "sub"), None, None, None, None),
        check_vma=False,
    )
```

```python
import functools

import jax
import jax.numpy as jnp
from jax import lax
from jax.experimental import pallas as pl
from jax.experimental.pallas import tpu as pltpu
from jax.sharding import PartitionSpec as P

NRHS = 128
HALF = 64
F32 = jnp.float32
BF16 = jnp.bfloat16


def turn(values):
    lane = lax.broadcasted_iota(jnp.int32, values.shape, 1)
    rolled = pltpu.roll(values, HALF, 1)
    return jnp.where(lane < HALF, -rolled, rolled)


def lower_body(jobs, count_ref, parent_ref, x_ref, basis_ref, up_ref, g_ref, leaf_ref, ready):
    boxes, dirs, rows, _ = basis_ref.shape
    rank = rows // 2
    first = lax.axis_index("rhs") * dirs
    even = pl.ds(0, rank, stride=2)
    odd = pl.ds(1, rank, stride=2)
    ready("start")
    for b in range(boxes):
        ready(b)
        x = x_ref[b]
        spread = jnp.concatenate([x, -x[HALF:], x[:HALF]], axis=0)
        for d in range(dirs):
            slot = b * dirs + d
            g = lax.dot_general(
                basis_ref[b, d], spread, (((1,), (1,)), ((), ())), preferred_element_type=F32
            )
            g_ref[slot, 0] = g[:, :NRHS]
            g_ref[slot, 1] = g[:, NRHS:]
            plain = g_ref[slot, 0, even, :] + g_ref[slot, 1, odd, :]
            turned = g_ref[slot, 1, even, :] - g_ref[slot, 0, odd, :]
            live = first + d < count_ref[b]
            plain = jnp.where(live, plain, jnp.zeros_like(plain)).astype(BF16)
            turned = jnp.where(live, turned, jnp.zeros_like(turned)).astype(BF16)
            base = (b % 2) * 2 * rank
            leaf_ref[b // 2, d, base : base + rank, :] = plain
            leaf_ref[b // 2, d, base + rank : base + 2 * rank, :] = turned
    ready("up")
    for out_ref, p, j in jobs:
        mid = jnp.dot(up_ref[p, j], leaf_ref[p, parent_ref[j]], preferred_element_type=F32)
        out_ref[...] = mid.astype(BF16)


def both_cores(order):
    return [(k, which) for k in order for which in (0, 1)]


def target(k, which, h, local):
    z = jnp.bitwise_xor(lax.axis_index("blk"), k)
    core = jnp.bitwise_xor(lax.axis_index("sub"), which)
    return (z * 2 + core) * local + h


def lower_cold_kernel(order, count_hbm, parent_hbm, x_hbm, basis_hbm, up_hbm, *refs):
    n = len(order)
    outs = refs[:n]
    g_ref, leaf_ref, count_ref, parent_ref, x_ref, basis_ref, up_ref, sems = refs[n:]
    boxes = basis_ref.shape[0]
    pairs, local = outs[0].shape[1:3]
    copies = {
        "x": pltpu.make_async_copy(x_hbm, x_ref, sems.at[0]),
        "count": pltpu.make_async_copy(count_hbm, count_ref, sems.at[1]),
        "parent": pltpu.make_async_copy(parent_hbm, parent_ref, sems.at[2]),
        "up": pltpu.make_async_copy(up_hbm, up_ref, sems.at[3]),
    }
    for b in range(boxes):
        copies[b] = pltpu.make_async_copy(basis_hbm.at[b], basis_ref.at[b], sems.at[4 + b])
    for name in ["x", 0, "count"] + list(range(1, boxes)) + ["up", "parent"]:
        copies[name].start()

    def ready(name):
        for other in {"start": ["x", "count"], "up": ["up", "parent"]}.get(name, [name]):
            copies[other].wait()

    jobs = [
        (out.at[which, p, h], p, target(k, which, h, local))
        for out, k in zip(outs, order)
        for which in range(2)
        for p in range(pairs)
        for h in range(local)
    ]
    lower_body(jobs, count_ref, parent_ref, x_ref, basis_ref, up_ref, g_ref, leaf_ref, ready)


def lower_warm_kernel(routes, count_ref, parent_ref, x_ref, basis_ref, up_ref, *refs):
    n = len(routes)
    outs = refs[:n]
    g_ref, leaf_ref = refs[n:]
    pairs, local = outs[0].shape[:2]
    jobs = [
        (out.at[p, h], p, target(k, which, h, local))
        for out, (k, which) in zip(outs, routes)
        for p in range(pairs)
        for h in range(local)
    ]
    lower_body(
        jobs, count_ref, parent_ref, x_ref, basis_ref, up_ref, g_ref, leaf_ref, lambda name: None
    )


def lower(order, cold, count, parents, x, basis, up):
    boxes, dirs, rows, leaf = basis.shape
    pairs, dirs_up, rank, _ = up.shape
    local = dirs_up // (2 * len(order))
    args = [count, parents, x, basis, up]
    smem = pl.BlockSpec(memory_space=pltpu.SMEM)
    vmem = pl.BlockSpec(memory_space=pltpu.VMEM)
    hbm = pl.BlockSpec(memory_space=pltpu.HBM)
    scratch = [
        pltpu.VMEM((boxes * dirs, 2, rows, NRHS), F32),
        pltpu.VMEM((pairs, dirs, 4 * rank, NRHS), BF16),
    ]
    if cold:
        scratch += [
            pltpu.SMEM(count.shape, jnp.int32),
            pltpu.SMEM(parents.shape, jnp.int32),
            pltpu.VMEM(x.shape, BF16),
            pltpu.VMEM(basis.shape, BF16),
            pltpu.VMEM(up.shape, BF16),
            pltpu.SemaphoreType.DMA((4 + boxes,)),
        ]
        kernel = functools.partial(lower_cold_kernel, order)
        blocks = [pltpu.VMEM((2, pairs, local, rank, NRHS), BF16)] * len(order)
        args = [pltpu.with_memory_space_constraint(arg, pltpu.HBM) for arg in args]
    else:
        routes = both_cores(order)
        kernel = functools.partial(lower_warm_kernel, routes)
        blocks = [pltpu.VMEM((pairs, local, rank, NRHS), BF16)] * len(routes)
    return pl.pallas_call(
        kernel,
        out_shape=blocks,
        in_specs=[hbm] * 5 if cold else [smem, smem, vmem, vmem, vmem],
        out_specs=[vmem] * len(blocks),
        scratch_shapes=scratch,
        compiler_params=pltpu.CompilerParams(
            vmem_limit_bytes=32 * 1024 * 1024
        ),
        cost_estimate=pl.CostEstimate(
            flops=1_000_000, bytes_accessed=10_000, transcendentals=0
        ),
        name="lower_cold" if cold else "lower_warm",
    )(*args)


def collect_kernel(first_ref, second_ref, *refs):
    ins, out_ref = refs[:-1], refs[-1]
    for i, ref in enumerate(ins):
        out_ref[i] = ref[1]


def collect(after, blocks):
    vmem = pl.BlockSpec(memory_space=pltpu.VMEM)
    return pl.pallas_call(
        collect_kernel,
        out_shape=jax.ShapeDtypeStruct((len(blocks),) + blocks[0].shape[1:], BF16),
        in_specs=[pl.BlockSpec(memory_space=pl.ANY)] * 2 + [vmem] * len(blocks),
        out_specs=vmem,
        name="collect",
    )(*after, *blocks)


def spread_mid(mid_ref, k, which, spread_ref):
    pairs, local, rank, _ = mid_ref.shape
    z = jnp.bitwise_xor(lax.axis_index("blk"), k)
    core = jnp.bitwise_xor(lax.axis_index("sub"), which)
    for p in range(pairs):
        source = (z * 2 + core) * pairs + p
        for h in range(local):
            mid = mid_ref[p, h]
            spread_ref[source, h, :rank] = mid
            spread_ref[source, h, rank:] = turn(mid.astype(F32)).astype(BF16)


def upper_half(perm_ref, spread_ref, down_ref, row_ref, h):
    groups = down_ref.shape[0]
    rank = spread_ref.shape[2] // 2
    tops = ([], [])
    for q in range(groups):
        parts = [spread_ref[perm_ref[2 * q + s], h] for s in range(2)]
        top = jnp.dot(
            down_ref[q, h], jnp.concatenate(parts, axis=0), preferred_element_type=F32
        )
        for t in range(2):
            piece = top[t * rank : (t + 1) * rank]
            tops[t].extend([piece.astype(BF16), turn(piece).astype(BF16)])
    results = []
    for t in range(2):
        rows = jnp.concatenate([row_ref[h, t, q] for q in range(groups)], axis=1)
        results.append(
            jnp.dot(rows, jnp.concatenate(tops[t], axis=0), preferred_element_type=F32)
        )
    return results


def upper_first_kernel(order, perm_ref, down_ref, row_ref, got_ref, *refs):
    n = len(order)
    mids, out_ref, spread_ref = refs[:n], refs[n], refs[n + 1]
    for i, k in enumerate(order):
        spread_mid(mids[i].at[0], k, 0, spread_ref)
        spread_mid(got_ref.at[i], k, 1, spread_ref)
    for h in range(out_ref.shape[0]):
        results = upper_half(perm_ref, spread_ref, down_ref, row_ref, h)
        for t in range(2):
            out_ref[h, t] = results[t].astype(BF16)


def upper_last_kernel(order, own_first, perm_ref, down_ref, row_ref, held_ref, *refs):
    routes = both_cores(order)
    n = len(routes)
    mids, out_ref, spread_ref, mix_ref = refs[:n], refs[n], refs[n + 1], refs[n + 2]
    leaf = held_ref.shape[2]
    for mid_ref, (k, which) in zip(mids, routes):
        spread_mid(mid_ref, k, which, spread_ref)
    if own_first:
        swap = lax.axis_index("rhs") == 1
    for h in range(out_ref.shape[0]):
        results = upper_half(perm_ref, spread_ref, down_ref, row_ref, h)
        for t in range(2):
            low = held_ref[h, t].astype(F32)
            high = results[t]
            if own_first:
                low, high = jnp.where(swap, high, low), jnp.where(swap, low, high)
            lane = lax.broadcasted_iota(jnp.int32, low.shape, 1)
            left = lane < HALF
            real = jnp.where(left, low, pltpu.roll(high, HALF, 1))
            imag = jnp.where(left, pltpu.roll(low, HALF, 1), high)
            mix_ref[h, t, pl.ds(0, leaf, stride=2), :] = real
            mix_ref[h, t, pl.ds(1, leaf, stride=2), :] = imag
            out_ref[h, t] = mix_ref[h, t].astype(BF16)


def upper(order, perm, mids, down, row, other, last, own_first):
    groups, local, _, width = down.shape
    leaf = row.shape[3]
    smem = pl.BlockSpec(memory_space=pltpu.SMEM)
    vmem = pl.BlockSpec(memory_space=pltpu.VMEM)
    spread = pltpu.VMEM((2 * groups, local, width // 2, NRHS), BF16)
    if last:
        kernel = functools.partial(upper_last_kernel, order, own_first)
        rows = 2 * leaf
        scratch = [spread, pltpu.VMEM((local, 2, rows, NRHS), F32)]
    else:
        kernel = functools.partial(upper_first_kernel, order)
        rows = leaf
        scratch = [spread]
    return pl.pallas_call(
        kernel,
        out_shape=jax.ShapeDtypeStruct((local, 2, rows, NRHS), BF16),
        in_specs=[smem] + [vmem] * (3 + len(mids)),
        out_specs=vmem,
        scratch_shapes=scratch,
        compiler_params=pltpu.CompilerParams(vmem_limit_bytes=32 * 1024 * 1024),
        cost_estimate=pl.CostEstimate(
            flops=1_000_000, bytes_accessed=10_000, transcendentals=0
        ),
        name="upper_last" if last else "upper_first",
    )(perm, down, row, other, *mids)


def along_blk(blocks, order):
    moved = []
    for block, k in zip(blocks, order):
        if k:
            block = lax.ppermute(block, "blk", [(m, m ^ k) for m in range(len(order))])
        moved.append(block)
    return moved


def direct(blocks, order):
    moved = []
    for block, (k, which) in zip(blocks, both_cores(order)):
        code = 2 * k + which
        if code:
            pairs = [(m, m ^ code) for m in range(2 * len(order))]
            block = lax.ppermute(block, ("blk", "sub"), pairs)
        moved.append(block)
    return moved


def on_device(
    columns, x_panels, leaf_basis, leaf_count, parent_map, up_transfer, mid_perm, down_transfer, row_basis
):
    boxes, directions, rank, _, leaf = leaf_basis.shape
    basis = leaf_basis.reshape(boxes, directions, rank * 2, leaf)
    groups, _, local = down_transfer.shape[:3]
    down = down_transfer.reshape(groups, local, 2 * rank, 4 * rank)
    row = row_basis.reshape(local, 2, groups, leaf, 2 * rank)
    flipped = jnp.transpose(x_panels, (0, 2, 3, 1))
    own_first = flipped.shape[2] == HALF
    order = tuple(range(columns - 1, -1, -1))
    swap = [(0, 1), (1, 0)]
    if own_first:
        first, second = flipped, flipped
    else:
        whole = lax.all_gather(flipped, "rhs", axis=2, tiled=True)
        first, second = whole[:, :, :HALF], whole[:, :, HALF:]
    first = first.reshape(boxes, 2 * HALF, leaf)
    blocks = lower(order, True, leaf_count, parent_map, first, basis, up_transfer)
    if own_first:
        blocks, second = lax.optimization_barrier((blocks, second))
        second = lax.ppermute(second, "rhs", swap)
    moved = along_blk(blocks, order)
    second = second.reshape(boxes, 2 * HALF, leaf)
    blocks = lower(order, False, leaf_count, parent_map, second, basis, up_transfer)
    blocks = direct(blocks, order)
    got = lax.ppermute(collect(blocks[:2], moved), "sub", swap)
    held = upper(order, mid_perm, moved, down, row, got, False, own_first)
    result = upper(order, mid_perm, blocks, down, row, held, True, own_first)
    return result.reshape(1, local, 2, leaf, 2, NRHS)


def solution(mesh):
    return jax.shard_map(
        functools.partial(on_device, mesh.shape["blk"]),
        mesh=mesh,
        in_specs=(
            P(("grp", "blk", "sub"), None, None, "rhs"),
            P(("blk", "sub"), "rhs", None, None, None),
            P(("blk", "sub")),
            P("rhs"),
            P(("blk", "sub"), "rhs", None, None),
            P(),
            P(None, "rhs", ("blk", "sub"), None, None, None),
            P("rhs", ("blk", "sub"), None, None, None, None),
        ),
        out_specs=P(("grp", "rhs"), ("blk", "sub"), None, None, None, None),
        check_vma=False,
    )
```

```python
import functools

import jax
import jax.numpy as jnp
from jax import lax
from jax.experimental import pallas as pl
from jax.experimental.pallas import tpu as pltpu
from jax.sharding import PartitionSpec as P

NRHS = 128
F32 = jnp.float32
BF16 = jnp.bfloat16
PARAMS = pltpu.CompilerParams(vmem_limit_bytes=32 * 1024 * 1024)
COST = pl.CostEstimate(flops=1_000_000, bytes_accessed=10_000, transcendentals=0)


def both_cores(steps):
    return [(k, which) for k in steps for which in (0, 1)]


def partner(k, which):
    z = jnp.bitwise_xor(lax.axis_index("blk"), k)
    core = jnp.bitwise_xor(lax.axis_index("sub"), which)
    return z * 2 + core


def load_kernel(basis_hbm, up_hbm, basis_ref, up_ref, sems):
    copies = [
        pltpu.make_async_copy(basis_hbm, basis_ref, sems.at[0]),
        pltpu.make_async_copy(up_hbm, up_ref, sems.at[1]),
    ]
    for copy in copies:
        copy.start()
    for copy in copies:
        copy.wait()


def load(*arrays):
    return pl.pallas_call(
        load_kernel,
        out_shape=[pltpu.VMEM(array.shape, array.dtype) for array in arrays],
        in_specs=[pl.BlockSpec(memory_space=pltpu.HBM)] * len(arrays),
        out_specs=[pl.BlockSpec(memory_space=pltpu.VMEM)] * len(arrays),
        scratch_shapes=[pltpu.SemaphoreType.DMA((len(arrays),))],
        compiler_params=PARAMS,
        cost_estimate=COST,
        name="load",
    )(*[pltpu.with_memory_space_constraint(array, pltpu.HBM) for array in arrays])


def up_stage(outs, routes, parent_ref, up_ref, leaf_ref):
    pairs, local = outs[0].shape[:2]
    for out, (k, which) in zip(outs, routes):
        dest = partner(k, which)
        for p in range(pairs):
            for h in range(local):
                j = dest * local + h
                mid = jnp.dot(
                    up_ref[p, j], leaf_ref[p, parent_ref[j]], preferred_element_type=F32
                )
                out[p, h] = mid.astype(BF16)


def lower_kernel(routes, count_ref, parent_ref, *refs):
    n = len(routes)
    xs, (basis_ref, up_ref) = refs[: -n - 4], refs[-n - 4 : -n - 2]
    outs, leaf_ref, g_ref = refs[-n - 2 : -2], refs[-2], refs[-1]
    boxes, dirs, rows, _ = basis_ref.shape
    rank = rows // 2
    first = lax.axis_index("rhs") * dirs
    even = pl.ds(0, rank, stride=2)
    odd = pl.ds(1, rank, stride=2)
    for b in range(boxes):
        if len(xs) == 2:
            own, other = xs[0][b], xs[1][b]
            swap = lax.axis_index("rhs") == 1
            low, high = jnp.where(swap, other, own), jnp.where(swap, own, other)
            spread = jnp.concatenate([low[0], high[0], low[1], high[1]], axis=0)
        else:
            spread = jnp.concatenate([xs[0][b, 0], xs[0][b, 1]], axis=0)
        for d in range(dirs):
            slot = b * dirs + d
            g = lax.dot_general(
                basis_ref[b, d], spread, (((1,), (1,)), ((), ())), preferred_element_type=F32
            )
            g_ref[slot, 0] = g[:, :NRHS]
            g_ref[slot, 1] = g[:, NRHS:]
            real = g_ref[slot, 0, even, :] - g_ref[slot, 1, odd, :]
            imag = g_ref[slot, 1, even, :] + g_ref[slot, 0, odd, :]
            live = first + d < count_ref[b]
            real = jnp.where(live, real, jnp.zeros_like(real)).astype(BF16)
            imag = jnp.where(live, imag, jnp.zeros_like(imag)).astype(BF16)
            base = (b % 2) * 2 * rank
            leaf_ref[b // 2, d, base : base + rank, :NRHS] = real
            leaf_ref[b // 2, d, base : base + rank, NRHS:] = imag
            leaf_ref[b // 2, d, base + rank : base + 2 * rank, :NRHS] = -imag
            leaf_ref[b // 2, d, base + rank : base + 2 * rank, NRHS:] = real
    up_stage(outs, routes, parent_ref, up_ref, leaf_ref)


def lower(routes, dests, count, parents, xs, basis, up):
    boxes, dirs, rows, _ = basis.shape
    pairs, dirs_up, rank, _ = up.shape
    block = pltpu.VMEM((pairs, dirs_up // dests, rank, 2 * NRHS), BF16)
    smem = pl.BlockSpec(memory_space=pltpu.SMEM)
    vmem = pl.BlockSpec(memory_space=pltpu.VMEM)
    return pl.pallas_call(
        functools.partial(lower_kernel, routes),
        out_shape=[block] * len(routes) + [pltpu.VMEM((pairs, dirs, 4 * rank, 2 * NRHS), BF16)],
        in_specs=[smem, smem] + [vmem] * (2 + len(xs)),
        out_specs=[vmem] * (len(routes) + 1),
        scratch_shapes=[pltpu.VMEM((boxes * dirs, 2, rows, NRHS), F32)],
        compiler_params=PARAMS,
        cost_estimate=COST,
        name="lower",
    )(count, parents, *xs, basis, up)


def rest_kernel(routes, parent_ref, up_ref, leaf_ref, *outs):
    up_stage(outs, routes, parent_ref, up_ref, leaf_ref)


def rest(routes, dests, parents, up, leaf):
    pairs, dirs_up, rank, _ = up.shape
    block = pltpu.VMEM((pairs, dirs_up // dests, rank, 2 * NRHS), BF16)
    smem = pl.BlockSpec(memory_space=pltpu.SMEM)
    vmem = pl.BlockSpec(memory_space=pltpu.VMEM)
    return pl.pallas_call(
        functools.partial(rest_kernel, routes),
        out_shape=[block] * len(routes),
        in_specs=[smem, vmem, vmem],
        out_specs=[vmem] * len(routes),
        compiler_params=PARAMS,
        cost_estimate=COST,
        name="rest",
    )(parents, up, leaf)


def upper_kernel(routes, perm_hbm, down_ref, row_ref, *refs):
    n = len(routes)
    mids = refs[:n]
    out_hbm, spread_ref, mix_ref, out_ref, perm_ref, sems = refs[n:]
    groups, local = down_ref.shape[:2]
    rank = spread_ref.shape[2] // 2
    leaf = row_ref.shape[3]
    fetch = pltpu.make_async_copy(perm_hbm, perm_ref, sems.at[local])
    fetch.start()
    for mid_ref, (k, which) in zip(mids, routes):
        pairs = mid_ref.shape[0]
        for p in range(pairs):
            source = partner(k, which) * pairs + p
            for h in range(local):
                mid = mid_ref[p, h]
                spread_ref[source, h, :rank] = mid
                spread_ref[source, h, rank:, :NRHS] = -mid[:, NRHS:]
                spread_ref[source, h, rank:, NRHS:] = mid[:, :NRHS]
    fetch.wait()
    copies = []
    for h in range(local):
        tops = ([], [])
        for q in range(groups):
            parts = [spread_ref[perm_ref[2 * q + s], h] for s in range(2)]
            top = jnp.dot(
                down_ref[q, h], jnp.concatenate(parts, axis=0), preferred_element_type=F32
            ).astype(BF16)
            for t in range(2):
                piece = top[t * rank : (t + 1) * rank]
                tops[t].append(piece)
                tops[t].append(jnp.concatenate([-piece[:, NRHS:], piece[:, :NRHS]], axis=1))
        for t in range(2):
            rows = jnp.concatenate([row_ref[h, t, q] for q in range(groups)], axis=1)
            field = jnp.dot(rows, jnp.concatenate(tops[t], axis=0), preferred_element_type=F32)
            mix_ref[h, t, pl.ds(0, leaf, stride=2), :] = field[:, :NRHS]
            mix_ref[h, t, pl.ds(1, leaf, stride=2), :] = field[:, NRHS:]
            out_ref[h, t] = mix_ref[h, t].astype(BF16)
        copies.append(pltpu.make_async_copy(out_ref.at[h], out_hbm.at[h], sems.at[h]))
        copies[-1].start()
    for copy in copies:
        copy.wait()


def upper(routes, perm, down, row, mids):
    groups, local, _, width = down.shape
    leaf = row.shape[3]
    vmem = pl.BlockSpec(memory_space=pltpu.VMEM)
    hbm = pl.BlockSpec(memory_space=pltpu.HBM)
    shape = (local, 2, 2 * leaf, NRHS)
    return pl.pallas_call(
        functools.partial(upper_kernel, routes),
        out_shape=jax.ShapeDtypeStruct(shape, BF16),
        in_specs=[hbm] + [vmem] * (2 + len(mids)),
        out_specs=hbm,
        scratch_shapes=[
            pltpu.VMEM((2 * groups, local, width // 2, 2 * NRHS), BF16),
            pltpu.VMEM(shape, F32),
            pltpu.VMEM(shape, BF16),
            pltpu.SMEM(perm.shape, jnp.int32),
            pltpu.SemaphoreType.DMA((local + 1,)),
        ],
        compiler_params=PARAMS,
        cost_estimate=COST,
        name="upper",
    )(pltpu.with_memory_space_constraint(perm, pltpu.HBM), down, row, *mids)


def send(block, route, dests):
    code = 2 * route[0] + route[1]
    if not code:
        return block
    return lax.ppermute(block, ("blk", "sub"), [(m, m ^ code) for m in range(dests)])


def on_device(
    columns, x_panels, leaf_basis, leaf_count, parent_map, up_transfer, mid_perm, down_transfer, row_basis
):
    boxes, directions, rank, _, leaf = leaf_basis.shape
    basis = leaf_basis.reshape(boxes, directions, rank * 2, leaf)
    groups, _, local = down_transfer.shape[:3]
    down = down_transfer.reshape(groups, local, 2 * rank, 4 * rank)
    row = row_basis.reshape(local, 2, groups, leaf, 2 * rank)
    x = jnp.transpose(x_panels, (0, 2, 3, 1))
    if 2 * x.shape[2] == NRHS:
        xs = [x, lax.ppermute(x, "rhs", [(0, 1), (1, 0)])]
    else:
        xs = [lax.all_gather(x, "rhs", axis=2, tiled=True)]
    basis, up = load(basis, up_transfer)
    dests = 2 * columns
    routes = both_cores(range(columns - 1, -1, -1))
    *early, leaf_coef = lower(routes[:2], dests, leaf_count, parent_map, xs, basis, up)
    late = rest(routes[2:], dests, parent_map, up, leaf_coef)
    mids = [send(block, route, dests) for block, route in zip([*early, *late], routes)]
    result = upper(routes, mid_perm, down, row, mids)
    return result.reshape(1, local, 2, leaf, 2, NRHS)


def solution(mesh):
    return jax.shard_map(
        functools.partial(on_device, mesh.shape["blk"]),
        mesh=mesh,
        in_specs=(
            P(("grp", "blk", "sub"), None, None, "rhs"),
            P(("blk", "sub"), "rhs", None, None, None),
            P(("blk", "sub")),
            P("rhs"),
            P(("blk", "sub"), "rhs", None, None),
            P(),
            P(None, "rhs", ("blk", "sub"), None, None, None),
            P("rhs", ("blk", "sub"), None, None, None, None),
        ),
        out_specs=P(("grp", "rhs"), ("blk", "sub"), None, None, None, None),
        check_vma=False,
    )
```

```python
import functools

import jax
import jax.numpy as jnp
from jax import lax
from jax.experimental import pallas as pl
from jax.experimental.pallas import tpu as pltpu
from jax.sharding import PartitionSpec as P

NRHS = 128
HALF = 64
F32 = jnp.float32
BF16 = jnp.bfloat16
PARAMS = pltpu.CompilerParams(vmem_limit_bytes=32 * 1024 * 1024)
COST = pl.CostEstimate(flops=1_000_000, bytes_accessed=10_000, transcendentals=0)


def both_cores(steps):
    return [(k, which) for k in steps for which in (0, 1)]


def partner(k, which):
    z = jnp.bitwise_xor(lax.axis_index("blk"), k)
    core = jnp.bitwise_xor(lax.axis_index("sub"), which)
    return z * 2 + core


def up_stage(outs, routes, parent_ref, up_ref, leaf_ref, cut=lambda mid: mid):
    pairs, local = outs[0].shape[:2]
    for out, (k, which) in zip(outs, routes):
        dest = partner(k, which)
        for p in range(pairs):
            for h in range(local):
                j = dest * local + h
                mid = jnp.dot(
                    up_ref[p, j], leaf_ref[p, parent_ref[j]], preferred_element_type=F32
                )
                out[p, h] = cut(mid).astype(BF16)


def leaf_stage(spreads, combine, count_ref, basis_ref, g_ref, leaf_ref, ready):
    boxes, dirs, rows, _ = basis_ref.shape
    rank = rows // 2
    width = leaf_ref.shape[3]
    first = lax.axis_index("rhs") * dirs
    even = pl.ds(0, rank, stride=2)
    odd = pl.ds(1, rank, stride=2)
    for b in range(boxes):
        ready(b)
        spread = spreads(b)
        for d in range(dirs):
            slot = b * dirs + d
            g = lax.dot_general(
                basis_ref[b, d], spread, (((1,), (1,)), ((), ())), preferred_element_type=F32
            )
            g_ref[slot, 0] = g[:, :NRHS]
            g_ref[slot, 1] = g[:, NRHS:]
            live = first + d < count_ref[b]
            pieces = combine(
                [g_ref[slot, i, even, :] for i in range(2)],
                [g_ref[slot, i, odd, :] for i in range(2)],
            )
            pieces = [jnp.where(live, x, jnp.zeros_like(x)).astype(BF16) for x in pieces]
            base = (b % 2) * 2 * rank
            top, bottom = slice(base, base + rank), slice(base + rank, base + 2 * rank)
            if width == NRHS:
                leaf_ref[b // 2, d, top, :] = pieces[0]
                leaf_ref[b // 2, d, bottom, :] = pieces[1]
            else:
                leaf_ref[b // 2, d, top, :NRHS] = pieces[0]
                leaf_ref[b // 2, d, top, NRHS:] = pieces[1]
                leaf_ref[b // 2, d, bottom, :NRHS] = -pieces[1]
                leaf_ref[b // 2, d, bottom, NRHS:] = pieces[0]


def half_columns(even, odd):
    return even[0] + odd[1], even[1] - odd[0]


def all_columns(even, odd):
    return even[0] - odd[1], even[1] + odd[0]


def own_kernel(routes, count_hbm, parent_hbm, x_hbm, basis_hbm, up_hbm, *refs):
    n = len(routes)
    outs, basis_ref, up_ref = refs[:n], refs[n], refs[n + 1]
    count_ref, parent_ref, x_ref, leaf_ref, g_ref, sems = refs[n + 2 :]
    boxes = basis_ref.shape[0]
    copies = {
        "x": pltpu.make_async_copy(x_hbm, x_ref, sems.at[0]),
        "count": pltpu.make_async_copy(count_hbm, count_ref, sems.at[1]),
        "parent": pltpu.make_async_copy(parent_hbm, parent_ref, sems.at[2]),
        "up": pltpu.make_async_copy(up_hbm, up_ref, sems.at[3]),
    }
    for b in range(boxes):
        copies[b] = pltpu.make_async_copy(basis_hbm.at[b], basis_ref.at[b], sems.at[4 + b])
    for name in ["x", 0, "count"] + list(range(1, boxes)) + ["up", "parent"]:
        copies[name].start()
    copies["x"].wait()
    copies["count"].wait()

    def spreads(b):
        real, imag = x_ref[b, 0], x_ref[b, 1]
        return jnp.concatenate([real, imag, -imag, real], axis=0)

    leaf_stage(
        spreads, half_columns, count_ref, basis_ref, g_ref, leaf_ref, lambda b: copies[b].wait()
    )
    copies["up"].wait()
    copies["parent"].wait()
    up_stage(outs, routes, parent_ref, up_ref, leaf_ref)


def own(routes, dests, count, parents, x, basis, up):
    boxes, dirs, rows, _ = basis.shape
    pairs, dirs_up, rank, _ = up.shape
    block = pltpu.VMEM((pairs, dirs_up // dests, rank, NRHS), BF16)
    args = [count, parents, x, basis, up]
    return pl.pallas_call(
        functools.partial(own_kernel, routes),
        out_shape=[block] * len(routes)
        + [pltpu.VMEM(basis.shape, BF16), pltpu.VMEM(up.shape, BF16)],
        in_specs=[pl.BlockSpec(memory_space=pltpu.HBM)] * 5,
        out_specs=[pl.BlockSpec(memory_space=pltpu.VMEM)] * (len(routes) + 2),
        scratch_shapes=[
            pltpu.SMEM(count.shape, jnp.int32),
            pltpu.SMEM(parents.shape, jnp.int32),
            pltpu.VMEM(x.shape, BF16),
            pltpu.VMEM((pairs, dirs, 4 * rank, NRHS), BF16),
            pltpu.VMEM((boxes * dirs, 2, rows, NRHS), F32),
            pltpu.SemaphoreType.DMA((4 + boxes,)),
        ],
        compiler_params=PARAMS,
        cost_estimate=COST,
        name="own",
    )(*[pltpu.with_memory_space_constraint(arg, pltpu.HBM) for arg in args])


def other_columns(mid):
    left = lax.broadcasted_iota(jnp.int32, (mid.shape[0], NRHS), 1) < HALF
    real, imag = mid[:, :NRHS], mid[:, NRHS:]
    low = jnp.where(left, real, pltpu.roll(imag, HALF, 1))
    high = jnp.where(left, pltpu.roll(real, HALF, 1), imag)
    return jnp.where(lax.axis_index("rhs") == 1, low, high)


def lower_kernel(full, halved, count_ref, parent_ref, *refs):
    n, m = len(full), len(halved)
    g_ref, leaf_ref = refs[-2:]
    outs = refs[-2 - n - m : -2]
    *xs, basis_ref, up_ref = refs[: -2 - n - m]

    def spreads(b):
        if len(xs) == 1:
            return jnp.concatenate([xs[0][b, 0], xs[0][b, 1]], axis=0)
        own, other = xs[0][b], xs[1][b]
        swap = lax.axis_index("rhs") == 1
        low, high = jnp.where(swap, other, own), jnp.where(swap, own, other)
        return jnp.concatenate([low[0], high[0], low[1], high[1]], axis=0)

    leaf_stage(spreads, all_columns, count_ref, basis_ref, g_ref, leaf_ref, lambda b: None)
    up_stage(outs[:n], full, parent_ref, up_ref, leaf_ref)
    if halved:
        up_stage(outs[n:], halved, parent_ref, up_ref, leaf_ref, other_columns)


def lower(full, halved, dests, count, parents, xs, basis, up):
    boxes, dirs, rows, _ = basis.shape
    pairs, dirs_up, rank, _ = up.shape
    shape = (pairs, dirs_up // dests, rank)
    smem = pl.BlockSpec(memory_space=pltpu.SMEM)
    vmem = pl.BlockSpec(memory_space=pltpu.VMEM)
    n = len(full) + len(halved)
    return pl.pallas_call(
        functools.partial(lower_kernel, full, halved),
        out_shape=[pltpu.VMEM(shape + (2 * NRHS,), BF16)] * len(full)
        + [pltpu.VMEM(shape + (NRHS,), BF16)] * len(halved),
        in_specs=[smem, smem] + [vmem] * (2 + len(xs)),
        out_specs=[vmem] * n,
        scratch_shapes=[
            pltpu.VMEM((boxes * dirs, 2, rows, NRHS), F32),
            pltpu.VMEM((pairs, dirs, 4 * rank, 2 * NRHS), BF16),
        ],
        compiler_params=PARAMS,
        cost_estimate=COST,
        name="lower",
    )(count, parents, *xs, basis, up)


def upper_kernel(full, halved, perm_hbm, down_ref, row_ref, *refs):
    n, m = len(full), len(halved)
    mids, own_mids, other_mids = refs[:n], refs[n : n + m], refs[n + m : n + 2 * m]
    out_hbm, spread_ref, mix_ref, out_ref, perm_ref, sems = refs[n + 2 * m :]
    groups, local = down_ref.shape[:2]
    rank = spread_ref.shape[2] // 2
    leaf = row_ref.shape[3]
    fetch = pltpu.make_async_copy(perm_hbm, perm_ref, sems.at[local])
    fetch.start()

    def put(source, h, real, imag):
        spread_ref[source, h, :rank, :NRHS] = real
        spread_ref[source, h, :rank, NRHS:] = imag
        spread_ref[source, h, rank:, :NRHS] = -imag
        spread_ref[source, h, rank:, NRHS:] = real

    left = lax.broadcasted_iota(jnp.int32, (rank, NRHS), 1) < HALF
    for own_ref, other_ref, (k, which) in zip(own_mids, other_mids, halved):
        pairs = own_ref.shape[0]
        swap = lax.axis_index("rhs") == 1
        for p in range(pairs):
            for h in range(local):
                low, high = own_ref[p, h].astype(F32), other_ref[p, h].astype(F32)
                low, high = jnp.where(swap, high, low), jnp.where(swap, low, high)
                real = jnp.where(left, low, pltpu.roll(high, HALF, 1)).astype(BF16)
                imag = jnp.where(left, pltpu.roll(low, HALF, 1), high).astype(BF16)
                put(partner(k, which) * pairs + p, h, real, imag)
    for mid_ref, (k, which) in zip(mids, full):
        pairs = mid_ref.shape[0]
        for p in range(pairs):
            for h in range(local):
                mid = mid_ref[p, h]
                put(partner(k, which) * pairs + p, h, mid[:, :NRHS], mid[:, NRHS:])
    fetch.wait()
    copies = []
    for h in range(local):
        tops = ([], [])
        for q in range(groups):
            parts = [spread_ref[perm_ref[2 * q + s], h] for s in range(2)]
            top = jnp.dot(
                down_ref[q, h], jnp.concatenate(parts, axis=0), preferred_element_type=F32
            ).astype(BF16)
            for t in range(2):
                piece = top[t * rank : (t + 1) * rank]
                tops[t].append(piece)
                tops[t].append(jnp.concatenate([-piece[:, NRHS:], piece[:, :NRHS]], axis=1))
        for t in range(2):
            rows = jnp.concatenate([row_ref[h, t, q] for q in range(groups)], axis=1)
            field = jnp.dot(rows, jnp.concatenate(tops[t], axis=0), preferred_element_type=F32)
            mix_ref[h, t, pl.ds(0, leaf, stride=2), :] = field[:, :NRHS]
            mix_ref[h, t, pl.ds(1, leaf, stride=2), :] = field[:, NRHS:]
            out_ref[h, t] = mix_ref[h, t].astype(BF16)
        copies.append(pltpu.make_async_copy(out_ref.at[h], out_hbm.at[h], sems.at[h]))
        copies[-1].start()
    for copy in copies:
        copy.wait()


def upper(full, halved, perm, down, row, mids):
    groups, local, _, width = down.shape
    leaf = row.shape[3]
    vmem = pl.BlockSpec(memory_space=pltpu.VMEM)
    hbm = pl.BlockSpec(memory_space=pltpu.HBM)
    shape = (local, 2, 2 * leaf, NRHS)
    return pl.pallas_call(
        functools.partial(upper_kernel, full, halved),
        out_shape=jax.ShapeDtypeStruct(shape, BF16),
        in_specs=[hbm] + [vmem] * (2 + len(mids)),
        out_specs=hbm,
        scratch_shapes=[
            pltpu.VMEM((2 * groups, local, width // 2, 2 * NRHS), BF16),
            pltpu.VMEM(shape, F32),
            pltpu.VMEM(shape, BF16),
            pltpu.SMEM(perm.shape, jnp.int32),
            pltpu.SemaphoreType.DMA((local + 1,)),
        ],
        compiler_params=PARAMS,
        cost_estimate=COST,
        name="upper",
    )(pltpu.with_memory_space_constraint(perm, pltpu.HBM), down, row, *mids)


def send(block, route, dests):
    code = 2 * route[0] + route[1]
    if not code:
        return block
    return lax.ppermute(block, ("blk", "sub"), [(m, m ^ code) for m in range(dests)])


def on_device(
    columns, x_panels, leaf_basis, leaf_count, parent_map, up_transfer, mid_perm, down_transfer, row_basis
):
    boxes, directions, rank, _, leaf = leaf_basis.shape
    basis = leaf_basis.reshape(boxes, directions, rank * 2, leaf)
    groups, _, local = down_transfer.shape[:3]
    down = down_transfer.reshape(groups, local, 2 * rank, 4 * rank)
    row = row_basis.reshape(local, 2, groups, leaf, 2 * rank)
    x = jnp.transpose(x_panels, (0, 2, 3, 1))
    dests = 2 * columns
    full = [(2, 0), (1, 0), (0, 1), (2, 1), (1, 1), (0, 0)]
    farther = both_cores(range(columns - 1, 2, -1))
    if 2 * x.shape[2] == NRHS:
        halved = farther
        xs = [x, lax.ppermute(x, "rhs", [(0, 1), (1, 0)])]
        *own_mids, basis, up = own(halved, dests, leaf_count, parent_map, x, basis, up_transfer)
        own_mids = [send(mid, route, dests) for mid, route in zip(own_mids, halved)]
    else:
        full, halved, own_mids, up = farther + full, [], [], up_transfer
        xs = [lax.all_gather(x, "rhs", axis=2, tiled=True)]
    mids = lower(full, halved, dests, leaf_count, parent_map, xs, basis, up)
    mids = [send(mid, route, dests) for mid, route in zip(mids, full + halved)]
    n = len(full)
    result = upper(full, halved, mid_perm, down, row, [*mids[:n], *own_mids, *mids[n:]])
    return result.reshape(1, local, 2, leaf, 2, NRHS)


def solution(mesh):
    return jax.shard_map(
        functools.partial(on_device, mesh.shape["blk"]),
        mesh=mesh,
        in_specs=(
            P(("grp", "blk", "sub"), None, None, "rhs"),
            P(("blk", "sub"), "rhs", None, None, None),
            P(("blk", "sub")),
            P("rhs"),
            P(("blk", "sub"), "rhs", None, None),
            P(),
            P(None, "rhs", ("blk", "sub"), None, None, None),
            P("rhs", ("blk", "sub"), None, None, None, None),
        ),
        out_specs=P(("grp", "rhs"), ("blk", "sub"), None, None, None, None),
        check_vma=False,
    )
```

```python
import functools

import jax
import jax.numpy as jnp
from jax import lax
from jax.experimental import pallas as pl
from jax.experimental.pallas import tpu as pltpu
from jax.sharding import PartitionSpec as P

NRHS = 128
HALF = 64
F32 = jnp.float32
BF16 = jnp.bfloat16
PARAMS = pltpu.CompilerParams(vmem_limit_bytes=32 * 1024 * 1024)
COST = pl.CostEstimate(flops=1_000_000, bytes_accessed=10_000, transcendentals=0)


def both_cores(steps):
    return [(k, which) for k in steps for which in (0, 1)]


def partner(k, which):
    z = jnp.bitwise_xor(lax.axis_index("blk"), k)
    core = jnp.bitwise_xor(lax.axis_index("sub"), which)
    return z * 2 + core


def up_stage(outs, routes, parent_ref, up_ref, leaf_ref, cut=lambda mid: mid):
    pairs, local = outs[0].shape[:2]
    for out, (k, which) in zip(outs, routes):
        dest = partner(k, which)
        for p in range(pairs):
            for h in range(local):
                j = dest * local + h
                mid = jnp.dot(
                    up_ref[p, j], leaf_ref[p, parent_ref[j]], preferred_element_type=F32
                )
                out[p, h] = cut(mid).astype(BF16)


def leaf_stage(spreads, combine, count_ref, basis_ref, g_ref, leaf_ref, ready):
    boxes, dirs, rows, _ = basis_ref.shape
    rank = rows // 2
    width = leaf_ref.shape[3]
    first = lax.axis_index("rhs") * dirs
    even = pl.ds(0, rank, stride=2)
    odd = pl.ds(1, rank, stride=2)
    for b in range(boxes):
        ready(b)
        spread = spreads(b)
        for d in range(dirs):
            g = lax.dot_general(
                basis_ref[b, d], spread, (((1,), (1,)), ((), ())), preferred_element_type=F32
            )
            g_ref[b * dirs + d, 0] = g[:, :NRHS]
            g_ref[b * dirs + d, 1] = g[:, NRHS:]
        if b == 0:
            ready("count")
        for d in range(dirs):
            slot = b * dirs + d
            live = first + d < count_ref[b]
            pieces = combine(
                [g_ref[slot, i, even, :] for i in range(2)],
                [g_ref[slot, i, odd, :] for i in range(2)],
            )
            pieces = [jnp.where(live, x, jnp.zeros_like(x)).astype(BF16) for x in pieces]
            base = (b % 2) * 2 * rank
            top, bottom = slice(base, base + rank), slice(base + rank, base + 2 * rank)
            if width == NRHS:
                leaf_ref[b // 2, d, top, :] = pieces[0]
                leaf_ref[b // 2, d, bottom, :] = pieces[1]
            else:
                leaf_ref[b // 2, d, top, :NRHS] = pieces[0]
                leaf_ref[b // 2, d, top, NRHS:] = pieces[1]
                leaf_ref[b // 2, d, bottom, :NRHS] = -pieces[1]
                leaf_ref[b // 2, d, bottom, NRHS:] = pieces[0]


def half_columns(even, odd):
    return even[0] + odd[1], even[1] - odd[0]


def all_columns(even, odd):
    return even[0] - odd[1], even[1] + odd[0]


def own_kernel(routes, count_hbm, parent_hbm, x_hbm, basis_hbm, up_hbm, *refs):
    n = len(routes)
    outs, basis_ref, up_ref = refs[:n], refs[n], refs[n + 1]
    count_ref, parent_ref, x_ref, leaf_ref, g_ref, sems = refs[n + 2 :]
    boxes = basis_ref.shape[0]
    copies = {
        "x": pltpu.make_async_copy(x_hbm, x_ref, sems.at[0]),
        "count": pltpu.make_async_copy(count_hbm, count_ref, sems.at[1]),
        "parent": pltpu.make_async_copy(parent_hbm, parent_ref, sems.at[2]),
        "up": pltpu.make_async_copy(up_hbm, up_ref, sems.at[3]),
    }
    for b in range(boxes):
        copies[b] = pltpu.make_async_copy(basis_hbm.at[b], basis_ref.at[b], sems.at[4 + b])
    for name in ["x", 0, "count"] + list(range(1, boxes)) + ["up", "parent"]:
        copies[name].start()
    copies["x"].wait()

    def spreads(b):
        real, imag = x_ref[b, 0], x_ref[b, 1]
        return jnp.concatenate([real, imag, -imag, real], axis=0)

    leaf_stage(
        spreads, half_columns, count_ref, basis_ref, g_ref, leaf_ref, lambda name: copies[name].wait()
    )
    copies["up"].wait()
    copies["parent"].wait()
    up_stage(outs, routes, parent_ref, up_ref, leaf_ref)


def own(routes, dests, count, parents, x, basis, up):
    boxes, dirs, rows, _ = basis.shape
    pairs, dirs_up, rank, _ = up.shape
    block = pltpu.VMEM((pairs, dirs_up // dests, rank, NRHS), BF16)
    args = [count, parents, x, basis, up]
    return pl.pallas_call(
        functools.partial(own_kernel, routes),
        out_shape=[block] * len(routes)
        + [pltpu.VMEM(basis.shape, BF16), pltpu.VMEM(up.shape, BF16)],
        in_specs=[pl.BlockSpec(memory_space=pltpu.HBM)] * 5,
        out_specs=[pl.BlockSpec(memory_space=pltpu.VMEM)] * (len(routes) + 2),
        scratch_shapes=[
            pltpu.SMEM(count.shape, jnp.int32),
            pltpu.SMEM(parents.shape, jnp.int32),
            pltpu.VMEM(x.shape, BF16),
            pltpu.VMEM((pairs, dirs, 4 * rank, NRHS), BF16),
            pltpu.VMEM((boxes * dirs, 2, rows, NRHS), F32),
            pltpu.SemaphoreType.DMA((4 + boxes,)),
        ],
        compiler_params=PARAMS,
        cost_estimate=COST,
        name="own",
    )(*[pltpu.with_memory_space_constraint(arg, pltpu.HBM) for arg in args])


def other_columns(mid):
    left = lax.broadcasted_iota(jnp.int32, (mid.shape[0], NRHS), 1) < HALF
    real, imag = mid[:, :NRHS], mid[:, NRHS:]
    low = jnp.where(left, real, pltpu.roll(imag, HALF, 1))
    high = jnp.where(left, pltpu.roll(real, HALF, 1), imag)
    return jnp.where(lax.axis_index("rhs") == 1, low, high)


def lower_kernel(full, halved, count_hbm, parent_hbm, *refs):
    n, m = len(full), len(halved)
    g_ref, leaf_ref, count_ref, parent_ref, sems = refs[-5:]
    outs = refs[-5 - n - m : -5]
    *xs, basis_ref, up_ref = refs[: -5 - n - m]
    copies = {
        "count": pltpu.make_async_copy(count_hbm, count_ref, sems.at[0]),
        "parent": pltpu.make_async_copy(parent_hbm, parent_ref, sems.at[1]),
    }
    for copy in copies.values():
        copy.start()

    def ready(name):
        if name in copies:
            copies[name].wait()

    def spreads(b):
        if len(xs) == 1:
            return jnp.concatenate([xs[0][b, 0], xs[0][b, 1]], axis=0)
        own, other = xs[0][b], xs[1][b]
        swap = lax.axis_index("rhs") == 1
        low, high = jnp.where(swap, other, own), jnp.where(swap, own, other)
        return jnp.concatenate([low[0], high[0], low[1], high[1]], axis=0)

    leaf_stage(spreads, all_columns, count_ref, basis_ref, g_ref, leaf_ref, ready)
    ready("parent")
    up_stage(outs[:n], full, parent_ref, up_ref, leaf_ref)
    if halved:
        up_stage(outs[n:], halved, parent_ref, up_ref, leaf_ref, other_columns)


def lower(full, halved, dests, count, parents, xs, basis, up):
    boxes, dirs, rows, _ = basis.shape
    pairs, dirs_up, rank, _ = up.shape
    shape = (pairs, dirs_up // dests, rank)
    hbm = pl.BlockSpec(memory_space=pltpu.HBM)
    vmem = pl.BlockSpec(memory_space=pltpu.VMEM)
    n = len(full) + len(halved)
    return pl.pallas_call(
        functools.partial(lower_kernel, full, halved),
        out_shape=[pltpu.VMEM(shape + (2 * NRHS,), BF16)] * len(full)
        + [pltpu.VMEM(shape + (NRHS,), BF16)] * len(halved),
        in_specs=[hbm, hbm] + [vmem] * (2 + len(xs)),
        out_specs=[vmem] * n,
        scratch_shapes=[
            pltpu.VMEM((boxes * dirs, 2, rows, NRHS), F32),
            pltpu.VMEM((pairs, dirs, 4 * rank, 2 * NRHS), BF16),
            pltpu.SMEM(count.shape, jnp.int32),
            pltpu.SMEM(parents.shape, jnp.int32),
            pltpu.SemaphoreType.DMA((2,)),
        ],
        compiler_params=PARAMS,
        cost_estimate=COST,
        name="lower",
    )(*[pltpu.with_memory_space_constraint(a, pltpu.HBM) for a in (count, parents)], *xs, basis, up)


def twist(top):
    return jnp.concatenate([-top[:, NRHS:], top[:, :NRHS]], axis=1)


def twisted_rows(tops):
    return jnp.concatenate([rows for top in tops for rows in (top, twist(top))], axis=0)


def upper_kernel(full, halved, last, perm_hbm, down_ref, row_ref, *refs):
    n, m = len(full), len(halved)
    mids, own_mids, other_mids = refs[:n], refs[n : n + m], refs[n + m : n + 2 * m]
    field_ref, top_ref, spread_ref, perm_ref, sem = refs[n + 2 * m :]
    groups, local = down_ref.shape[:2]
    rank = spread_ref.shape[2] // 2
    leaf = row_ref.shape[3]
    fetch = pltpu.make_async_copy(perm_hbm, perm_ref, sem.at[0])
    fetch.start()

    def put(source, h, real, imag):
        spread_ref[source, h, :rank, :NRHS] = real
        spread_ref[source, h, :rank, NRHS:] = imag
        spread_ref[source, h, rank:, :NRHS] = -imag
        spread_ref[source, h, rank:, NRHS:] = real

    left = lax.broadcasted_iota(jnp.int32, (rank, NRHS), 1) < HALF
    for own_ref, other_ref, (k, which) in zip(own_mids, other_mids, halved):
        swap = lax.axis_index("rhs") == 1
        for h in range(local):
            low, high = own_ref[0, h].astype(F32), other_ref[0, h].astype(F32)
            low, high = jnp.where(swap, high, low), jnp.where(swap, low, high)
            real = jnp.where(left, low, pltpu.roll(high, HALF, 1)).astype(BF16)
            imag = jnp.where(left, pltpu.roll(low, HALF, 1), high).astype(BF16)
            put(partner(k, which), h, real, imag)
    for mid_ref, (k, which) in zip(mids, full):
        for h in range(local):
            mid = mid_ref[0, h]
            put(partner(k, which), h, mid[:, :NRHS], mid[:, NRHS:])
    missing = partner(*last)
    for h in range(local):
        spread_ref[missing, h] = jnp.zeros(spread_ref.shape[2:], BF16)
    fetch.wait()
    for h in range(local):
        tops = ([], [])
        for q in range(groups):
            children = [perm_ref[2 * q + s] for s in range(2)]
            top = jnp.dot(
                down_ref[q, h],
                jnp.concatenate([spread_ref[child, h] for child in children], axis=0),
                preferred_element_type=F32,
            )
            lacks = jnp.logical_or(children[0] == missing, children[1] == missing)
            top_ref[jnp.where(lacks, 0, 1), h] = top
            top = jnp.where(lacks, jnp.zeros_like(top), top).astype(BF16)
            for t in range(2):
                tops[t].append(top[t * rank : (t + 1) * rank])
        for t in range(2):
            rows = jnp.concatenate([row_ref[h, t, q] for q in range(groups)], axis=1)
            field = jnp.dot(rows, twisted_rows(tops[t]), preferred_element_type=F32)
            field_ref[h, t, pl.ds(0, leaf, stride=2), :] = field[:, :NRHS]
            field_ref[h, t, pl.ds(1, leaf, stride=2), :] = field[:, NRHS:]


def upper(full, halved, last, perm, down, row, mids):
    groups, local, _, width = down.shape
    leaf = row.shape[3]
    rank = width // 4
    vmem = pl.BlockSpec(memory_space=pltpu.VMEM)
    hbm = pl.BlockSpec(memory_space=pltpu.HBM)
    return pl.pallas_call(
        functools.partial(upper_kernel, full, halved, last),
        out_shape=[
            pltpu.VMEM((local, 2, 2 * leaf, NRHS), F32),
            pltpu.VMEM((2, local, 2 * rank, 2 * NRHS), F32),
        ],
        in_specs=[hbm] + [vmem] * (2 + len(mids)),
        out_specs=[vmem] * 2,
        scratch_shapes=[
            pltpu.VMEM((2 * groups, local, 2 * rank, 2 * NRHS), BF16),
            pltpu.SMEM(perm.shape, jnp.int32),
            pltpu.SemaphoreType.DMA((1,)),
        ],
        compiler_params=PARAMS,
        cost_estimate=COST,
        name="upper",
    )(pltpu.with_memory_space_constraint(perm, pltpu.HBM), down, row, *mids)


def finish_kernel(last, perm_hbm, down_ref, row_ref, field_ref, top_ref, mid_ref, out_hbm, mix_ref, out_ref, perm_ref, sems):
    groups, local = down_ref.shape[:2]
    rank = mid_ref.shape[2]
    leaf = row_ref.shape[3]
    fetch = pltpu.make_async_copy(perm_hbm, perm_ref, sems.at[local])
    fetch.start()
    fetch.wait()
    missing = partner(*last)
    group, child = 0, 0
    for i in range(2 * groups):
        found = perm_ref[i] == missing
        group = jnp.where(found, i // 2, group)
        child = jnp.where(found, i % 2, child)
    copies = []
    for h in range(local):
        mid = mid_ref[0, h]
        spread = twisted_rows([mid])
        zeros = jnp.zeros_like(spread)
        spread = jnp.concatenate(
            [jnp.where(child == 0, spread, zeros), jnp.where(child == 1, spread, zeros)], axis=0
        )
        top = top_ref[0, h] + jnp.dot(down_ref[group, h], spread, preferred_element_type=F32)
        top = top.astype(BF16)
        for t in range(2):
            rows = twisted_rows([top[t * rank : (t + 1) * rank]])
            field = jnp.dot(row_ref[h, t, group], rows, preferred_element_type=F32)
            mix_ref[h, t, pl.ds(0, leaf, stride=2), :] = field[:, :NRHS]
            mix_ref[h, t, pl.ds(1, leaf, stride=2), :] = field[:, NRHS:]
            out_ref[h, t] = (field_ref[h, t] + mix_ref[h, t]).astype(BF16)
        copies.append(pltpu.make_async_copy(out_ref.at[h], out_hbm.at[h], sems.at[h]))
        copies[-1].start()
    for copy in copies:
        copy.wait()


def finish(last, perm, down, row, field, top, mid):
    vmem = pl.BlockSpec(memory_space=pltpu.VMEM)
    hbm = pl.BlockSpec(memory_space=pltpu.HBM)
    return pl.pallas_call(
        functools.partial(finish_kernel, last),
        out_shape=jax.ShapeDtypeStruct(field.shape, BF16),
        in_specs=[hbm] + [vmem] * 5,
        out_specs=hbm,
        scratch_shapes=[
            pltpu.VMEM(field.shape, F32),
            pltpu.VMEM(field.shape, BF16),
            pltpu.SMEM(perm.shape, jnp.int32),
            pltpu.SemaphoreType.DMA((field.shape[0] + 1,)),
        ],
        compiler_params=PARAMS,
        cost_estimate=COST,
        name="finish",
    )(pltpu.with_memory_space_constraint(perm, pltpu.HBM), down, row, field, top, mid)


def send(block, route, dests):
    code = 2 * route[0] + route[1]
    if not code:
        return block
    return lax.ppermute(block, ("blk", "sub"), [(m, m ^ code) for m in range(dests)])


def on_device(
    columns, x_panels, leaf_basis, leaf_count, parent_map, up_transfer, mid_perm, down_transfer, row_basis
):
    boxes, directions, rank, _, leaf = leaf_basis.shape
    basis = leaf_basis.reshape(boxes, directions, rank * 2, leaf)
    groups, _, local = down_transfer.shape[:3]
    down = down_transfer.reshape(groups, local, 2 * rank, 4 * rank)
    row = row_basis.reshape(local, 2, groups, leaf, 2 * rank)
    x = jnp.transpose(x_panels, (0, 2, 3, 1))
    dests = 2 * columns
    two = both_cores((2,))
    full = both_cores(range(columns - 1, 3, -1)) + [(3, 0), (1, 0), (0, 1), (1, 1), (0, 0)]
    last = (3, 1)
    if 2 * x.shape[2] == NRHS:
        halved = two
        xs = [x, lax.ppermute(x, "rhs", [(0, 1), (1, 0)])]
        *own_mids, basis, up = own(halved, dests, leaf_count, parent_map, x, basis, up_transfer)
        own_mids = [send(mid, route, dests) for mid, route in zip(own_mids, halved)]
    else:
        full, halved, own_mids, up = two + full, [], [], up_transfer
        xs = [lax.all_gather(x, "rhs", axis=2, tiled=True)]
    n = len(full)
    routes = full + [last] + halved
    mids = lower(full + [last], halved, dests, leaf_count, parent_map, xs, basis, up)
    mids = [send(mid, route, dests) for mid, route in zip(mids, routes)]
    field, top = upper(
        full, halved, last, mid_perm, down, row, [*mids[:n], *own_mids, *mids[n + 1 :]]
    )
    result = finish(last, mid_perm, down, row, field, top, mids[n])
    return result.reshape(1, local, 2, leaf, 2, NRHS)


def solution(mesh):
    return jax.shard_map(
        functools.partial(on_device, mesh.shape["blk"]),
        mesh=mesh,
        in_specs=(
            P(("grp", "blk", "sub"), None, None, "rhs"),
            P(("blk", "sub"), "rhs", None, None, None),
            P(("blk", "sub")),
            P("rhs"),
            P(("blk", "sub"), "rhs", None, None),
            P(),
            P(None, "rhs", ("blk", "sub"), None, None, None),
            P("rhs", ("blk", "sub"), None, None, None, None),
        ),
        out_specs=P(("grp", "rhs"), ("blk", "sub"), None, None, None, None),
        check_vma=False,
    )
```

```python
import functools

import jax
import jax.numpy as jnp
from jax import lax
from jax.experimental import pallas as pl
from jax.experimental.pallas import tpu as pltpu
from jax.sharding import PartitionSpec as P

NRHS = 128
HALF = 64
F32 = jnp.float32
BF16 = jnp.bfloat16
PARAMS = pltpu.CompilerParams(vmem_limit_bytes=32 * 1024 * 1024)
COST = pl.CostEstimate(flops=1_000_000, bytes_accessed=10_000, transcendentals=0)


def both_cores(steps):
    return [(k, which) for k in steps for which in (0, 1)]


def partner(k, which):
    z = jnp.bitwise_xor(lax.axis_index("blk"), k)
    core = jnp.bitwise_xor(lax.axis_index("sub"), which)
    return z * 2 + core


def up_stage(outs, routes, parent_ref, up_ref, leaf_ref, cut=lambda mid: mid):
    pairs, local = outs[0].shape[:2]
    for out, (k, which) in zip(outs, routes):
        dest = partner(k, which)
        for p in range(pairs):
            for h in range(local):
                j = dest * local + h
                mid = jnp.dot(
                    up_ref[p, j], leaf_ref[p, parent_ref[j]], preferred_element_type=F32
                )
                out[p, h] = cut(mid).astype(BF16)


def chunks(count):
    middle = (count + 1) // 2
    return [group for group in (range(middle), range(middle, count)) if group]


def leaf_stage(spreads, combine, count_ref, basis_ref, g_ref, leaf_ref, ready):
    boxes, dirs, rows, _ = basis_ref.shape
    rank = rows // 2
    width = leaf_ref.shape[3]
    first = lax.axis_index("rhs") * dirs
    even = pl.ds(0, rank, stride=2)
    odd = pl.ds(1, rank, stride=2)
    for b, group in [(b, group) for b in range(boxes) for group in chunks(dirs)]:
        ready((b, group))
        spread = spreads(b)
        for d in group:
            g = lax.dot_general(
                basis_ref[b, d], spread, (((1,), (1,)), ((), ())), preferred_element_type=F32
            )
            g_ref[b * dirs + d, 0] = g[:, :NRHS]
            g_ref[b * dirs + d, 1] = g[:, NRHS:]
        if b == 0 and 0 in group:
            ready("count")
        for d in group:
            slot = b * dirs + d
            live = first + d < count_ref[b]
            pieces = combine(
                [g_ref[slot, i, even, :] for i in range(2)],
                [g_ref[slot, i, odd, :] for i in range(2)],
            )
            pieces = [jnp.where(live, x, jnp.zeros_like(x)).astype(BF16) for x in pieces]
            base = (b % 2) * 2 * rank
            top, bottom = slice(base, base + rank), slice(base + rank, base + 2 * rank)
            if width == NRHS:
                leaf_ref[b // 2, d, top, :] = pieces[0]
                leaf_ref[b // 2, d, bottom, :] = pieces[1]
            else:
                leaf_ref[b // 2, d, top, :NRHS] = pieces[0]
                leaf_ref[b // 2, d, top, NRHS:] = pieces[1]
                leaf_ref[b // 2, d, bottom, :NRHS] = -pieces[1]
                leaf_ref[b // 2, d, bottom, NRHS:] = pieces[0]


def half_columns(even, odd):
    return even[0] + odd[1], even[1] - odd[0]


def all_columns(even, odd):
    return even[0] - odd[1], even[1] + odd[0]


def own_kernel(routes, count_hbm, parent_hbm, x_hbm, basis_hbm, up_hbm, *refs):
    n = len(routes)
    outs, basis_ref, up_ref = refs[:n], refs[n], refs[n + 1]
    count_ref, parent_ref, x_ref, leaf_ref, g_ref, sems = refs[n + 2 :]
    boxes = basis_ref.shape[0]
    copies = {
        "x": pltpu.make_async_copy(x_hbm, x_ref, sems.at[0]),
        "count": pltpu.make_async_copy(count_hbm, count_ref, sems.at[1]),
        "parent": pltpu.make_async_copy(parent_hbm, parent_ref, sems.at[2]),
        "up": pltpu.make_async_copy(up_hbm, up_ref, sems.at[3]),
    }
    parts = [(b, group) for b in range(boxes) for group in chunks(basis_ref.shape[1])]
    for i, (b, group) in enumerate(parts):
        at = (b, pl.ds(group.start, len(group)))
        copies[b, group] = pltpu.make_async_copy(basis_hbm.at[at], basis_ref.at[at], sems.at[4 + i])
    for name in ["x", parts[0], "count", *parts[1:], "up", "parent"]:
        copies[name].start()
    copies["x"].wait()

    def spreads(b):
        real, imag = x_ref[b, 0], x_ref[b, 1]
        return jnp.concatenate([real, imag, -imag, real], axis=0)

    leaf_stage(
        spreads, half_columns, count_ref, basis_ref, g_ref, leaf_ref, lambda name: copies[name].wait()
    )
    copies["up"].wait()
    copies["parent"].wait()
    up_stage(outs, routes, parent_ref, up_ref, leaf_ref)


def own(routes, dests, count, parents, x, basis, up):
    boxes, dirs, rows, _ = basis.shape
    pairs, dirs_up, rank, _ = up.shape
    block = pltpu.VMEM((pairs, dirs_up // dests, rank, NRHS), BF16)
    args = [count, parents, x, basis, up]
    return pl.pallas_call(
        functools.partial(own_kernel, routes),
        out_shape=[block] * len(routes)
        + [pltpu.VMEM(basis.shape, BF16), pltpu.VMEM(up.shape, BF16)],
        in_specs=[pl.BlockSpec(memory_space=pltpu.HBM)] * 5,
        out_specs=[pl.BlockSpec(memory_space=pltpu.VMEM)] * (len(routes) + 2),
        scratch_shapes=[
            pltpu.SMEM(count.shape, jnp.int32),
            pltpu.SMEM(parents.shape, jnp.int32),
            pltpu.VMEM(x.shape, BF16),
            pltpu.VMEM((pairs, dirs, 4 * rank, NRHS), BF16),
            pltpu.VMEM((boxes * dirs, 2, rows, NRHS), F32),
            pltpu.SemaphoreType.DMA((4 + 2 * boxes,)),
        ],
        compiler_params=PARAMS,
        cost_estimate=COST,
        name="own",
    )(*[pltpu.with_memory_space_constraint(arg, pltpu.HBM) for arg in args])


def other_columns(mid):
    left = lax.broadcasted_iota(jnp.int32, (mid.shape[0], NRHS), 1) < HALF
    real, imag = mid[:, :NRHS], mid[:, NRHS:]
    low = jnp.where(left, real, pltpu.roll(imag, HALF, 1))
    high = jnp.where(left, pltpu.roll(real, HALF, 1), imag)
    return jnp.where(lax.axis_index("rhs") == 1, low, high)


def lower_kernel(full, halved, count_hbm, parent_hbm, *refs):
    n, m = len(full), len(halved)
    g_ref, leaf_ref, count_ref, parent_ref, sems = refs[-5:]
    outs = refs[-5 - n - m : -5]
    *xs, basis_ref, up_ref = refs[: -5 - n - m]
    copies = {
        "count": pltpu.make_async_copy(count_hbm, count_ref, sems.at[0]),
        "parent": pltpu.make_async_copy(parent_hbm, parent_ref, sems.at[1]),
    }
    for copy in copies.values():
        copy.start()

    def ready(name):
        if name in copies:
            copies[name].wait()

    def spreads(b):
        if len(xs) == 1:
            return jnp.concatenate([xs[0][b, 0], xs[0][b, 1]], axis=0)
        own, other = xs[0][b], xs[1][b]
        swap = lax.axis_index("rhs") == 1
        low, high = jnp.where(swap, other, own), jnp.where(swap, own, other)
        return jnp.concatenate([low[0], high[0], low[1], high[1]], axis=0)

    leaf_stage(spreads, all_columns, count_ref, basis_ref, g_ref, leaf_ref, ready)
    ready("parent")
    up_stage(outs[:n], full, parent_ref, up_ref, leaf_ref)
    if halved:
        up_stage(outs[n:], halved, parent_ref, up_ref, leaf_ref, other_columns)


def lower(full, halved, dests, count, parents, xs, basis, up):
    boxes, dirs, rows, _ = basis.shape
    pairs, dirs_up, rank, _ = up.shape
    shape = (pairs, dirs_up // dests, rank)
    hbm = pl.BlockSpec(memory_space=pltpu.HBM)
    vmem = pl.BlockSpec(memory_space=pltpu.VMEM)
    n = len(full) + len(halved)
    return pl.pallas_call(
        functools.partial(lower_kernel, full, halved),
        out_shape=[pltpu.VMEM(shape + (2 * NRHS,), BF16)] * len(full)
        + [pltpu.VMEM(shape + (NRHS,), BF16)] * len(halved),
        in_specs=[hbm, hbm] + [vmem] * (2 + len(xs)),
        out_specs=[vmem] * n,
        scratch_shapes=[
            pltpu.VMEM((boxes * dirs, 2, rows, NRHS), F32),
            pltpu.VMEM((pairs, dirs, 4 * rank, 2 * NRHS), BF16),
            pltpu.SMEM(count.shape, jnp.int32),
            pltpu.SMEM(parents.shape, jnp.int32),
            pltpu.SemaphoreType.DMA((2,)),
        ],
        compiler_params=PARAMS,
        cost_estimate=COST,
        name="lower",
    )(*[pltpu.with_memory_space_constraint(a, pltpu.HBM) for a in (count, parents)], *xs, basis, up)


def twist(top):
    return jnp.concatenate([-top[:, NRHS:], top[:, :NRHS]], axis=1)


def twisted_rows(tops):
    return jnp.concatenate([rows for top in tops for rows in (top, twist(top))], axis=0)


def late_groups(late, perm_ref, groups):
    found = []
    for route in late:
        source = partner(*route)
        group, child = 0, 0
        for i in range(2 * groups):
            hit = perm_ref[i] == source
            group = jnp.where(hit, i // 2, group)
            child = jnp.where(hit, i % 2, child)
        found.append((group, child))
    return found


def prep_kernel(late, perm_hbm, down_ref, row_ref, after_ref, down_out, row_out, mix_ref, perm_ref, sem):
    groups, local = down_ref.shape[:2]
    leaf, width = row_ref.shape[3:]
    fetch = pltpu.make_async_copy(perm_hbm, perm_ref, sem.at[0])
    fetch.start()
    fetch.wait()
    found = late_groups(late, perm_ref, groups)
    (group_a, _), (group_b, _) = found
    left = lax.broadcasted_iota(jnp.int32, (leaf, width), 1) < width // 2
    for h in range(local):
        for i, (group, _) in enumerate(found):
            block = down_ref[group, h]
            rows = block.shape[0]
            for j, (other, child) in enumerate(found):
                part = jnp.where(child == 0, block[:, :width], block[:, width:])
                if i != j:
                    part = jnp.where(group == other, part, jnp.zeros_like(part))
                if i == 1:
                    part = jnp.where(group_a == group_b, jnp.zeros_like(part), part)
                down_out[h, i * rows : (i + 1) * rows, j * width : (j + 1) * width] = part
            for t in range(2):
                block = row_ref[h, t, group].astype(F32)
                slot = (h * 2 + t) * 2 + i
                mix_ref[slot, pl.ds(0, leaf, stride=2), :] = jnp.where(left, block, -block)
                mix_ref[slot, pl.ds(1, leaf, stride=2), :] = pltpu.roll(block, width // 2, 1)
                row_out[h, t, :, i * width : (i + 1) * width] = mix_ref[slot].astype(BF16)


def prep(late, perm, down, row, after):
    groups, local, rows, width = down.shape
    leaf = row.shape[3]
    vmem = pl.BlockSpec(memory_space=pltpu.VMEM)
    hbm = pl.BlockSpec(memory_space=pltpu.HBM)
    return pl.pallas_call(
        functools.partial(prep_kernel, late),
        out_shape=[
            pltpu.VMEM((local, 2 * rows, width), BF16),
            pltpu.VMEM((local, 2, 2 * leaf, width), BF16),
        ],
        in_specs=[hbm, vmem, vmem, pl.BlockSpec(memory_space=pl.ANY)],
        out_specs=[vmem] * 2,
        scratch_shapes=[
            pltpu.VMEM((4 * local, 2 * leaf, width // 2), F32),
            pltpu.SMEM(perm.shape, jnp.int32),
            pltpu.SemaphoreType.DMA((1,)),
        ],
        compiler_params=PARAMS,
        cost_estimate=COST,
        name="prep",
    )(pltpu.with_memory_space_constraint(perm, pltpu.HBM), down, row, after)


def upper_kernel(full, halved, late, perm_hbm, down_ref, row_ref, *refs):
    n, m = len(full), len(halved)
    mids, own_mids, other_mids = refs[:n], refs[n : n + m], refs[n + m : n + 2 * m]
    field_ref, top_ref, spread_ref, perm_ref, sem = refs[n + 2 * m :]
    groups, local = down_ref.shape[:2]
    rank = spread_ref.shape[2] // 2
    leaf = row_ref.shape[3]
    fetch = pltpu.make_async_copy(perm_hbm, perm_ref, sem.at[0])
    fetch.start()

    def put(source, h, real, imag):
        spread_ref[source, h, :rank, :NRHS] = real
        spread_ref[source, h, :rank, NRHS:] = imag
        spread_ref[source, h, rank:, :NRHS] = -imag
        spread_ref[source, h, rank:, NRHS:] = real

    left = lax.broadcasted_iota(jnp.int32, (rank, NRHS), 1) < HALF
    for own_ref, other_ref, (k, which) in zip(own_mids, other_mids, halved):
        swap = lax.axis_index("rhs") == 1
        for h in range(local):
            low, high = own_ref[0, h].astype(F32), other_ref[0, h].astype(F32)
            low, high = jnp.where(swap, high, low), jnp.where(swap, low, high)
            real = jnp.where(left, low, pltpu.roll(high, HALF, 1)).astype(BF16)
            imag = jnp.where(left, pltpu.roll(low, HALF, 1), high).astype(BF16)
            put(partner(k, which), h, real, imag)
    for mid_ref, (k, which) in zip(mids, full):
        for h in range(local):
            mid = mid_ref[0, h]
            put(partner(k, which), h, mid[:, :NRHS], mid[:, NRHS:])
    for route in late:
        for h in range(local):
            spread_ref[partner(*route), h] = jnp.zeros(spread_ref.shape[2:], BF16)
    for h in range(local):
        top_ref[1, h] = jnp.zeros(top_ref.shape[2:], F32)
    fetch.wait()
    (group_a, _), (group_b, _) = late_groups(late, perm_ref, groups)
    for h in range(local):
        tops = ([], [])
        for q in range(groups):
            parts = [spread_ref[perm_ref[2 * q + s], h] for s in range(2)]
            top = jnp.dot(
                down_ref[q, h], jnp.concatenate(parts, axis=0), preferred_element_type=F32
            )
            is_a, is_b = group_a == q, group_b == q
            top_ref[jnp.where(is_a, 0, jnp.where(is_b, 1, 2)), h] = top
            lacks = jnp.logical_or(is_a, is_b)
            top = jnp.where(lacks, jnp.zeros_like(top), top).astype(BF16)
            for t in range(2):
                tops[t].append(top[t * rank : (t + 1) * rank])
        for t in range(2):
            rows = jnp.concatenate([row_ref[h, t, q] for q in range(groups)], axis=1)
            field = jnp.dot(rows, twisted_rows(tops[t]), preferred_element_type=F32)
            field_ref[h, t, pl.ds(0, leaf, stride=2), :] = field[:, :NRHS]
            field_ref[h, t, pl.ds(1, leaf, stride=2), :] = field[:, NRHS:]


def upper(full, halved, late, perm, down, row, mids):
    groups, local, _, width = down.shape
    leaf = row.shape[3]
    rank = width // 4
    vmem = pl.BlockSpec(memory_space=pltpu.VMEM)
    hbm = pl.BlockSpec(memory_space=pltpu.HBM)
    return pl.pallas_call(
        functools.partial(upper_kernel, full, halved, late),
        out_shape=[
            pltpu.VMEM((local, 2, 2 * leaf, NRHS), F32),
            pltpu.VMEM((3, local, 2 * rank, 2 * NRHS), F32),
        ],
        in_specs=[hbm] + [vmem] * (2 + len(mids)),
        out_specs=[vmem] * 2,
        scratch_shapes=[
            pltpu.VMEM((2 * groups, local, 2 * rank, 2 * NRHS), BF16),
            pltpu.SMEM(perm.shape, jnp.int32),
            pltpu.SemaphoreType.DMA((1,)),
        ],
        compiler_params=PARAMS,
        cost_estimate=COST,
        name="upper",
    )(pltpu.with_memory_space_constraint(perm, pltpu.HBM), down, row, *mids)


def finish_kernel(down_ref, row_ref, field_ref, top_ref, *refs):
    mids, (out_hbm, out_ref, sems) = refs[:-3], refs[-3:]
    local = field_ref.shape[0]
    rank = mids[0].shape[2]
    copies = []
    for i, group in enumerate(chunks(local)):
        for h in group:
            spread = twisted_rows([mid[0, h] for mid in mids])
            top = jnp.concatenate([top_ref[0, h], top_ref[1, h]], axis=0)
            top = top + jnp.dot(down_ref[h], spread, preferred_element_type=F32)
            top = top.astype(BF16)
            for t in range(2):
                pieces = [top[r : r + rank] for r in (t * rank, (2 + t) * rank)]
                values = jnp.concatenate(
                    [half for piece in pieces for half in (piece[:, :NRHS], piece[:, NRHS:])],
                    axis=0,
                )
                field = jnp.dot(row_ref[h, t], values, preferred_element_type=F32)
                out_ref[h, t] = (field_ref[h, t] + field).astype(BF16)
        at = pl.ds(group.start, len(group))
        copies.append(pltpu.make_async_copy(out_ref.at[at], out_hbm.at[at], sems.at[i]))
        copies[-1].start()
    for copy in copies:
        copy.wait()


def finish(down, row, field, top, mids):
    vmem = pl.BlockSpec(memory_space=pltpu.VMEM)
    return pl.pallas_call(
        finish_kernel,
        out_shape=jax.ShapeDtypeStruct(field.shape, BF16),
        in_specs=[vmem] * (4 + len(mids)),
        out_specs=pl.BlockSpec(memory_space=pltpu.HBM),
        scratch_shapes=[pltpu.VMEM(field.shape, BF16), pltpu.SemaphoreType.DMA((2,))],
        compiler_params=PARAMS,
        cost_estimate=COST,
        name="finish",
    )(down, row, field, top, *mids)


def send(block, route, dests):
    code = 2 * route[0] + route[1]
    if not code:
        return block
    return lax.ppermute(block, ("blk", "sub"), [(m, m ^ code) for m in range(dests)])


def on_device(
    columns, x_panels, leaf_basis, leaf_count, parent_map, up_transfer, mid_perm, down_transfer, row_basis
):
    boxes, directions, rank, _, leaf = leaf_basis.shape
    basis = leaf_basis.reshape(boxes, directions, rank * 2, leaf)
    groups, _, local = down_transfer.shape[:3]
    down = down_transfer.reshape(groups, local, 2 * rank, 4 * rank)
    row = row_basis.reshape(local, 2, groups, leaf, 2 * rank)
    x = jnp.transpose(x_panels, (0, 2, 3, 1))
    dests = 2 * columns
    two = both_cores((2,))
    full = both_cores(range(columns - 1, 3, -1)) + [(3, 0), (1, 0), (1, 1), (0, 0)]
    late = [(3, 1), (0, 1)]
    if 2 * x.shape[2] == NRHS:
        halved = two
        xs = [x, lax.ppermute(x, "rhs", [(0, 1), (1, 0)])]
        *own_mids, basis, up = own(halved, dests, leaf_count, parent_map, x, basis, up_transfer)
        own_mids = [send(mid, route, dests) for mid, route in zip(own_mids, halved)]
    else:
        full, halved, own_mids, up = two + full, [], [], up_transfer
        xs = [lax.all_gather(x, "rhs", axis=2, tiled=True)]
    n = len(full)
    routes = full + late + halved
    mids = lower(full + late, halved, dests, leaf_count, parent_map, xs, basis, up)
    mids = [send(mid, route, dests) for mid, route in zip(mids, routes)]
    down_late, row_late = prep(late, mid_perm, down, row, [*own_mids, mids[0]][0])
    field, top = upper(
        full, halved, late, mid_perm, down, row, [*mids[:n], *own_mids, *mids[n + 2 :]]
    )
    result = finish(down_late, row_late, field, top, mids[n : n + 2])
    return result.reshape(1, local, 2, leaf, 2, NRHS)


def solution(mesh):
    return jax.shard_map(
        functools.partial(on_device, mesh.shape["blk"]),
        mesh=mesh,
        in_specs=(
            P(("grp", "blk", "sub"), None, None, "rhs"),
            P(("blk", "sub"), "rhs", None, None, None),
            P(("blk", "sub")),
            P("rhs"),
            P(("blk", "sub"), "rhs", None, None),
            P(),
            P(None, "rhs", ("blk", "sub"), None, None, None),
            P("rhs", ("blk", "sub"), None, None, None, None),
        ),
        out_specs=P(("grp", "rhs"), ("blk", "sub"), None, None, None, None),
        check_vma=False,
    )
```

```python
import functools

import jax
import jax.numpy as jnp
from jax import lax
from jax.experimental import pallas as pl
from jax.experimental.pallas import tpu as pltpu
from jax.sharding import PartitionSpec as P

NRHS = 128
HALF = 64
F32 = jnp.float32
BF16 = jnp.bfloat16
PARAMS = pltpu.CompilerParams(vmem_limit_bytes=32 * 1024 * 1024)
COST = pl.CostEstimate(flops=1_000_000, bytes_accessed=10_000, transcendentals=0)


def both_cores(steps):
    return [(k, which) for k in steps for which in (0, 1)]


def partner(k, which):
    z = jnp.bitwise_xor(lax.axis_index("blk"), k)
    core = jnp.bitwise_xor(lax.axis_index("sub"), which)
    return z * 2 + core


def up_stage(outs, routes, parent_ref, up_ref, leaf_ref, cut=lambda mid: mid):
    pairs, local = outs[0].shape[:2]
    for out, (k, which) in zip(outs, routes):
        dest = partner(k, which)
        for p in range(pairs):
            for h in range(local):
                j = dest * local + h
                mid = jnp.dot(
                    up_ref[p, j], leaf_ref[p, parent_ref[j]], preferred_element_type=F32
                )
                out[p, h] = cut(mid).astype(BF16)


def chunks(count):
    middle = (count + 1) // 2
    return [group for group in (range(middle), range(middle, count)) if group]


def leaf_stage(spreads, combine, count_ref, basis_ref, g_ref, leaf_ref, ready):
    boxes, dirs, rows, _ = basis_ref.shape
    rank = rows // 2
    width = leaf_ref.shape[3]
    first = lax.axis_index("rhs") * dirs
    even = pl.ds(0, rank, stride=2)
    odd = pl.ds(1, rank, stride=2)
    for b in range(boxes):
        ready(b)
        spread = spreads(b)
        for d in range(dirs):
            g = lax.dot_general(
                basis_ref[b, d], spread, (((1,), (1,)), ((), ())), preferred_element_type=F32
            )
            g_ref[b * dirs + d, 0] = g[:, :NRHS]
            g_ref[b * dirs + d, 1] = g[:, NRHS:]
        if b == 0:
            ready("count")
        for d in range(dirs):
            slot = b * dirs + d
            live = first + d < count_ref[b]
            pieces = combine(
                [g_ref[slot, i, even, :] for i in range(2)],
                [g_ref[slot, i, odd, :] for i in range(2)],
            )
            pieces = [jnp.where(live, x, jnp.zeros_like(x)).astype(BF16) for x in pieces]
            base = (b % 2) * 2 * rank
            top, bottom = slice(base, base + rank), slice(base + rank, base + 2 * rank)
            if width == NRHS:
                leaf_ref[b // 2, d, top, :] = pieces[0]
                leaf_ref[b // 2, d, bottom, :] = pieces[1]
            else:
                leaf_ref[b // 2, d, top, :NRHS] = pieces[0]
                leaf_ref[b // 2, d, top, NRHS:] = pieces[1]
                leaf_ref[b // 2, d, bottom, :NRHS] = -pieces[1]
                leaf_ref[b // 2, d, bottom, NRHS:] = pieces[0]


def half_columns(even, odd):
    return even[0] + odd[1], even[1] - odd[0]


def all_columns(even, odd):
    return even[0] - odd[1], even[1] + odd[0]


def own_kernel(routes, count_hbm, parent_hbm, x_hbm, basis_hbm, up_hbm, *refs):
    n = len(routes)
    outs, basis_ref, up_ref = refs[:n], refs[n], refs[n + 1]
    count_ref, parent_ref, x_ref, leaf_ref, g_ref, sems = refs[n + 2 :]
    boxes = basis_ref.shape[0]
    copies = {
        "x": pltpu.make_async_copy(x_hbm, x_ref, sems.at[0]),
        "count": pltpu.make_async_copy(count_hbm, count_ref, sems.at[1]),
        "parent": pltpu.make_async_copy(parent_hbm, parent_ref, sems.at[2]),
        "up": pltpu.make_async_copy(up_hbm, up_ref, sems.at[3]),
    }
    for b in range(boxes):
        copies[b] = pltpu.make_async_copy(basis_hbm.at[b], basis_ref.at[b], sems.at[4 + b])
    for name in ["x", 0, "count"] + list(range(1, boxes)) + ["up", "parent"]:
        copies[name].start()
    copies["x"].wait()

    def spreads(b):
        real, imag = x_ref[b, 0], x_ref[b, 1]
        return jnp.concatenate([real, imag, -imag, real], axis=0)

    leaf_stage(
        spreads, half_columns, count_ref, basis_ref, g_ref, leaf_ref, lambda name: copies[name].wait()
    )
    copies["up"].wait()
    copies["parent"].wait()
    up_stage(outs, routes, parent_ref, up_ref, leaf_ref)


def own(routes, dests, count, parents, x, basis, up):
    boxes, dirs, rows, _ = basis.shape
    pairs, dirs_up, rank, _ = up.shape
    block = pltpu.VMEM((pairs, dirs_up // dests, rank, NRHS), BF16)
    args = [count, parents, x, basis, up]
    return pl.pallas_call(
        functools.partial(own_kernel, routes),
        out_shape=[block] * len(routes)
        + [pltpu.VMEM(basis.shape, BF16), pltpu.VMEM(up.shape, BF16)],
        in_specs=[pl.BlockSpec(memory_space=pltpu.HBM)] * 5,
        out_specs=[pl.BlockSpec(memory_space=pltpu.VMEM)] * (len(routes) + 2),
        scratch_shapes=[
            pltpu.SMEM(count.shape, jnp.int32),
            pltpu.SMEM(parents.shape, jnp.int32),
            pltpu.VMEM(x.shape, BF16),
            pltpu.VMEM((pairs, dirs, 4 * rank, NRHS), BF16),
            pltpu.VMEM((boxes * dirs, 2, rows, NRHS), F32),
            pltpu.SemaphoreType.DMA((4 + boxes,)),
        ],
        compiler_params=PARAMS,
        cost_estimate=COST,
        name="own",
    )(*[pltpu.with_memory_space_constraint(arg, pltpu.HBM) for arg in args])


def other_columns(mid):
    left = lax.broadcasted_iota(jnp.int32, (mid.shape[0], NRHS), 1) < HALF
    real, imag = mid[:, :NRHS], mid[:, NRHS:]
    low = jnp.where(left, real, pltpu.roll(imag, HALF, 1))
    high = jnp.where(left, pltpu.roll(real, HALF, 1), imag)
    return jnp.where(lax.axis_index("rhs") == 1, low, high)


def lower_kernel(full, halved, count_hbm, parent_hbm, *refs):
    n, m = len(full), len(halved)
    g_ref, leaf_ref, count_ref, parent_ref, sems = refs[-5:]
    outs = refs[-5 - n - m : -5]
    *xs, basis_ref, up_ref = refs[: -5 - n - m]
    copies = {
        "count": pltpu.make_async_copy(count_hbm, count_ref, sems.at[0]),
        "parent": pltpu.make_async_copy(parent_hbm, parent_ref, sems.at[1]),
    }
    for copy in copies.values():
        copy.start()

    def ready(name):
        if name in copies:
            copies[name].wait()

    def spreads(b):
        if len(xs) == 1:
            return jnp.concatenate([xs[0][b, 0], xs[0][b, 1]], axis=0)
        own, other = xs[0][b], xs[1][b]
        swap = lax.axis_index("rhs") == 1
        low, high = jnp.where(swap, other, own), jnp.where(swap, own, other)
        return jnp.concatenate([low[0], high[0], low[1], high[1]], axis=0)

    leaf_stage(spreads, all_columns, count_ref, basis_ref, g_ref, leaf_ref, ready)
    ready("parent")
    up_stage(outs[:n], full, parent_ref, up_ref, leaf_ref)
    if halved:
        up_stage(outs[n:], halved, parent_ref, up_ref, leaf_ref, other_columns)


def lower(full, halved, dests, count, parents, xs, basis, up):
    boxes, dirs, rows, _ = basis.shape
    pairs, dirs_up, rank, _ = up.shape
    shape = (pairs, dirs_up // dests, rank)
    hbm = pl.BlockSpec(memory_space=pltpu.HBM)
    vmem = pl.BlockSpec(memory_space=pltpu.VMEM)
    n = len(full) + len(halved)
    return pl.pallas_call(
        functools.partial(lower_kernel, full, halved),
        out_shape=[pltpu.VMEM(shape + (2 * NRHS,), BF16)] * len(full)
        + [pltpu.VMEM(shape + (NRHS,), BF16)] * len(halved),
        in_specs=[hbm, hbm] + [vmem] * (2 + len(xs)),
        out_specs=[vmem] * n,
        scratch_shapes=[
            pltpu.VMEM((boxes * dirs, 2, rows, NRHS), F32),
            pltpu.VMEM((pairs, dirs, 4 * rank, 2 * NRHS), BF16),
            pltpu.SMEM(count.shape, jnp.int32),
            pltpu.SMEM(parents.shape, jnp.int32),
            pltpu.SemaphoreType.DMA((2,)),
        ],
        compiler_params=PARAMS,
        cost_estimate=COST,
        name="lower",
    )(*[pltpu.with_memory_space_constraint(a, pltpu.HBM) for a in (count, parents)], *xs, basis, up)


def twist(top):
    return jnp.concatenate([-top[:, NRHS:], top[:, :NRHS]], axis=1)


def twisted_rows(tops):
    return jnp.concatenate([rows for top in tops for rows in (top, twist(top))], axis=0)


def late_place(late, perm_ref, groups):
    source = partner(*late)
    group, child = 0, 0
    for i in range(2 * groups):
        hit = perm_ref[i] == source
        group = jnp.where(hit, i // 2, group)
        child = jnp.where(hit, i % 2, child)
    return group, child


def prep_kernel(late, perm_hbm, down_ref, row_ref, after_ref, down_out, row_out, perm_ref, sem):
    groups, local = down_ref.shape[:2]
    width = row_ref.shape[4]
    fetch = pltpu.make_async_copy(perm_hbm, perm_ref, sem.at[0])
    fetch.start()
    fetch.wait()
    group, child = late_place(late, perm_ref, groups)
    for h in range(local):
        block = down_ref[group, h]
        down_out[h] = jnp.where(child == 0, block[:, :width], block[:, width:])
        for t in range(2):
            row_out[h, t] = row_ref[h, t, group]


def prep(late, perm, down, row, after):
    local, rows = down.shape[1:3]
    leaf, width = row.shape[3:]
    vmem = pl.BlockSpec(memory_space=pltpu.VMEM)
    hbm = pl.BlockSpec(memory_space=pltpu.HBM)
    return pl.pallas_call(
        functools.partial(prep_kernel, late),
        out_shape=[
            pltpu.VMEM((local, rows, width), BF16),
            pltpu.VMEM((local, 2, leaf, width), BF16),
        ],
        in_specs=[hbm, vmem, vmem, pl.BlockSpec(memory_space=pl.ANY)],
        out_specs=[vmem] * 2,
        scratch_shapes=[pltpu.SMEM(perm.shape, jnp.int32), pltpu.SemaphoreType.DMA((1,))],
        compiler_params=PARAMS,
        cost_estimate=COST,
        name="prep",
    )(pltpu.with_memory_space_constraint(perm, pltpu.HBM), down, row, after)


def upper_kernel(full, halved, late, perm_hbm, down_ref, row_ref, *refs):
    n, m = len(full), len(halved)
    mids, own_mids, other_mids = refs[:n], refs[n : n + m], refs[n + m : n + 2 * m]
    field_ref, top_ref, spread_ref, perm_ref, sem = refs[n + 2 * m :]
    groups, local = down_ref.shape[:2]
    rank = spread_ref.shape[2] // 2
    fetch = pltpu.make_async_copy(perm_hbm, perm_ref, sem.at[0])
    fetch.start()

    def put(source, h, real, imag):
        spread_ref[source, h, :rank, :NRHS] = real
        spread_ref[source, h, :rank, NRHS:] = imag
        spread_ref[source, h, rank:, :NRHS] = -imag
        spread_ref[source, h, rank:, NRHS:] = real

    left = lax.broadcasted_iota(jnp.int32, (rank, NRHS), 1) < HALF
    for own_ref, other_ref, (k, which) in zip(own_mids, other_mids, halved):
        swap = lax.axis_index("rhs") == 1
        for h in range(local):
            low, high = own_ref[0, h].astype(F32), other_ref[0, h].astype(F32)
            low, high = jnp.where(swap, high, low), jnp.where(swap, low, high)
            real = jnp.where(left, low, pltpu.roll(high, HALF, 1)).astype(BF16)
            imag = jnp.where(left, pltpu.roll(low, HALF, 1), high).astype(BF16)
            put(partner(k, which), h, real, imag)
    for mid_ref, (k, which) in zip(mids, full):
        for h in range(local):
            mid = mid_ref[0, h]
            put(partner(k, which), h, mid[:, :NRHS], mid[:, NRHS:])
    for h in range(local):
        spread_ref[partner(*late), h] = jnp.zeros(spread_ref.shape[2:], BF16)
    fetch.wait()
    group, _ = late_place(late, perm_ref, groups)
    for h in range(local):
        tops = ([], [])
        for q in range(groups):
            parts = [spread_ref[perm_ref[2 * q + s], h] for s in range(2)]
            top = jnp.dot(
                down_ref[q, h], jnp.concatenate(parts, axis=0), preferred_element_type=F32
            )
            lacks = group == q
            top_ref[jnp.where(lacks, 0, 1), h] = top
            top = jnp.where(lacks, jnp.zeros_like(top), top).astype(BF16)
            for t in range(2):
                tops[t].append(top[t * rank : (t + 1) * rank])
        for t in range(2):
            rows = jnp.concatenate([row_ref[h, t, q] for q in range(groups)], axis=1)
            field_ref[h, t] = jnp.dot(rows, twisted_rows(tops[t]), preferred_element_type=F32)


def upper(full, halved, late, perm, down, row, mids):
    groups, local, _, width = down.shape
    leaf = row.shape[3]
    rank = width // 4
    vmem = pl.BlockSpec(memory_space=pltpu.VMEM)
    hbm = pl.BlockSpec(memory_space=pltpu.HBM)
    return pl.pallas_call(
        functools.partial(upper_kernel, full, halved, late),
        out_shape=[
            pltpu.VMEM((local, 2, leaf, 2 * NRHS), F32),
            pltpu.VMEM((2, local, 2 * rank, 2 * NRHS), F32),
        ],
        in_specs=[hbm] + [vmem] * (2 + len(mids)),
        out_specs=[vmem] * 2,
        scratch_shapes=[
            pltpu.VMEM((2 * groups, local, 2 * rank, 2 * NRHS), BF16),
            pltpu.SMEM(perm.shape, jnp.int32),
            pltpu.SemaphoreType.DMA((1,)),
        ],
        compiler_params=PARAMS,
        cost_estimate=COST,
        name="upper",
    )(pltpu.with_memory_space_constraint(perm, pltpu.HBM), down, row, *mids)


def finish_kernel(down_ref, row_ref, field_ref, top_ref, mid_ref, out_hbm, mix_ref, out_ref, sems):
    local, _, leaf, _ = field_ref.shape
    rank = mid_ref.shape[2]
    copies = []
    for i, group in enumerate(chunks(local)):
        for h in group:
            top = top_ref[0, h] + jnp.dot(
                down_ref[h], twisted_rows([mid_ref[0, h]]), preferred_element_type=F32
            )
            top = top.astype(BF16)
            for t in range(2):
                rows = twisted_rows([top[t * rank : (t + 1) * rank]])
                field = field_ref[h, t] + jnp.dot(
                    row_ref[h, t], rows, preferred_element_type=F32
                )
                mix_ref[h, t, pl.ds(0, leaf, stride=2), :] = field[:, :NRHS]
                mix_ref[h, t, pl.ds(1, leaf, stride=2), :] = field[:, NRHS:]
                out_ref[h, t] = mix_ref[h, t].astype(BF16)
        at = pl.ds(group.start, len(group))
        copies.append(pltpu.make_async_copy(out_ref.at[at], out_hbm.at[at], sems.at[i]))
        copies[-1].start()
    for copy in copies:
        copy.wait()


def finish(down, row, field, top, mid):
    local, _, leaf, _ = field.shape
    shape = (local, 2, 2 * leaf, NRHS)
    vmem = pl.BlockSpec(memory_space=pltpu.VMEM)
    return pl.pallas_call(
        finish_kernel,
        out_shape=jax.ShapeDtypeStruct(shape, BF16),
        in_specs=[vmem] * 5,
        out_specs=pl.BlockSpec(memory_space=pltpu.HBM),
        scratch_shapes=[
            pltpu.VMEM(shape, F32),
            pltpu.VMEM(shape, BF16),
            pltpu.SemaphoreType.DMA((2,)),
        ],
        compiler_params=PARAMS,
        cost_estimate=COST,
        name="finish",
    )(down, row, field, top, mid)


def send(block, route, dests):
    code = 2 * route[0] + route[1]
    if not code:
        return block
    return lax.ppermute(block, ("blk", "sub"), [(m, m ^ code) for m in range(dests)])


def on_device(
    columns, x_panels, leaf_basis, leaf_count, parent_map, up_transfer, mid_perm, down_transfer, row_basis
):
    boxes, directions, rank, _, leaf = leaf_basis.shape
    basis = leaf_basis.reshape(boxes, directions, rank * 2, leaf)
    groups, _, local = down_transfer.shape[:3]
    down = down_transfer.reshape(groups, local, 2 * rank, 4 * rank)
    row = row_basis.reshape(local, 2, groups, leaf, 2 * rank)
    x = jnp.transpose(x_panels, (0, 2, 3, 1))
    dests = 2 * columns
    two = both_cores((2,))
    full = both_cores(range(columns - 1, 3, -1)) + [(3, 0), (1, 0), (0, 1), (1, 1), (0, 0)]
    late = (3, 1)
    if 2 * x.shape[2] == NRHS:
        halved = two
        xs = [x, lax.ppermute(x, "rhs", [(0, 1), (1, 0)])]
        *own_mids, basis, up = own(halved, dests, leaf_count, parent_map, x, basis, up_transfer)
        own_mids = [send(mid, route, dests) for mid, route in zip(own_mids, halved)]
    else:
        full, halved, own_mids, up = two + full, [], [], up_transfer
        xs = [lax.all_gather(x, "rhs", axis=2, tiled=True)]
    n = len(full)
    routes = full + [late] + halved
    mids = lower(full + [late], halved, dests, leaf_count, parent_map, xs, basis, up)
    mids = [send(mid, route, dests) for mid, route in zip(mids, routes)]
    down_late, row_late = prep(late, mid_perm, down, row, [*own_mids, mids[0]][0])
    field, top = upper(
        full, halved, late, mid_perm, down, row, [*mids[:n], *own_mids, *mids[n + 1 :]]
    )
    result = finish(down_late, row_late, field, top, mids[n])
    return result.reshape(1, local, 2, leaf, 2, NRHS)


def solution(mesh):
    return jax.shard_map(
        functools.partial(on_device, mesh.shape["blk"]),
        mesh=mesh,
        in_specs=(
            P(("grp", "blk", "sub"), None, None, "rhs"),
            P(("blk", "sub"), "rhs", None, None, None),
            P(("blk", "sub")),
            P("rhs"),
            P(("blk", "sub"), "rhs", None, None),
            P(),
            P(None, "rhs", ("blk", "sub"), None, None, None),
            P("rhs", ("blk", "sub"), None, None, None, None),
        ),
        out_specs=P(("grp", "rhs"), ("blk", "sub"), None, None, None, None),
        check_vma=False,
    )
```

```python
import functools

import jax
import jax.numpy as jnp
from jax import lax
from jax.experimental import pallas as pl
from jax.experimental.pallas import tpu as pltpu
from jax.sharding import PartitionSpec as P

NRHS = 128
HALF = 64
F32 = jnp.float32
BF16 = jnp.bfloat16
PARAMS = pltpu.CompilerParams(vmem_limit_bytes=32 * 1024 * 1024)
COST = pl.CostEstimate(flops=1_000_000, bytes_accessed=10_000, transcendentals=0)


def both_cores(steps):
    return [(k, which) for k in steps for which in (0, 1)]


def partner(k, which):
    z = jnp.bitwise_xor(lax.axis_index("blk"), k)
    core = jnp.bitwise_xor(lax.axis_index("sub"), which)
    return z * 2 + core


def up_stage(outs, routes, parent_ref, up_ref, leaf_ref, cut=lambda mid: mid):
    pairs, local = outs[0].shape[:2]
    for out, (k, which) in zip(outs, routes):
        dest = partner(k, which)
        for p in range(pairs):
            for h in range(local):
                j = dest * local + h
                mid = jnp.dot(
                    up_ref[p, j], leaf_ref[p, parent_ref[j]], preferred_element_type=F32
                )
                out[p, h] = cut(mid).astype(BF16)


def chunks(count):
    middle = (count + 1) // 2
    return [group for group in (range(middle), range(middle, count)) if group]


def leaf_stage(spreads, combine, count_ref, basis_ref, g_ref, leaf_ref, ready):
    boxes, dirs, rows, _ = basis_ref.shape
    rank = rows // 2
    width = leaf_ref.shape[3]
    first = lax.axis_index("rhs") * dirs
    even = pl.ds(0, rank, stride=2)
    odd = pl.ds(1, rank, stride=2)
    for b in range(boxes):
        ready(b)
        spread = spreads(b)
        for d in range(dirs):
            g = lax.dot_general(
                basis_ref[b, d], spread, (((1,), (1,)), ((), ())), preferred_element_type=F32
            )
            g_ref[b * dirs + d, 0] = g[:, :NRHS]
            g_ref[b * dirs + d, 1] = g[:, NRHS:]
        if b == 0:
            ready("count")
        for d in range(dirs):
            slot = b * dirs + d
            live = first + d < count_ref[b]
            pieces = combine(
                [g_ref[slot, i, even, :] for i in range(2)],
                [g_ref[slot, i, odd, :] for i in range(2)],
            )
            pieces = [jnp.where(live, x, jnp.zeros_like(x)).astype(BF16) for x in pieces]
            base = (b % 2) * 2 * rank
            top, bottom = slice(base, base + rank), slice(base + rank, base + 2 * rank)
            if width == NRHS:
                leaf_ref[b // 2, d, top, :] = pieces[0]
                leaf_ref[b // 2, d, bottom, :] = pieces[1]
            else:
                leaf_ref[b // 2, d, top, :NRHS] = pieces[0]
                leaf_ref[b // 2, d, top, NRHS:] = pieces[1]
                leaf_ref[b // 2, d, bottom, :NRHS] = -pieces[1]
                leaf_ref[b // 2, d, bottom, NRHS:] = pieces[0]


def half_columns(even, odd):
    return even[0] + odd[1], even[1] - odd[0]


def all_columns(even, odd):
    return even[0] - odd[1], even[1] + odd[0]


def own_kernel(routes, count_hbm, parent_hbm, x_hbm, basis_hbm, up_hbm, out_ref, basis_ref, up_ref, *refs):
    count_ref, parent_ref, x_ref, leaf_ref, g_ref, sems = refs
    boxes = basis_ref.shape[0]
    copies = {
        "x": pltpu.make_async_copy(x_hbm, x_ref, sems.at[0]),
        "count": pltpu.make_async_copy(count_hbm, count_ref, sems.at[1]),
        "parent": pltpu.make_async_copy(parent_hbm, parent_ref, sems.at[2]),
        "up": pltpu.make_async_copy(up_hbm, up_ref, sems.at[3]),
    }
    for b in range(boxes):
        copies[b] = pltpu.make_async_copy(basis_hbm.at[b], basis_ref.at[b], sems.at[4 + b])
    for name in ["x", 0, "count"] + list(range(1, boxes)) + ["up", "parent"]:
        copies[name].start()
    copies["x"].wait()

    def spreads(b):
        real, imag = x_ref[b, 0], x_ref[b, 1]
        return jnp.concatenate([real, imag, -imag, real], axis=0)

    leaf_stage(
        spreads, half_columns, count_ref, basis_ref, g_ref, leaf_ref, lambda name: copies[name].wait()
    )
    copies["up"].wait()
    copies["parent"].wait()
    outs = [out_ref.at[i] for i in range(len(routes))]
    up_stage(outs, routes, parent_ref, up_ref, leaf_ref)


def own(routes, dests, count, parents, x, basis, up):
    boxes, dirs, rows, _ = basis.shape
    pairs, dirs_up, rank, _ = up.shape
    block = pltpu.VMEM((len(routes), pairs, dirs_up // dests, rank, NRHS), BF16)
    args = [count, parents, x, basis, up]
    return pl.pallas_call(
        functools.partial(own_kernel, routes),
        out_shape=[block, pltpu.VMEM(basis.shape, BF16), pltpu.VMEM(up.shape, BF16)],
        in_specs=[pl.BlockSpec(memory_space=pltpu.HBM)] * 5,
        out_specs=[pl.BlockSpec(memory_space=pltpu.VMEM)] * 3,
        scratch_shapes=[
            pltpu.SMEM(count.shape, jnp.int32),
            pltpu.SMEM(parents.shape, jnp.int32),
            pltpu.VMEM(x.shape, BF16),
            pltpu.VMEM((pairs, dirs, 4 * rank, NRHS), BF16),
            pltpu.VMEM((boxes * dirs, 2, rows, NRHS), F32),
            pltpu.SemaphoreType.DMA((4 + boxes,)),
        ],
        compiler_params=PARAMS,
        cost_estimate=COST,
        name="own",
    )(*[pltpu.with_memory_space_constraint(arg, pltpu.HBM) for arg in args])


def other_columns(mid):
    left = lax.broadcasted_iota(jnp.int32, (mid.shape[0], NRHS), 1) < HALF
    real, imag = mid[:, :NRHS], mid[:, NRHS:]
    low = jnp.where(left, real, pltpu.roll(imag, HALF, 1))
    high = jnp.where(left, pltpu.roll(real, HALF, 1), imag)
    return jnp.where(lax.axis_index("rhs") == 1, low, high)


def lower_kernel(full, halved, count_hbm, parent_hbm, *refs):
    n = len(full) + bool(halved)
    g_ref, leaf_ref, count_ref, parent_ref, sems = refs[-5:]
    outs = refs[-5 - n : -5]
    *xs, basis_ref, up_ref = refs[: -5 - n]
    copies = {
        "count": pltpu.make_async_copy(count_hbm, count_ref, sems.at[0]),
        "parent": pltpu.make_async_copy(parent_hbm, parent_ref, sems.at[1]),
    }
    for copy in copies.values():
        copy.start()

    def ready(name):
        if name in copies:
            copies[name].wait()

    def spreads(b):
        if len(xs) == 1:
            return jnp.concatenate([xs[0][b, 0], xs[0][b, 1]], axis=0)
        own, other = xs[0][b], xs[1][b]
        swap = lax.axis_index("rhs") == 1
        low, high = jnp.where(swap, other, own), jnp.where(swap, own, other)
        return jnp.concatenate([low[0], high[0], low[1], high[1]], axis=0)

    leaf_stage(spreads, all_columns, count_ref, basis_ref, g_ref, leaf_ref, ready)
    ready("parent")
    if halved:
        halves = [outs[-1].at[i] for i in range(len(halved))]
        up_stage(halves, halved, parent_ref, up_ref, leaf_ref, other_columns)
    up_stage(outs[: len(full)], full, parent_ref, up_ref, leaf_ref)


def lower(full, halved, dests, count, parents, xs, basis, up):
    boxes, dirs, rows, _ = basis.shape
    pairs, dirs_up, rank, _ = up.shape
    shape = (pairs, dirs_up // dests, rank)
    hbm = pl.BlockSpec(memory_space=pltpu.HBM)
    vmem = pl.BlockSpec(memory_space=pltpu.VMEM)
    n = len(full) + bool(halved)
    return pl.pallas_call(
        functools.partial(lower_kernel, full, halved),
        out_shape=[pltpu.VMEM(shape + (2 * NRHS,), BF16)] * len(full)
        + [pltpu.VMEM((len(halved),) + shape + (NRHS,), BF16)] * bool(halved),
        in_specs=[hbm, hbm] + [vmem] * (2 + len(xs)),
        out_specs=[vmem] * n,
        scratch_shapes=[
            pltpu.VMEM((boxes * dirs, 2, rows, NRHS), F32),
            pltpu.VMEM((pairs, dirs, 4 * rank, 2 * NRHS), BF16),
            pltpu.SMEM(count.shape, jnp.int32),
            pltpu.SMEM(parents.shape, jnp.int32),
            pltpu.SemaphoreType.DMA((2,)),
        ],
        compiler_params=PARAMS,
        cost_estimate=COST,
        name="lower",
    )(*[pltpu.with_memory_space_constraint(a, pltpu.HBM) for a in (count, parents)], *xs, basis, up)


def twist(top):
    return jnp.concatenate([-top[:, NRHS:], top[:, :NRHS]], axis=1)


def twisted_rows(tops):
    return jnp.concatenate([rows for top in tops for rows in (top, twist(top))], axis=0)


def hand_kernel(own_ref, other_ref, out_ref):
    out_ref[0] = own_ref[1]
    out_ref[1] = other_ref[1]


def hand(own, other):
    vmem = pl.BlockSpec(memory_space=pltpu.VMEM)
    return pl.pallas_call(
        hand_kernel,
        out_shape=pltpu.VMEM(own.shape, BF16),
        in_specs=[vmem] * 2,
        out_specs=vmem,
        compiler_params=PARAMS,
        cost_estimate=COST,
        name="hand",
    )(own, other)


def late_place(late, perm_ref, groups):
    source = partner(*late)
    group, child = 0, 0
    for i in range(2 * groups):
        hit = perm_ref[i] == source
        group = jnp.where(hit, i // 2, group)
        child = jnp.where(hit, i % 2, child)
    return group, child


def prep_kernel(late, perm_hbm, down_ref, row_ref, after_ref, down_out, row_out, perm_ref, sem):
    groups, local = down_ref.shape[:2]
    width = row_ref.shape[4]
    fetch = pltpu.make_async_copy(perm_hbm, perm_ref, sem.at[0])
    fetch.start()
    fetch.wait()
    group, child = late_place(late, perm_ref, groups)
    for h in range(local):
        block = down_ref[group, h]
        down_out[h] = jnp.where(child == 0, block[:, :width], block[:, width:])
        for t in range(2):
            row_out[h, t] = row_ref[h, t, group]


def prep(late, perm, down, row, after):
    local, rows = down.shape[1:3]
    leaf, width = row.shape[3:]
    vmem = pl.BlockSpec(memory_space=pltpu.VMEM)
    hbm = pl.BlockSpec(memory_space=pltpu.HBM)
    return pl.pallas_call(
        functools.partial(prep_kernel, late),
        out_shape=[
            pltpu.VMEM((local, rows, width), BF16),
            pltpu.VMEM((local, 2, leaf, width), BF16),
        ],
        in_specs=[hbm, vmem, vmem, pl.BlockSpec(memory_space=pl.ANY)],
        out_specs=[vmem] * 2,
        scratch_shapes=[pltpu.SMEM(perm.shape, jnp.int32), pltpu.SemaphoreType.DMA((1,))],
        compiler_params=PARAMS,
        cost_estimate=COST,
        name="prep",
    )(pltpu.with_memory_space_constraint(perm, pltpu.HBM), down, row, after)


def upper_kernel(full, halved, late, perm_hbm, down_ref, row_ref, *refs):
    n = len(full)
    mids, (field_ref, top_ref, spread_ref, perm_ref, sem) = refs[:n], refs[-5:]
    halves = []
    if halved:
        own_ref, other_ref, handed_ref = refs[n:-5]
        halves = [(own_ref.at[0], other_ref.at[0]), (handed_ref.at[0], handed_ref.at[1])]
    groups, local = down_ref.shape[:2]
    rank = spread_ref.shape[2] // 2
    fetch = pltpu.make_async_copy(perm_hbm, perm_ref, sem.at[0])
    fetch.start()

    def put(source, h, real, imag):
        spread_ref[source, h, :rank, :NRHS] = real
        spread_ref[source, h, :rank, NRHS:] = imag
        spread_ref[source, h, rank:, :NRHS] = -imag
        spread_ref[source, h, rank:, NRHS:] = real

    left = lax.broadcasted_iota(jnp.int32, (rank, NRHS), 1) < HALF
    for (own_ref, other_ref), (k, which) in zip(halves, halved):
        swap = lax.axis_index("rhs") == 1
        for h in range(local):
            low, high = own_ref[0, h].astype(F32), other_ref[0, h].astype(F32)
            low, high = jnp.where(swap, high, low), jnp.where(swap, low, high)
            real = jnp.where(left, low, pltpu.roll(high, HALF, 1)).astype(BF16)
            imag = jnp.where(left, pltpu.roll(low, HALF, 1), high).astype(BF16)
            put(partner(k, which), h, real, imag)
    for mid_ref, (k, which) in zip(mids, full):
        for h in range(local):
            mid = mid_ref[0, h]
            put(partner(k, which), h, mid[:, :NRHS], mid[:, NRHS:])
    for h in range(local):
        spread_ref[partner(*late), h] = jnp.zeros(spread_ref.shape[2:], BF16)
    fetch.wait()
    group, _ = late_place(late, perm_ref, groups)
    for h in range(local):
        tops = ([], [])
        for q in range(groups):
            parts = [spread_ref[perm_ref[2 * q + s], h] for s in range(2)]
            top = jnp.dot(
                down_ref[q, h], jnp.concatenate(parts, axis=0), preferred_element_type=F32
            )
            lacks = group == q
            top_ref[jnp.where(lacks, 0, 1), h] = top
            top = jnp.where(lacks, jnp.zeros_like(top), top).astype(BF16)
            for t in range(2):
                tops[t].append(top[t * rank : (t + 1) * rank])
        for t in range(2):
            rows = jnp.concatenate([row_ref[h, t, q] for q in range(groups)], axis=1)
            field_ref[h, t] = jnp.dot(rows, twisted_rows(tops[t]), preferred_element_type=F32)


def upper(full, halved, late, perm, down, row, mids):
    groups, local, _, width = down.shape
    leaf = row.shape[3]
    rank = width // 4
    vmem = pl.BlockSpec(memory_space=pltpu.VMEM)
    hbm = pl.BlockSpec(memory_space=pltpu.HBM)
    return pl.pallas_call(
        functools.partial(upper_kernel, full, halved, late),
        out_shape=[
            pltpu.VMEM((local, 2, leaf, 2 * NRHS), F32),
            pltpu.VMEM((2, local, 2 * rank, 2 * NRHS), F32),
        ],
        in_specs=[hbm] + [vmem] * (2 + len(mids)),
        out_specs=[vmem] * 2,
        scratch_shapes=[
            pltpu.VMEM((2 * groups, local, 2 * rank, 2 * NRHS), BF16),
            pltpu.SMEM(perm.shape, jnp.int32),
            pltpu.SemaphoreType.DMA((1,)),
        ],
        compiler_params=PARAMS,
        cost_estimate=COST,
        name="upper",
    )(pltpu.with_memory_space_constraint(perm, pltpu.HBM), down, row, *mids)


def finish_kernel(down_ref, row_ref, field_ref, top_ref, mid_ref, out_hbm, mix_ref, out_ref, sems):
    local, _, leaf, _ = field_ref.shape
    rank = mid_ref.shape[2]
    copies = []
    for i, group in enumerate(chunks(local)):
        for h in group:
            top = top_ref[0, h] + jnp.dot(
                down_ref[h], twisted_rows([mid_ref[0, h]]), preferred_element_type=F32
            )
            top = top.astype(BF16)
            for t in range(2):
                rows = twisted_rows([top[t * rank : (t + 1) * rank]])
                field = field_ref[h, t] + jnp.dot(
                    row_ref[h, t], rows, preferred_element_type=F32
                )
                mix_ref[h, t, pl.ds(0, leaf, stride=2), :] = field[:, :NRHS]
                mix_ref[h, t, pl.ds(1, leaf, stride=2), :] = field[:, NRHS:]
                out_ref[h, t] = mix_ref[h, t].astype(BF16)
        at = pl.ds(group.start, len(group))
        copies.append(pltpu.make_async_copy(out_ref.at[at], out_hbm.at[at], sems.at[i]))
        copies[-1].start()
    for copy in copies:
        copy.wait()


def finish(down, row, field, top, mid):
    local, _, leaf, _ = field.shape
    shape = (local, 2, 2 * leaf, NRHS)
    vmem = pl.BlockSpec(memory_space=pltpu.VMEM)
    return pl.pallas_call(
        finish_kernel,
        out_shape=jax.ShapeDtypeStruct(shape, BF16),
        in_specs=[vmem] * 5,
        out_specs=pl.BlockSpec(memory_space=pltpu.HBM),
        scratch_shapes=[
            pltpu.VMEM(shape, F32),
            pltpu.VMEM(shape, BF16),
            pltpu.SemaphoreType.DMA((2,)),
        ],
        compiler_params=PARAMS,
        cost_estimate=COST,
        name="finish",
    )(down, row, field, top, mid)


def send(block, route, dests):
    code = 2 * route[0] + route[1]
    if not code:
        return block
    return lax.ppermute(block, ("blk", "sub"), [(m, m ^ code) for m in range(dests)])


def on_device(
    columns, x_panels, leaf_basis, leaf_count, parent_map, up_transfer, mid_perm, down_transfer, row_basis
):
    boxes, directions, rank, _, leaf = leaf_basis.shape
    basis = leaf_basis.reshape(boxes, directions, rank * 2, leaf)
    groups, _, local = down_transfer.shape[:3]
    down = down_transfer.reshape(groups, local, 2 * rank, 4 * rank)
    row = row_basis.reshape(local, 2, groups, leaf, 2 * rank)
    x = jnp.transpose(x_panels, (0, 2, 3, 1))
    dests = 2 * columns
    two = both_cores((2,))
    full = both_cores(range(columns - 1, 3, -1)) + [(1, 0), (0, 1), (3, 0), (1, 1), (0, 0)]
    late = (3, 1)
    split = 2 * x.shape[2] == NRHS
    swap = [(0, 1), (1, 0)]
    if split:
        halved = two
        xs = [x, lax.ppermute(x, "rhs", swap)]
        own_two, basis, up = own(halved, dests, leaf_count, parent_map, x, basis, up_transfer)
        own_two = lax.ppermute(own_two, "blk", [(m, m ^ 2) for m in range(columns)])
    else:
        full, halved, up = two + full, [], up_transfer
        xs = [lax.all_gather(x, "rhs", axis=2, tiled=True)]
    n = len(full)
    mids = lower(full + [late], halved, dests, leaf_count, parent_map, xs, basis, up)
    halves = []
    if split:
        other_two = lax.ppermute(mids[-1], "blk", [(m, m ^ 2) for m in range(columns)])
        halves = [own_two, other_two, lax.ppermute(hand(own_two, other_two), "sub", swap)]
    mids = [send(mid, route, dests) for mid, route in zip(mids, full + [late])]
    down_late, row_late = prep(late, mid_perm, down, row, (halves + mids)[0])
    field, top = upper(full, halved, late, mid_perm, down, row, [*mids[:n], *halves])
    result = finish(down_late, row_late, field, top, mids[n])
    return result.reshape(1, local, 2, leaf, 2, NRHS)


def solution(mesh):
    return jax.shard_map(
        functools.partial(on_device, mesh.shape["blk"]),
        mesh=mesh,
        in_specs=(
            P(("grp", "blk", "sub"), None, None, "rhs"),
            P(("blk", "sub"), "rhs", None, None, None),
            P(("blk", "sub")),
            P("rhs"),
            P(("blk", "sub"), "rhs", None, None),
            P(),
            P(None, "rhs", ("blk", "sub"), None, None, None),
            P("rhs", ("blk", "sub"), None, None, None, None),
        ),
        out_specs=P(("grp", "rhs"), ("blk", "sub"), None, None, None, None),
        check_vma=False,
    )
```

```python
import functools

import jax
import jax.numpy as jnp
from jax import lax
from jax.experimental import pallas as pl
from jax.experimental.pallas import tpu as pltpu
from jax.sharding import PartitionSpec as P

NRHS = 128
HALF = 64
F32 = jnp.float32
BF16 = jnp.bfloat16
PARAMS = pltpu.CompilerParams(vmem_limit_bytes=32 * 1024 * 1024)
COST = pl.CostEstimate(flops=1_000_000, bytes_accessed=10_000, transcendentals=0)


def both_cores(steps):
    return [(k, which) for k in steps for which in (0, 1)]


def partner(k, which):
    z = jnp.bitwise_xor(lax.axis_index("blk"), k)
    core = jnp.bitwise_xor(lax.axis_index("sub"), which)
    return z * 2 + core


def up_stage(outs, routes, parent_ref, up_ref, leaf_ref, cut=lambda mid: mid):
    pairs, local = outs[0].shape[:2]
    for out, (k, which) in zip(outs, routes):
        dest = partner(k, which)
        for p in range(pairs):
            for h in range(local):
                j = dest * local + h
                mid = jnp.dot(
                    up_ref[p, j], leaf_ref[p, parent_ref[j]], preferred_element_type=F32
                )
                out[p, h] = cut(mid).astype(BF16)


def chunks(count):
    middle = (count + 1) // 2
    return [group for group in (range(middle), range(middle, count)) if group]


def leaf_stage(spreads, combine, count_ref, basis_ref, g_ref, leaf_ref, ready):
    boxes, dirs, rows, _ = basis_ref.shape
    rank = rows // 2
    width = leaf_ref.shape[3]
    first = lax.axis_index("rhs") * dirs
    even = pl.ds(0, rank, stride=2)
    odd = pl.ds(1, rank, stride=2)
    for b in range(boxes):
        ready(b)
        spread = spreads(b)
        for d in range(dirs):
            g = lax.dot_general(
                basis_ref[b, d], spread, (((1,), (1,)), ((), ())), preferred_element_type=F32
            )
            g_ref[b * dirs + d, 0] = g[:, :NRHS]
            g_ref[b * dirs + d, 1] = g[:, NRHS:]
        if b == 0:
            ready("count")
        for d in range(dirs):
            slot = b * dirs + d
            live = first + d < count_ref[b]
            pieces = combine(
                [g_ref[slot, i, even, :] for i in range(2)],
                [g_ref[slot, i, odd, :] for i in range(2)],
            )
            pieces = [jnp.where(live, x, jnp.zeros_like(x)).astype(BF16) for x in pieces]
            base = (b % 2) * 2 * rank
            top, bottom = slice(base, base + rank), slice(base + rank, base + 2 * rank)
            if width == NRHS:
                leaf_ref[b // 2, d, top, :] = pieces[0]
                leaf_ref[b // 2, d, bottom, :] = pieces[1]
            else:
                leaf_ref[b // 2, d, top, :NRHS] = pieces[0]
                leaf_ref[b // 2, d, top, NRHS:] = pieces[1]
                leaf_ref[b // 2, d, bottom, :NRHS] = -pieces[1]
                leaf_ref[b // 2, d, bottom, NRHS:] = pieces[0]


def half_columns(even, odd):
    return even[0] + odd[1], even[1] - odd[0]


def all_columns(even, odd):
    return even[0] - odd[1], even[1] + odd[0]


def own_kernel(routes, count_hbm, parent_hbm, x_hbm, basis_hbm, up_hbm, out_ref, basis_ref, up_ref, *refs):
    count_ref, parent_ref, x_ref, leaf_ref, g_ref, sems = refs
    boxes = basis_ref.shape[0]
    copies = {
        "x": pltpu.make_async_copy(x_hbm, x_ref, sems.at[0]),
        "count": pltpu.make_async_copy(count_hbm, count_ref, sems.at[1]),
        "parent": pltpu.make_async_copy(parent_hbm, parent_ref, sems.at[2]),
        "up": pltpu.make_async_copy(up_hbm, up_ref, sems.at[3]),
    }
    for b in range(boxes):
        copies[b] = pltpu.make_async_copy(basis_hbm.at[b], basis_ref.at[b], sems.at[4 + b])
    for name in ["x", 0, "count"] + list(range(1, boxes)) + ["up", "parent"]:
        copies[name].start()
    copies["x"].wait()

    def spreads(b):
        real, imag = x_ref[b, 0], x_ref[b, 1]
        return jnp.concatenate([real, imag, -imag, real], axis=0)

    leaf_stage(
        spreads, half_columns, count_ref, basis_ref, g_ref, leaf_ref, lambda name: copies[name].wait()
    )
    copies["up"].wait()
    copies["parent"].wait()
    outs = [out_ref.at[i] for i in range(len(routes))]
    up_stage(outs, routes, parent_ref, up_ref, leaf_ref)


def own(routes, dests, count, parents, x, basis, up):
    boxes, dirs, rows, _ = basis.shape
    pairs, dirs_up, rank, _ = up.shape
    block = pltpu.VMEM((len(routes), pairs, dirs_up // dests, rank, NRHS), BF16)
    args = [count, parents, x, basis, up]
    return pl.pallas_call(
        functools.partial(own_kernel, routes),
        out_shape=[block, pltpu.VMEM(basis.shape, BF16), pltpu.VMEM(up.shape, BF16)],
        in_specs=[pl.BlockSpec(memory_space=pltpu.HBM)] * 5,
        out_specs=[pl.BlockSpec(memory_space=pltpu.VMEM)] * 3,
        scratch_shapes=[
            pltpu.SMEM(count.shape, jnp.int32),
            pltpu.SMEM(parents.shape, jnp.int32),
            pltpu.VMEM(x.shape, BF16),
            pltpu.VMEM((pairs, dirs, 4 * rank, NRHS), BF16),
            pltpu.VMEM((boxes * dirs, 2, rows, NRHS), F32),
            pltpu.SemaphoreType.DMA((4 + boxes,)),
        ],
        compiler_params=PARAMS,
        cost_estimate=COST,
        name="own",
    )(*[pltpu.with_memory_space_constraint(arg, pltpu.HBM) for arg in args])


def other_columns(mid):
    left = lax.broadcasted_iota(jnp.int32, (mid.shape[0], NRHS), 1) < HALF
    real, imag = mid[:, :NRHS], mid[:, NRHS:]
    low = jnp.where(left, real, pltpu.roll(imag, HALF, 1))
    high = jnp.where(left, pltpu.roll(real, HALF, 1), imag)
    return jnp.where(lax.axis_index("rhs") == 1, low, high)


def lower_kernel(full, halved, count_hbm, parent_hbm, *refs):
    n = len(full) + bool(halved)
    g_ref, leaf_ref, count_ref, parent_ref, sems = refs[-5:]
    outs = refs[-5 - n : -5]
    *xs, basis_ref, up_ref = refs[: -5 - n]
    copies = {
        "count": pltpu.make_async_copy(count_hbm, count_ref, sems.at[0]),
        "parent": pltpu.make_async_copy(parent_hbm, parent_ref, sems.at[1]),
    }
    for copy in copies.values():
        copy.start()

    def ready(name):
        if name in copies:
            copies[name].wait()

    def spreads(b):
        if len(xs) == 1:
            return jnp.concatenate([xs[0][b, 0], xs[0][b, 1]], axis=0)
        own, other = xs[0][b], xs[1][b]
        swap = lax.axis_index("rhs") == 1
        low, high = jnp.where(swap, other, own), jnp.where(swap, own, other)
        return jnp.concatenate([low[0], high[0], low[1], high[1]], axis=0)

    leaf_stage(spreads, all_columns, count_ref, basis_ref, g_ref, leaf_ref, ready)
    ready("parent")
    if halved:
        halves = [outs[-1].at[i] for i in range(len(halved))]
        up_stage(halves, halved, parent_ref, up_ref, leaf_ref, other_columns)
    up_stage(outs[: len(full)], full, parent_ref, up_ref, leaf_ref)


def lower(full, halved, dests, count, parents, xs, basis, up):
    boxes, dirs, rows, _ = basis.shape
    pairs, dirs_up, rank, _ = up.shape
    shape = (pairs, dirs_up // dests, rank)
    hbm = pl.BlockSpec(memory_space=pltpu.HBM)
    vmem = pl.BlockSpec(memory_space=pltpu.VMEM)
    n = len(full) + bool(halved)
    return pl.pallas_call(
        functools.partial(lower_kernel, full, halved),
        out_shape=[pltpu.VMEM(shape + (2 * NRHS,), BF16)] * len(full)
        + [pltpu.VMEM((len(halved),) + shape + (NRHS,), BF16)] * bool(halved),
        in_specs=[hbm, hbm] + [vmem] * (2 + len(xs)),
        out_specs=[vmem] * n,
        scratch_shapes=[
            pltpu.VMEM((boxes * dirs, 2, rows, NRHS), F32),
            pltpu.VMEM((pairs, dirs, 4 * rank, 2 * NRHS), BF16),
            pltpu.SMEM(count.shape, jnp.int32),
            pltpu.SMEM(parents.shape, jnp.int32),
            pltpu.SemaphoreType.DMA((2,)),
        ],
        compiler_params=PARAMS,
        cost_estimate=COST,
        name="lower",
    )(*[pltpu.with_memory_space_constraint(a, pltpu.HBM) for a in (count, parents)], *xs, basis, up)


def twist(top):
    return jnp.concatenate([-top[:, NRHS:], top[:, :NRHS]], axis=1)


def twisted_rows(tops):
    return jnp.concatenate([rows for top in tops for rows in (top, twist(top))], axis=0)


def hand_kernel(own_ref, other_ref, out_ref):
    out_ref[0] = own_ref[1]
    out_ref[1] = other_ref[1]


def hand(own, other):
    vmem = pl.BlockSpec(memory_space=pltpu.VMEM)
    return pl.pallas_call(
        hand_kernel,
        out_shape=pltpu.VMEM(own.shape, BF16),
        in_specs=[vmem] * 2,
        out_specs=vmem,
        compiler_params=PARAMS,
        cost_estimate=COST,
        name="hand",
    )(own, other)


def late_place(late, perm_ref, groups):
    source = partner(*late)
    group, child = 0, 0
    for i in range(2 * groups):
        hit = perm_ref[i] == source
        group = jnp.where(hit, i // 2, group)
        child = jnp.where(hit, i % 2, child)
    return group, child


def prep_kernel(late, perm_hbm, down_ref, row_ref, after_ref, down_out, row_out, perm_ref, sem):
    groups, local = down_ref.shape[:2]
    width = row_ref.shape[4]
    fetch = pltpu.make_async_copy(perm_hbm, perm_ref, sem.at[0])
    fetch.start()
    fetch.wait()
    group, child = late_place(late, perm_ref, groups)
    for h in range(local):
        block = down_ref[group, h]
        down_out[h] = jnp.where(child == 0, block[:, :width], block[:, width:])
        for t in range(2):
            row_out[h, t] = row_ref[h, t, group]


def prep(late, perm, down, row, after):
    local, rows = down.shape[1:3]
    leaf, width = row.shape[3:]
    vmem = pl.BlockSpec(memory_space=pltpu.VMEM)
    hbm = pl.BlockSpec(memory_space=pltpu.HBM)
    return pl.pallas_call(
        functools.partial(prep_kernel, late),
        out_shape=[
            pltpu.VMEM((local, rows, width), BF16),
            pltpu.VMEM((local, 2, leaf, width), BF16),
        ],
        in_specs=[hbm, vmem, vmem, pl.BlockSpec(memory_space=pl.ANY)],
        out_specs=[vmem] * 2,
        scratch_shapes=[pltpu.SMEM(perm.shape, jnp.int32), pltpu.SemaphoreType.DMA((1,))],
        compiler_params=PARAMS,
        cost_estimate=COST,
        name="prep",
    )(pltpu.with_memory_space_constraint(perm, pltpu.HBM), down, row, after)


def upper_kernel(full, halved, late, perm_hbm, down_ref, row_ref, *refs):
    n = len(full)
    mids, (field_ref, top_ref, spread_ref, perm_ref, sem) = refs[:n], refs[-5:]
    halves = []
    if halved:
        own_ref, other_ref, handed_ref = refs[n:-5]
        halves = [(own_ref.at[0], other_ref.at[0]), (handed_ref.at[0], handed_ref.at[1])]
    groups, local = down_ref.shape[:2]
    rank = spread_ref.shape[2] // 2
    fetch = pltpu.make_async_copy(perm_hbm, perm_ref, sem.at[0])
    fetch.start()

    def put(source, h, real, imag):
        spread_ref[source, h, :rank, :NRHS] = real
        spread_ref[source, h, :rank, NRHS:] = imag
        spread_ref[source, h, rank:, :NRHS] = -imag
        spread_ref[source, h, rank:, NRHS:] = real

    left = lax.broadcasted_iota(jnp.int32, (rank, NRHS), 1) < HALF
    for (own_ref, other_ref), (k, which) in zip(halves, halved):
        swap = lax.axis_index("rhs") == 1
        for h in range(local):
            low, high = own_ref[0, h].astype(F32), other_ref[0, h].astype(F32)
            low, high = jnp.where(swap, high, low), jnp.where(swap, low, high)
            real = jnp.where(left, low, pltpu.roll(high, HALF, 1)).astype(BF16)
            imag = jnp.where(left, pltpu.roll(low, HALF, 1), high).astype(BF16)
            put(partner(k, which), h, real, imag)
    for mid_ref, (k, which) in zip(mids, full):
        for h in range(local):
            mid = mid_ref[0, h]
            put(partner(k, which), h, mid[:, :NRHS], mid[:, NRHS:])
    for h in range(local):
        spread_ref[partner(*late), h] = jnp.zeros(spread_ref.shape[2:], BF16)
    fetch.wait()
    group, _ = late_place(late, perm_ref, groups)
    for h in range(local):
        tops = ([], [])
        for q in range(groups):
            parts = [spread_ref[perm_ref[2 * q + s], h] for s in range(2)]
            top = jnp.dot(
                down_ref[q, h], jnp.concatenate(parts, axis=0), preferred_element_type=F32
            )
            lacks = group == q
            top_ref[jnp.where(lacks, 0, 1), h] = top
            top = jnp.where(lacks, jnp.zeros_like(top), top).astype(BF16)
            for t in range(2):
                tops[t].append(top[t * rank : (t + 1) * rank])
        for t in range(2):
            rows = jnp.concatenate([row_ref[h, t, q] for q in range(groups)], axis=1)
            field_ref[h, t] = jnp.dot(rows, twisted_rows(tops[t]), preferred_element_type=F32)


def upper(full, halved, late, perm, down, row, mids):
    groups, local, _, width = down.shape
    leaf = row.shape[3]
    rank = width // 4
    vmem = pl.BlockSpec(memory_space=pltpu.VMEM)
    hbm = pl.BlockSpec(memory_space=pltpu.HBM)
    return pl.pallas_call(
        functools.partial(upper_kernel, full, halved, late),
        out_shape=[
            pltpu.VMEM((local, 2, leaf, 2 * NRHS), F32),
            pltpu.VMEM((2, local, 2 * rank, 2 * NRHS), F32),
        ],
        in_specs=[hbm] + [vmem] * (2 + len(mids)),
        out_specs=[vmem] * 2,
        scratch_shapes=[
            pltpu.VMEM((2 * groups, local, 2 * rank, 2 * NRHS), BF16),
            pltpu.SMEM(perm.shape, jnp.int32),
            pltpu.SemaphoreType.DMA((1,)),
        ],
        compiler_params=PARAMS,
        cost_estimate=COST,
        name="upper",
    )(pltpu.with_memory_space_constraint(perm, pltpu.HBM), down, row, *mids)


def finish_kernel(down_ref, row_ref, field_ref, top_ref, mid_ref, out_hbm, mix_ref, out_ref, sems):
    local, _, leaf, _ = field_ref.shape
    rank = mid_ref.shape[2]
    copies = []
    for i, group in enumerate(chunks(local)):
        for h in group:
            top = top_ref[0, h] + jnp.dot(
                down_ref[h], twisted_rows([mid_ref[0, h]]), preferred_element_type=F32
            )
            top = top.astype(BF16)
            for t in range(2):
                rows = twisted_rows([top[t * rank : (t + 1) * rank]])
                field = field_ref[h, t] + jnp.dot(
                    row_ref[h, t], rows, preferred_element_type=F32
                )
                mix_ref[h, t, pl.ds(0, leaf, stride=2), :] = field[:, :NRHS]
                mix_ref[h, t, pl.ds(1, leaf, stride=2), :] = field[:, NRHS:]
                out_ref[h, t] = mix_ref[h, t].astype(BF16)
        at = pl.ds(group.start, len(group))
        copies.append(pltpu.make_async_copy(out_ref.at[at], out_hbm.at[at], sems.at[i]))
        copies[-1].start()
    for copy in copies:
        copy.wait()


def finish(down, row, field, top, mid):
    local, _, leaf, _ = field.shape
    shape = (local, 2, 2 * leaf, NRHS)
    vmem = pl.BlockSpec(memory_space=pltpu.VMEM)
    return pl.pallas_call(
        finish_kernel,
        out_shape=jax.ShapeDtypeStruct(shape, BF16),
        in_specs=[vmem] * 5,
        out_specs=pl.BlockSpec(memory_space=pltpu.HBM),
        scratch_shapes=[
            pltpu.VMEM(shape, F32),
            pltpu.VMEM(shape, BF16),
            pltpu.SemaphoreType.DMA((2,)),
        ],
        compiler_params=PARAMS,
        cost_estimate=COST,
        name="finish",
    )(down, row, field, top, mid)


def send(block, route, dests):
    code = 2 * route[0] + route[1]
    if not code:
        return block
    return lax.ppermute(block, ("blk", "sub"), [(m, m ^ code) for m in range(dests)])


def on_device(
    columns, x_panels, leaf_basis, leaf_count, parent_map, up_transfer, mid_perm, down_transfer, row_basis
):
    boxes, directions, rank, _, leaf = leaf_basis.shape
    basis = leaf_basis.reshape(boxes, directions, rank * 2, leaf)
    groups, _, local = down_transfer.shape[:3]
    down = down_transfer.reshape(groups, local, 2 * rank, 4 * rank)
    row = row_basis.reshape(local, 2, groups, leaf, 2 * rank)
    x = jnp.transpose(x_panels, (0, 2, 3, 1))
    dests = 2 * columns
    two = both_cores((2,))
    full = both_cores(range(columns - 1, 3, -1)) + [(0, 1), (1, 0), (3, 0), (1, 1), (0, 0)]
    late = (3, 1)
    split = 2 * x.shape[2] == NRHS
    swap = [(0, 1), (1, 0)]
    if split:
        halved = two
        xs = [x, lax.ppermute(x, "rhs", swap)]
        own_two, basis, up = own(halved, dests, leaf_count, parent_map, x, basis, up_transfer)
        own_two = lax.ppermute(own_two, "blk", [(m, m ^ 2) for m in range(columns)])
    else:
        full, halved, up = two + full, [], up_transfer
        xs = [lax.all_gather(x, "rhs", axis=2, tiled=True)]
    n = len(full)
    mids = lower(full + [late], halved, dests, leaf_count, parent_map, xs, basis, up)
    halves = []
    if split:
        other_two = lax.ppermute(mids[-1], "blk", [(m, m ^ 2) for m in range(columns)])
        halves = [own_two, other_two, lax.ppermute(hand(own_two, other_two), "sub", swap)]
    mids = [send(mid, route, dests) for mid, route in zip(mids, full + [late])]
    down_late, row_late = prep(late, mid_perm, down, row, (halves + mids)[0])
    field, top = upper(full, halved, late, mid_perm, down, row, [*mids[:n], *halves])
    result = finish(down_late, row_late, field, top, mids[n])
    return result.reshape(1, local, 2, leaf, 2, NRHS)


def solution(mesh):
    return jax.shard_map(
        functools.partial(on_device, mesh.shape["blk"]),
        mesh=mesh,
        in_specs=(
            P(("grp", "blk", "sub"), None, None, "rhs"),
            P(("blk", "sub"), "rhs", None, None, None),
            P(("blk", "sub")),
            P("rhs"),
            P(("blk", "sub"), "rhs", None, None),
            P(),
            P(None, "rhs", ("blk", "sub"), None, None, None),
            P("rhs", ("blk", "sub"), None, None, None, None),
        ),
        out_specs=P(("grp", "rhs"), ("blk", "sub"), None, None, None, None),
        check_vma=False,
    )
```

```python
import functools

import jax
import jax.numpy as jnp
from jax import lax
from jax.experimental import pallas as pl
from jax.experimental.pallas import tpu as pltpu
from jax.sharding import PartitionSpec as P

NRHS = 128
HALF = 64
F32 = jnp.float32
BF16 = jnp.bfloat16
PARAMS = pltpu.CompilerParams(vmem_limit_bytes=32 * 1024 * 1024)
COST = pl.CostEstimate(flops=1_000_000, bytes_accessed=10_000, transcendentals=0)


def both_cores(steps):
    return [(k, which) for k in steps for which in (0, 1)]


def partner(k, which):
    z = jnp.bitwise_xor(lax.axis_index("blk"), k)
    core = jnp.bitwise_xor(lax.axis_index("sub"), which)
    return z * 2 + core


def up_stage(outs, routes, parent_ref, up_ref, leaf_ref, cut=lambda mid: mid):
    pairs, local = outs[0].shape[:2]
    for out, (k, which) in zip(outs, routes):
        dest = partner(k, which)
        for p in range(pairs):
            for h in range(local):
                j = dest * local + h
                mid = jnp.dot(
                    up_ref[p, j], leaf_ref[p, parent_ref[j]], preferred_element_type=F32
                )
                out[p, h] = cut(mid).astype(BF16)


def chunks(count):
    middle = (count + 1) // 2
    return [group for group in (range(middle), range(middle, count)) if group]


def leaf_stage(spreads, combine, count_ref, basis_ref, g_ref, leaf_ref, ready):
    boxes, dirs, rows, _ = basis_ref.shape
    rank = rows // 2
    width = leaf_ref.shape[3]
    first = lax.axis_index("rhs") * dirs
    even = pl.ds(0, rank, stride=2)
    odd = pl.ds(1, rank, stride=2)
    for b in range(boxes):
        ready(b)
        spread = spreads(b)
        for d in range(dirs):
            g = lax.dot_general(
                basis_ref[b, d], spread, (((1,), (1,)), ((), ())), preferred_element_type=F32
            )
            g_ref[b * dirs + d, 0] = g[:, :NRHS]
            g_ref[b * dirs + d, 1] = g[:, NRHS:]
        if b == 0:
            ready("count")
        for d in range(dirs):
            slot = b * dirs + d
            live = first + d < count_ref[b]
            pieces = combine(
                [g_ref[slot, i, even, :] for i in range(2)],
                [g_ref[slot, i, odd, :] for i in range(2)],
            )
            pieces = [jnp.where(live, x, jnp.zeros_like(x)).astype(BF16) for x in pieces]
            base = (b % 2) * 2 * rank
            top, bottom = slice(base, base + rank), slice(base + rank, base + 2 * rank)
            if width == NRHS:
                leaf_ref[b // 2, d, top, :] = pieces[0]
                leaf_ref[b // 2, d, bottom, :] = pieces[1]
            else:
                leaf_ref[b // 2, d, top, :NRHS] = pieces[0]
                leaf_ref[b // 2, d, top, NRHS:] = pieces[1]
                leaf_ref[b // 2, d, bottom, :NRHS] = -pieces[1]
                leaf_ref[b // 2, d, bottom, NRHS:] = pieces[0]


def half_columns(even, odd):
    return even[0] + odd[1], even[1] - odd[0]


def all_columns(even, odd):
    return even[0] - odd[1], even[1] + odd[0]


def own_kernel(routes, count_hbm, parent_hbm, x_hbm, basis_hbm, up_hbm, out_ref, basis_ref, up_ref, *refs):
    count_ref, parent_ref, x_ref, leaf_ref, g_ref, sems = refs
    boxes = basis_ref.shape[0]
    copies = {
        "x": pltpu.make_async_copy(x_hbm, x_ref, sems.at[0]),
        "count": pltpu.make_async_copy(count_hbm, count_ref, sems.at[1]),
        "parent": pltpu.make_async_copy(parent_hbm, parent_ref, sems.at[2]),
        "up": pltpu.make_async_copy(up_hbm, up_ref, sems.at[3]),
    }
    for b in range(boxes):
        copies[b] = pltpu.make_async_copy(basis_hbm.at[b], basis_ref.at[b], sems.at[4 + b])
    for name in ["x", 0, "count"] + list(range(1, boxes)) + ["up", "parent"]:
        copies[name].start()
    copies["x"].wait()

    def spreads(b):
        real, imag = x_ref[b, 0], x_ref[b, 1]
        return jnp.concatenate([real, imag, -imag, real], axis=0)

    leaf_stage(
        spreads, half_columns, count_ref, basis_ref, g_ref, leaf_ref, lambda name: copies[name].wait()
    )
    copies["up"].wait()
    copies["parent"].wait()
    outs = [out_ref.at[i] for i in range(len(routes))]
    up_stage(outs, routes, parent_ref, up_ref, leaf_ref)


def own(routes, dests, count, parents, x, basis, up):
    boxes, dirs, rows, _ = basis.shape
    pairs, dirs_up, rank, _ = up.shape
    block = pltpu.VMEM((len(routes), pairs, dirs_up // dests, rank, NRHS), BF16)
    args = [count, parents, x, basis, up]
    return pl.pallas_call(
        functools.partial(own_kernel, routes),
        out_shape=[block, pltpu.VMEM(basis.shape, BF16), pltpu.VMEM(up.shape, BF16)],
        in_specs=[pl.BlockSpec(memory_space=pltpu.HBM)] * 5,
        out_specs=[pl.BlockSpec(memory_space=pltpu.VMEM)] * 3,
        scratch_shapes=[
            pltpu.SMEM(count.shape, jnp.int32),
            pltpu.SMEM(parents.shape, jnp.int32),
            pltpu.VMEM(x.shape, BF16),
            pltpu.VMEM((pairs, dirs, 4 * rank, NRHS), BF16),
            pltpu.VMEM((boxes * dirs, 2, rows, NRHS), F32),
            pltpu.SemaphoreType.DMA((4 + boxes,)),
        ],
        compiler_params=PARAMS,
        cost_estimate=COST,
        name="own",
    )(*[pltpu.with_memory_space_constraint(arg, pltpu.HBM) for arg in args])


def other_columns(mid):
    left = lax.broadcasted_iota(jnp.int32, (mid.shape[0], NRHS), 1) < HALF
    real, imag = mid[:, :NRHS], mid[:, NRHS:]
    low = jnp.where(left, real, pltpu.roll(imag, HALF, 1))
    high = jnp.where(left, pltpu.roll(real, HALF, 1), imag)
    return jnp.where(lax.axis_index("rhs") == 1, low, high)


def lower_kernel(full, halved, count_hbm, parent_hbm, *refs):
    n = len(full) + bool(halved)
    g_ref, leaf_ref, count_ref, parent_ref, sems = refs[-5:]
    outs = refs[-5 - n : -5]
    *xs, basis_ref, up_ref = refs[: -5 - n]
    copies = {
        "count": pltpu.make_async_copy(count_hbm, count_ref, sems.at[0]),
        "parent": pltpu.make_async_copy(parent_hbm, parent_ref, sems.at[1]),
    }
    for copy in copies.values():
        copy.start()

    def ready(name):
        if name in copies:
            copies[name].wait()

    def spreads(b):
        if len(xs) == 1:
            return jnp.concatenate([xs[0][b, 0], xs[0][b, 1]], axis=0)
        own, other = xs[0][b], xs[1][b]
        swap = lax.axis_index("rhs") == 1
        low, high = jnp.where(swap, other, own), jnp.where(swap, own, other)
        return jnp.concatenate([low[0], high[0], low[1], high[1]], axis=0)

    leaf_stage(spreads, all_columns, count_ref, basis_ref, g_ref, leaf_ref, ready)
    ready("parent")
    if halved:
        halves = [outs[-1].at[i] for i in range(len(halved))]
        up_stage(halves, halved, parent_ref, up_ref, leaf_ref, other_columns)
    up_stage(outs[: len(full)], full, parent_ref, up_ref, leaf_ref)


def lower(full, halved, dests, count, parents, xs, basis, up):
    boxes, dirs, rows, _ = basis.shape
    pairs, dirs_up, rank, _ = up.shape
    shape = (pairs, dirs_up // dests, rank)
    hbm = pl.BlockSpec(memory_space=pltpu.HBM)
    vmem = pl.BlockSpec(memory_space=pltpu.VMEM)
    n = len(full) + bool(halved)
    return pl.pallas_call(
        functools.partial(lower_kernel, full, halved),
        out_shape=[pltpu.VMEM(shape + (2 * NRHS,), BF16)] * len(full)
        + [pltpu.VMEM((len(halved),) + shape + (NRHS,), BF16)] * bool(halved),
        in_specs=[hbm, hbm] + [vmem] * (2 + len(xs)),
        out_specs=[vmem] * n,
        scratch_shapes=[
            pltpu.VMEM((boxes * dirs, 2, rows, NRHS), F32),
            pltpu.VMEM((pairs, dirs, 4 * rank, 2 * NRHS), BF16),
            pltpu.SMEM(count.shape, jnp.int32),
            pltpu.SMEM(parents.shape, jnp.int32),
            pltpu.SemaphoreType.DMA((2,)),
        ],
        compiler_params=PARAMS,
        cost_estimate=COST,
        name="lower",
    )(*[pltpu.with_memory_space_constraint(a, pltpu.HBM) for a in (count, parents)], *xs, basis, up)


def twist(top):
    return jnp.concatenate([-top[:, NRHS:], top[:, :NRHS]], axis=1)


def twisted_rows(tops):
    return jnp.concatenate([rows for top in tops for rows in (top, twist(top))], axis=0)


def hand_kernel(own_ref, other_ref, out_ref):
    out_ref[0] = own_ref[1]
    out_ref[1] = other_ref[1]


def hand(own, other):
    vmem = pl.BlockSpec(memory_space=pltpu.VMEM)
    return pl.pallas_call(
        hand_kernel,
        out_shape=pltpu.VMEM(own.shape, BF16),
        in_specs=[vmem] * 2,
        out_specs=vmem,
        compiler_params=PARAMS,
        cost_estimate=COST,
        name="hand",
    )(own, other)


def late_groups(late, perm_ref, groups):
    found = []
    for route in late:
        source = partner(*route)
        group, child = 0, 0
        for i in range(2 * groups):
            hit = perm_ref[i] == source
            group = jnp.where(hit, i // 2, group)
            child = jnp.where(hit, i % 2, child)
        found.append((group, child))
    return found


def prep_kernel(late, perm_hbm, down_ref, row_ref, after_ref, down_out, row_out, perm_ref, sem):
    groups, local, rows = down_ref.shape[:3]
    width = row_ref.shape[4]
    fetch = pltpu.make_async_copy(perm_hbm, perm_ref, sem.at[0])
    fetch.start()
    fetch.wait()
    found = late_groups(late, perm_ref, groups)
    same = found[0][0] == found[1][0]
    for h in range(local):
        for i, (group, _) in enumerate(found):
            block = down_ref[group, h]
            for j, (_, child) in enumerate(found):
                part = jnp.where(child == 0, block[:, :width], block[:, width:])
                zeros = jnp.zeros_like(part)
                if i == 0 and j == 1:
                    part = jnp.where(same, part, zeros)
                elif i == 1:
                    part = zeros if j == 0 else jnp.where(same, zeros, part)
                down_out[h, i * rows : (i + 1) * rows, j * width : (j + 1) * width] = part
            for t in range(2):
                row_out[h, t, :, i * width : (i + 1) * width] = row_ref[h, t, group]


def prep(late, perm, down, row, after):
    local, rows = down.shape[1:3]
    leaf, width = row.shape[3:]
    vmem = pl.BlockSpec(memory_space=pltpu.VMEM)
    hbm = pl.BlockSpec(memory_space=pltpu.HBM)
    return pl.pallas_call(
        functools.partial(prep_kernel, late),
        out_shape=[
            pltpu.VMEM((local, 2 * rows, 2 * width), BF16),
            pltpu.VMEM((local, 2, leaf, 2 * width), BF16),
        ],
        in_specs=[hbm, vmem, vmem, pl.BlockSpec(memory_space=pl.ANY)],
        out_specs=[vmem] * 2,
        scratch_shapes=[pltpu.SMEM(perm.shape, jnp.int32), pltpu.SemaphoreType.DMA((1,))],
        compiler_params=PARAMS,
        cost_estimate=COST,
        name="prep",
    )(pltpu.with_memory_space_constraint(perm, pltpu.HBM), down, row, after)


def upper_kernel(full, halved, late, perm_hbm, down_ref, row_ref, *refs):
    n = len(full)
    mids, (field_ref, top_ref, spread_ref, perm_ref, sem) = refs[:n], refs[-5:]
    halves = []
    if halved:
        own_ref, other_ref, handed_ref = refs[n:-5]
        halves = [(own_ref.at[0], other_ref.at[0]), (handed_ref.at[0], handed_ref.at[1])]
    groups, local = down_ref.shape[:2]
    rank = spread_ref.shape[2] // 2
    fetch = pltpu.make_async_copy(perm_hbm, perm_ref, sem.at[0])
    fetch.start()

    def put(source, h, real, imag):
        spread_ref[source, h, :rank, :NRHS] = real
        spread_ref[source, h, :rank, NRHS:] = imag
        spread_ref[source, h, rank:, :NRHS] = -imag
        spread_ref[source, h, rank:, NRHS:] = real

    left = lax.broadcasted_iota(jnp.int32, (rank, NRHS), 1) < HALF
    for (own_ref, other_ref), (k, which) in zip(halves, halved):
        swap = lax.axis_index("rhs") == 1
        for h in range(local):
            low, high = own_ref[0, h].astype(F32), other_ref[0, h].astype(F32)
            low, high = jnp.where(swap, high, low), jnp.where(swap, low, high)
            real = jnp.where(left, low, pltpu.roll(high, HALF, 1)).astype(BF16)
            imag = jnp.where(left, pltpu.roll(low, HALF, 1), high).astype(BF16)
            put(partner(k, which), h, real, imag)
    for mid_ref, (k, which) in zip(mids, full):
        for h in range(local):
            mid = mid_ref[0, h]
            put(partner(k, which), h, mid[:, :NRHS], mid[:, NRHS:])
    for h in range(local):
        for route in late:
            spread_ref[partner(*route), h] = jnp.zeros(spread_ref.shape[2:], BF16)
        top_ref[1, h] = jnp.zeros(top_ref.shape[2:], F32)
    fetch.wait()
    (group_a, _), (group_b, _) = late_groups(late, perm_ref, groups)
    for h in range(local):
        tops = ([], [])
        for q in range(groups):
            parts = [spread_ref[perm_ref[2 * q + s], h] for s in range(2)]
            top = jnp.dot(
                down_ref[q, h], jnp.concatenate(parts, axis=0), preferred_element_type=F32
            )
            is_a, is_b = group_a == q, group_b == q
            top_ref[jnp.where(is_a, 0, jnp.where(is_b, 1, 2)), h] = top
            lacks = jnp.logical_or(is_a, is_b)
            top = jnp.where(lacks, jnp.zeros_like(top), top).astype(BF16)
            for t in range(2):
                tops[t].append(top[t * rank : (t + 1) * rank])
        for t in range(2):
            rows = jnp.concatenate([row_ref[h, t, q] for q in range(groups)], axis=1)
            field_ref[h, t] = jnp.dot(rows, twisted_rows(tops[t]), preferred_element_type=F32)


def upper(full, halved, late, perm, down, row, mids):
    groups, local, _, width = down.shape
    leaf = row.shape[3]
    rank = width // 4
    vmem = pl.BlockSpec(memory_space=pltpu.VMEM)
    hbm = pl.BlockSpec(memory_space=pltpu.HBM)
    return pl.pallas_call(
        functools.partial(upper_kernel, full, halved, late),
        out_shape=[
            pltpu.VMEM((local, 2, leaf, 2 * NRHS), F32),
            pltpu.VMEM((3, local, 2 * rank, 2 * NRHS), F32),
        ],
        in_specs=[hbm] + [vmem] * (2 + len(mids)),
        out_specs=[vmem] * 2,
        scratch_shapes=[
            pltpu.VMEM((2 * groups, local, 2 * rank, 2 * NRHS), BF16),
            pltpu.SMEM(perm.shape, jnp.int32),
            pltpu.SemaphoreType.DMA((1,)),
        ],
        compiler_params=PARAMS,
        cost_estimate=COST,
        name="upper",
    )(pltpu.with_memory_space_constraint(perm, pltpu.HBM), down, row, *mids)


def finish_kernel(down_ref, row_ref, field_ref, top_ref, mid_a, mid_b, out_hbm, mix_ref, out_ref, sems):
    local, _, leaf, _ = field_ref.shape
    rank = mid_a.shape[2]
    copies = []
    for i, group in enumerate(chunks(local)):
        for h in group:
            top = jnp.concatenate([top_ref[0, h], top_ref[1, h]], axis=0) + jnp.dot(
                down_ref[h], twisted_rows([mid_a[0, h], mid_b[0, h]]), preferred_element_type=F32
            )
            top = top.astype(BF16)
            for t in range(2):
                rows = twisted_rows([top[r : r + rank] for r in (t * rank, (2 + t) * rank)])
                field = field_ref[h, t] + jnp.dot(
                    row_ref[h, t], rows, preferred_element_type=F32
                )
                mix_ref[h, t, pl.ds(0, leaf, stride=2), :] = field[:, :NRHS]
                mix_ref[h, t, pl.ds(1, leaf, stride=2), :] = field[:, NRHS:]
                out_ref[h, t] = mix_ref[h, t].astype(BF16)
        at = pl.ds(group.start, len(group))
        copies.append(pltpu.make_async_copy(out_ref.at[at], out_hbm.at[at], sems.at[i]))
        copies[-1].start()
    for copy in copies:
        copy.wait()


def finish(down, row, field, top, mids):
    local, _, leaf, _ = field.shape
    shape = (local, 2, 2 * leaf, NRHS)
    vmem = pl.BlockSpec(memory_space=pltpu.VMEM)
    return pl.pallas_call(
        finish_kernel,
        out_shape=jax.ShapeDtypeStruct(shape, BF16),
        in_specs=[vmem] * 6,
        out_specs=pl.BlockSpec(memory_space=pltpu.HBM),
        scratch_shapes=[
            pltpu.VMEM(shape, F32),
            pltpu.VMEM(shape, BF16),
            pltpu.SemaphoreType.DMA((2,)),
        ],
        compiler_params=PARAMS,
        cost_estimate=COST,
        name="finish",
    )(down, row, field, top, *mids)


def send(block, route, dests):
    code = 2 * route[0] + route[1]
    if not code:
        return block
    return lax.ppermute(block, ("blk", "sub"), [(m, m ^ code) for m in range(dests)])


def on_device(
    columns, x_panels, leaf_basis, leaf_count, parent_map, up_transfer, mid_perm, down_transfer, row_basis
):
    boxes, directions, rank, _, leaf = leaf_basis.shape
    basis = leaf_basis.reshape(boxes, directions, rank * 2, leaf)
    groups, _, local = down_transfer.shape[:3]
    down = down_transfer.reshape(groups, local, 2 * rank, 4 * rank)
    row = row_basis.reshape(local, 2, groups, leaf, 2 * rank)
    x = jnp.transpose(x_panels, (0, 2, 3, 1))
    dests = 2 * columns
    two = both_cores((2,))
    full = both_cores(range(columns - 1, 3, -1)) + [(0, 1), (1, 0), (3, 0), (0, 0)]
    late = [(3, 1), (1, 1)]
    split = 2 * x.shape[2] == NRHS
    swap = [(0, 1), (1, 0)]
    if split:
        halved = two
        xs = [x, lax.ppermute(x, "rhs", swap)]
        own_two, basis, up = own(halved, dests, leaf_count, parent_map, x, basis, up_transfer)
        own_two = lax.ppermute(own_two, "blk", [(m, m ^ 2) for m in range(columns)])
    else:
        full, halved, up = two + full, [], up_transfer
        xs = [lax.all_gather(x, "rhs", axis=2, tiled=True)]
    n = len(full)
    mids = lower(full + late, halved, dests, leaf_count, parent_map, xs, basis, up)
    halves = []
    if split:
        other_two = lax.ppermute(mids[-1], "blk", [(m, m ^ 2) for m in range(columns)])
        halves = [own_two, other_two, lax.ppermute(hand(own_two, other_two), "sub", swap)]
    mids = [send(mid, route, dests) for mid, route in zip(mids, full + late)]
    down_late, row_late = prep(late, mid_perm, down, row, (halves + mids)[0])
    field, top = upper(full, halved, late, mid_perm, down, row, [*mids[:n], *halves])
    result = finish(down_late, row_late, field, top, mids[n : n + 2])
    return result.reshape(1, local, 2, leaf, 2, NRHS)


def solution(mesh):
    return jax.shard_map(
        functools.partial(on_device, mesh.shape["blk"]),
        mesh=mesh,
        in_specs=(
            P(("grp", "blk", "sub"), None, None, "rhs"),
            P(("blk", "sub"), "rhs", None, None, None),
            P(("blk", "sub")),
            P("rhs"),
            P(("blk", "sub"), "rhs", None, None),
            P(),
            P(None, "rhs", ("blk", "sub"), None, None, None),
            P("rhs", ("blk", "sub"), None, None, None, None),
        ),
        out_specs=P(("grp", "rhs"), ("blk", "sub"), None, None, None, None),
        check_vma=False,
    )
```

```python
import functools

import jax
import jax.numpy as jnp
from jax import lax
from jax.experimental import pallas as pl
from jax.experimental.pallas import tpu as pltpu
from jax.sharding import PartitionSpec as P

NRHS = 128
HALF = 64
F32 = jnp.float32
BF16 = jnp.bfloat16
PARAMS = pltpu.CompilerParams(vmem_limit_bytes=32 * 1024 * 1024)
COST = pl.CostEstimate(flops=1_000_000, bytes_accessed=10_000, transcendentals=0)


def both_cores(steps):
    return [(k, which) for k in steps for which in (0, 1)]


def partner(k, which):
    z = jnp.bitwise_xor(lax.axis_index("blk"), k)
    core = jnp.bitwise_xor(lax.axis_index("sub"), which)
    return z * 2 + core


def up_stage(outs, routes, parent_ref, up_ref, leaf_ref, cut=lambda mid: mid):
    pairs, local = outs[0].shape[:2]
    for out, (k, which) in zip(outs, routes):
        dest = partner(k, which)
        for p in range(pairs):
            for h in range(local):
                j = dest * local + h
                mid = jnp.dot(
                    up_ref[p, j], leaf_ref[p, parent_ref[j]], preferred_element_type=F32
                )
                out[p, h] = cut(mid).astype(BF16)


def chunks(count):
    middle = (count + 1) // 2
    return [group for group in (range(middle), range(middle, count)) if group]


def leaf_stage(spreads, combine, count_ref, basis_ref, g_ref, leaf_ref, ready):
    boxes, dirs, rows, _ = basis_ref.shape
    rank = rows // 2
    width = leaf_ref.shape[3]
    first = lax.axis_index("rhs") * dirs
    even = pl.ds(0, rank, stride=2)
    odd = pl.ds(1, rank, stride=2)
    for b in range(boxes):
        ready(b)
        spread = spreads(b)
        for d in range(dirs):
            g = lax.dot_general(
                basis_ref[b, d], spread, (((1,), (1,)), ((), ())), preferred_element_type=F32
            )
            g_ref[b * dirs + d, 0] = g[:, :NRHS]
            g_ref[b * dirs + d, 1] = g[:, NRHS:]
        if b == 0:
            ready("count")
        for d in range(dirs):
            slot = b * dirs + d
            live = first + d < count_ref[b]
            pieces = combine(
                [g_ref[slot, i, even, :] for i in range(2)],
                [g_ref[slot, i, odd, :] for i in range(2)],
            )
            pieces = [jnp.where(live, x, jnp.zeros_like(x)).astype(BF16) for x in pieces]
            base = (b % 2) * 2 * rank
            top, bottom = slice(base, base + rank), slice(base + rank, base + 2 * rank)
            if width == NRHS:
                leaf_ref[b // 2, d, top, :] = pieces[0]
                leaf_ref[b // 2, d, bottom, :] = pieces[1]
            else:
                leaf_ref[b // 2, d, top, :NRHS] = pieces[0]
                leaf_ref[b // 2, d, top, NRHS:] = pieces[1]
                leaf_ref[b // 2, d, bottom, :NRHS] = -pieces[1]
                leaf_ref[b // 2, d, bottom, NRHS:] = pieces[0]


def half_columns(even, odd):
    return even[0] + odd[1], even[1] - odd[0]


def all_columns(even, odd):
    return even[0] - odd[1], even[1] + odd[0]


def own_kernel(routes, count_hbm, parent_hbm, x_hbm, basis_hbm, up_hbm, *refs):
    n = len(routes)
    outs, basis_ref, up_ref = refs[:n], refs[n], refs[n + 1]
    count_ref, parent_ref, x_ref, leaf_ref, g_ref, sems = refs[n + 2 :]
    boxes = basis_ref.shape[0]
    copies = {
        "x": pltpu.make_async_copy(x_hbm, x_ref, sems.at[0]),
        "count": pltpu.make_async_copy(count_hbm, count_ref, sems.at[1]),
        "parent": pltpu.make_async_copy(parent_hbm, parent_ref, sems.at[2]),
        "up": pltpu.make_async_copy(up_hbm, up_ref, sems.at[3]),
    }
    for b in range(boxes):
        copies[b] = pltpu.make_async_copy(basis_hbm.at[b], basis_ref.at[b], sems.at[4 + b])
    for name in ["x", 0, "count"] + list(range(1, boxes)) + ["up", "parent"]:
        copies[name].start()
    for name in ["x", "count", *range(boxes)]:
        copies[name].wait()

    def spreads(b):
        real, imag = x_ref[b, 0], x_ref[b, 1]
        return jnp.concatenate([real, imag, -imag, real], axis=0)

    leaf_stage(
        spreads, half_columns, count_ref, basis_ref, g_ref, leaf_ref, lambda name: None
    )
    copies["up"].wait()
    copies["parent"].wait()
    up_stage(outs, routes, parent_ref, up_ref, leaf_ref)


def own(routes, dests, count, parents, x, basis, up):
    boxes, dirs, rows, _ = basis.shape
    pairs, dirs_up, rank, _ = up.shape
    block = pltpu.VMEM((pairs, dirs_up // dests, rank, NRHS), BF16)
    args = [count, parents, x, basis, up]
    return pl.pallas_call(
        functools.partial(own_kernel, routes),
        out_shape=[block] * len(routes)
        + [pltpu.VMEM(basis.shape, BF16), pltpu.VMEM(up.shape, BF16)],
        in_specs=[pl.BlockSpec(memory_space=pltpu.HBM)] * 5,
        out_specs=[pl.BlockSpec(memory_space=pltpu.VMEM)] * (len(routes) + 2),
        scratch_shapes=[
            pltpu.SMEM(count.shape, jnp.int32),
            pltpu.SMEM(parents.shape, jnp.int32),
            pltpu.VMEM(x.shape, BF16),
            pltpu.VMEM((pairs, dirs, 4 * rank, NRHS), BF16),
            pltpu.VMEM((boxes * dirs, 2, rows, NRHS), F32),
            pltpu.SemaphoreType.DMA((4 + boxes,)),
        ],
        compiler_params=PARAMS,
        cost_estimate=COST,
        name="own",
    )(*[pltpu.with_memory_space_constraint(arg, pltpu.HBM) for arg in args])


def other_columns(mid):
    left = lax.broadcasted_iota(jnp.int32, (mid.shape[0], NRHS), 1) < HALF
    real, imag = mid[:, :NRHS], mid[:, NRHS:]
    low = jnp.where(left, real, pltpu.roll(imag, HALF, 1))
    high = jnp.where(left, pltpu.roll(real, HALF, 1), imag)
    return jnp.where(lax.axis_index("rhs") == 1, low, high)


def lower_kernel(full, halved, count_hbm, parent_hbm, *refs):
    n, m = len(full), len(halved)
    g_ref, leaf_ref, count_ref, parent_ref, sems = refs[-5:]
    outs = refs[-5 - n - m : -5]
    *xs, basis_ref, up_ref = refs[: -5 - n - m]
    copies = {
        "count": pltpu.make_async_copy(count_hbm, count_ref, sems.at[0]),
        "parent": pltpu.make_async_copy(parent_hbm, parent_ref, sems.at[1]),
    }
    for copy in copies.values():
        copy.start()

    def ready(name):
        if name in copies:
            copies[name].wait()

    def spreads(b):
        if len(xs) == 1:
            return jnp.concatenate([xs[0][b, 0], xs[0][b, 1]], axis=0)
        own, other = xs[0][b], xs[1][b]
        swap = lax.axis_index("rhs") == 1
        low, high = jnp.where(swap, other, own), jnp.where(swap, own, other)
        return jnp.concatenate([low[0], high[0], low[1], high[1]], axis=0)

    leaf_stage(spreads, all_columns, count_ref, basis_ref, g_ref, leaf_ref, ready)
    ready("parent")
    up_stage(outs[:n], full, parent_ref, up_ref, leaf_ref)
    if halved:
        up_stage(outs[n:], halved, parent_ref, up_ref, leaf_ref, other_columns)


def lower(full, halved, dests, count, parents, xs, basis, up):
    boxes, dirs, rows, _ = basis.shape
    pairs, dirs_up, rank, _ = up.shape
    shape = (pairs, dirs_up // dests, rank)
    hbm = pl.BlockSpec(memory_space=pltpu.HBM)
    vmem = pl.BlockSpec(memory_space=pltpu.VMEM)
    n = len(full) + len(halved)
    return pl.pallas_call(
        functools.partial(lower_kernel, full, halved),
        out_shape=[pltpu.VMEM(shape + (2 * NRHS,), BF16)] * len(full)
        + [pltpu.VMEM(shape + (NRHS,), BF16)] * len(halved),
        in_specs=[hbm, hbm] + [vmem] * (2 + len(xs)),
        out_specs=[vmem] * n,
        scratch_shapes=[
            pltpu.VMEM((boxes * dirs, 2, rows, NRHS), F32),
            pltpu.VMEM((pairs, dirs, 4 * rank, 2 * NRHS), BF16),
            pltpu.SMEM(count.shape, jnp.int32),
            pltpu.SMEM(parents.shape, jnp.int32),
            pltpu.SemaphoreType.DMA((2,)),
        ],
        compiler_params=PARAMS,
        cost_estimate=COST,
        name="lower",
    )(*[pltpu.with_memory_space_constraint(a, pltpu.HBM) for a in (count, parents)], *xs, basis, up)


def twist(top):
    return jnp.concatenate([-top[:, NRHS:], top[:, :NRHS]], axis=1)


def twisted_rows(tops):
    return jnp.concatenate([rows for top in tops for rows in (top, twist(top))], axis=0)


def late_groups(late, perm_ref, groups):
    found = []
    for route in late:
        source = partner(*route)
        group, child = 0, 0
        for i in range(2 * groups):
            hit = perm_ref[i] == source
            group = jnp.where(hit, i // 2, group)
            child = jnp.where(hit, i % 2, child)
        found.append((group, child))
    return found


def prep_kernel(late, perm_hbm, down_ref, row_ref, after_ref, down_out, row_out, perm_ref, sem):
    groups, local, rows = down_ref.shape[:3]
    width = row_ref.shape[4]
    fetch = pltpu.make_async_copy(perm_hbm, perm_ref, sem.at[0])
    fetch.start()
    fetch.wait()
    found = late_groups(late, perm_ref, groups)
    same = found[0][0] == found[1][0]
    for h in range(local):
        for i, (group, _) in enumerate(found):
            block = down_ref[group, h]
            for j, (_, child) in enumerate(found):
                part = jnp.where(child == 0, block[:, :width], block[:, width:])
                zeros = jnp.zeros_like(part)
                if i == 0 and j == 1:
                    part = jnp.where(same, part, zeros)
                elif i == 1:
                    part = zeros if j == 0 else jnp.where(same, zeros, part)
                down_out[h, i * rows : (i + 1) * rows, j * width : (j + 1) * width] = part
            for t in range(2):
                row_out[h, t, :, i * width : (i + 1) * width] = row_ref[h, t, group]


def prep(late, perm, down, row, after):
    local, rows = down.shape[1:3]
    leaf, width = row.shape[3:]
    vmem = pl.BlockSpec(memory_space=pltpu.VMEM)
    hbm = pl.BlockSpec(memory_space=pltpu.HBM)
    return pl.pallas_call(
        functools.partial(prep_kernel, late),
        out_shape=[
            pltpu.VMEM((local, 2 * rows, 2 * width), BF16),
            pltpu.VMEM((local, 2, leaf, 2 * width), BF16),
        ],
        in_specs=[hbm, vmem, vmem, pl.BlockSpec(memory_space=pl.ANY)],
        out_specs=[vmem] * 2,
        scratch_shapes=[pltpu.SMEM(perm.shape, jnp.int32), pltpu.SemaphoreType.DMA((1,))],
        compiler_params=PARAMS,
        cost_estimate=COST,
        name="prep",
    )(pltpu.with_memory_space_constraint(perm, pltpu.HBM), down, row, after)


def upper_kernel(full, halved, late, perm_hbm, down_ref, row_ref, *refs):
    n, m = len(full), len(halved)
    mids, own_mids, other_mids = refs[:n], refs[n : n + m], refs[n + m : n + 2 * m]
    field_ref, top_ref, spread_ref, perm_ref, sem = refs[n + 2 * m :]
    groups, local = down_ref.shape[:2]
    rank = spread_ref.shape[2] // 2
    fetch = pltpu.make_async_copy(perm_hbm, perm_ref, sem.at[0])
    fetch.start()

    def put(source, h, real, imag):
        spread_ref[source, h, :rank, :NRHS] = real
        spread_ref[source, h, :rank, NRHS:] = imag
        spread_ref[source, h, rank:, :NRHS] = -imag
        spread_ref[source, h, rank:, NRHS:] = real

    left = lax.broadcasted_iota(jnp.int32, (rank, NRHS), 1) < HALF
    for own_ref, other_ref, (k, which) in zip(own_mids, other_mids, halved):
        swap = lax.axis_index("rhs") == 1
        for h in range(local):
            low, high = own_ref[0, h].astype(F32), other_ref[0, h].astype(F32)
            low, high = jnp.where(swap, high, low), jnp.where(swap, low, high)
            real = jnp.where(left, low, pltpu.roll(high, HALF, 1)).astype(BF16)
            imag = jnp.where(left, pltpu.roll(low, HALF, 1), high).astype(BF16)
            put(partner(k, which), h, real, imag)
    for mid_ref, (k, which) in zip(mids, full):
        for h in range(local):
            mid = mid_ref[0, h]
            put(partner(k, which), h, mid[:, :NRHS], mid[:, NRHS:])
    for h in range(local):
        for route in late:
            spread_ref[partner(*route), h] = jnp.zeros(spread_ref.shape[2:], BF16)
        top_ref[1, h] = jnp.zeros(top_ref.shape[2:], F32)
    fetch.wait()
    (group_a, _), (group_b, _) = late_groups(late, perm_ref, groups)
    for h in range(local):
        tops = ([], [])
        for q in range(groups):
            parts = [spread_ref[perm_ref[2 * q + s], h] for s in range(2)]
            top = jnp.dot(
                down_ref[q, h], jnp.concatenate(parts, axis=0), preferred_element_type=F32
            )
            is_a, is_b = group_a == q, group_b == q
            top_ref[jnp.where(is_a, 0, jnp.where(is_b, 1, 2)), h] = top
            lacks = jnp.logical_or(is_a, is_b)
            top = jnp.where(lacks, jnp.zeros_like(top), top).astype(BF16)
            for t in range(2):
                tops[t].append(top[t * rank : (t + 1) * rank])
        for t in range(2):
            rows = jnp.concatenate([row_ref[h, t, q] for q in range(groups)], axis=1)
            field_ref[h, t] = jnp.dot(rows, twisted_rows(tops[t]), preferred_element_type=F32)


def upper(full, halved, late, perm, down, row, mids):
    groups, local, _, width = down.shape
    leaf = row.shape[3]
    rank = width // 4
    vmem = pl.BlockSpec(memory_space=pltpu.VMEM)
    hbm = pl.BlockSpec(memory_space=pltpu.HBM)
    return pl.pallas_call(
        functools.partial(upper_kernel, full, halved, late),
        out_shape=[
            pltpu.VMEM((local, 2, leaf, 2 * NRHS), F32),
            pltpu.VMEM((3, local, 2 * rank, 2 * NRHS), F32),
        ],
        in_specs=[hbm] + [vmem] * (2 + len(mids)),
        out_specs=[vmem] * 2,
        scratch_shapes=[
            pltpu.VMEM((2 * groups, local, 2 * rank, 2 * NRHS), BF16),
            pltpu.SMEM(perm.shape, jnp.int32),
            pltpu.SemaphoreType.DMA((1,)),
        ],
        compiler_params=PARAMS,
        cost_estimate=COST,
        name="upper",
    )(pltpu.with_memory_space_constraint(perm, pltpu.HBM), down, row, *mids)


def finish_kernel(down_ref, row_ref, field_ref, top_ref, mid_a, mid_b, out_hbm, mix_ref, out_ref, sems):
    local, _, leaf, _ = field_ref.shape
    rank = mid_a.shape[2]
    copies = []
    for i, group in enumerate(chunks(local)):
        for h in group:
            top = jnp.concatenate([top_ref[0, h], top_ref[1, h]], axis=0) + jnp.dot(
                down_ref[h], twisted_rows([mid_a[0, h], mid_b[0, h]]), preferred_element_type=F32
            )
            top = top.astype(BF16)
            for t in range(2):
                rows = twisted_rows([top[r : r + rank] for r in (t * rank, (2 + t) * rank)])
                field = field_ref[h, t] + jnp.dot(
                    row_ref[h, t], rows, preferred_element_type=F32
                )
                mix_ref[h, t, pl.ds(0, leaf, stride=2), :] = field[:, :NRHS]
                mix_ref[h, t, pl.ds(1, leaf, stride=2), :] = field[:, NRHS:]
                out_ref[h, t] = mix_ref[h, t].astype(BF16)
        at = pl.ds(group.start, len(group))
        copies.append(pltpu.make_async_copy(out_ref.at[at], out_hbm.at[at], sems.at[i]))
        copies[-1].start()
    for copy in copies:
        copy.wait()


def finish(down, row, field, top, mids):
    local, _, leaf, _ = field.shape
    shape = (local, 2, 2 * leaf, NRHS)
    vmem = pl.BlockSpec(memory_space=pltpu.VMEM)
    return pl.pallas_call(
        finish_kernel,
        out_shape=jax.ShapeDtypeStruct(shape, BF16),
        in_specs=[vmem] * 6,
        out_specs=pl.BlockSpec(memory_space=pltpu.HBM),
        scratch_shapes=[
            pltpu.VMEM(shape, F32),
            pltpu.VMEM(shape, BF16),
            pltpu.SemaphoreType.DMA((2,)),
        ],
        compiler_params=PARAMS,
        cost_estimate=COST,
        name="finish",
    )(down, row, field, top, *mids)


def send(block, route, dests):
    code = 2 * route[0] + route[1]
    if not code:
        return block
    return lax.ppermute(block, ("blk", "sub"), [(m, m ^ code) for m in range(dests)])


def on_device(
    columns, x_panels, leaf_basis, leaf_count, parent_map, up_transfer, mid_perm, down_transfer, row_basis
):
    boxes, directions, rank, _, leaf = leaf_basis.shape
    basis = leaf_basis.reshape(boxes, directions, rank * 2, leaf)
    groups, _, local = down_transfer.shape[:3]
    down = down_transfer.reshape(groups, local, 2 * rank, 4 * rank)
    row = row_basis.reshape(local, 2, groups, leaf, 2 * rank)
    x = jnp.transpose(x_panels, (0, 2, 3, 1))
    dests = 2 * columns
    two = both_cores((2,))
    full = both_cores(range(columns - 1, 3, -1)) + [(3, 0), (1, 0), (0, 1), (0, 0)]
    late = [(1, 1), (3, 1)]
    if 2 * x.shape[2] == NRHS:
        halved = two
        xs = [x, lax.ppermute(x, "rhs", [(0, 1), (1, 0)])]
        *own_mids, basis, up = own(halved, dests, leaf_count, parent_map, x, basis, up_transfer)
        own_mids = [send(mid, route, dests) for mid, route in zip(own_mids, halved)]
    else:
        full, halved, own_mids, up = two + full, [], [], up_transfer
        xs = [lax.all_gather(x, "rhs", axis=2, tiled=True)]
    n = len(full)
    routes = full + late + halved
    mids = lower(full + late, halved, dests, leaf_count, parent_map, xs, basis, up)
    mids = [send(mid, route, dests) for mid, route in zip(mids, routes)]
    down_late, row_late = prep(late, mid_perm, down, row, [*own_mids, mids[0]][0])
    field, top = upper(
        full, halved, late, mid_perm, down, row, [*mids[:n], *own_mids, *mids[n + 2 :]]
    )
    result = finish(down_late, row_late, field, top, mids[n : n + 2])
    return result.reshape(1, local, 2, leaf, 2, NRHS)


def solution(mesh):
    return jax.shard_map(
        functools.partial(on_device, mesh.shape["blk"]),
        mesh=mesh,
        in_specs=(
            P(("grp", "blk", "sub"), None, None, "rhs"),
            P(("blk", "sub"), "rhs", None, None, None),
            P(("blk", "sub")),
            P("rhs"),
            P(("blk", "sub"), "rhs", None, None),
            P(),
            P(None, "rhs", ("blk", "sub"), None, None, None),
            P("rhs", ("blk", "sub"), None, None, None, None),
        ),
        out_specs=P(("grp", "rhs"), ("blk", "sub"), None, None, None, None),
        check_vma=False,
    )
```

```python
import functools

import jax
import jax.numpy as jnp
from jax import lax
from jax.experimental import pallas as pl
from jax.experimental.pallas import tpu as pltpu
from jax.sharding import PartitionSpec as P

NRHS = 128
HALF = 64
F32 = jnp.float32
BF16 = jnp.bfloat16
PARAMS = pltpu.CompilerParams(vmem_limit_bytes=32 * 1024 * 1024)
COST = pl.CostEstimate(flops=1_000_000, bytes_accessed=10_000, transcendentals=0)


def both_cores(steps):
    return [(k, which) for k in steps for which in (0, 1)]


def partner(k, which):
    z = jnp.bitwise_xor(lax.axis_index("blk"), k)
    core = jnp.bitwise_xor(lax.axis_index("sub"), which)
    return z * 2 + core


def up_stage(outs, routes, parent_ref, up_ref, leaf_ref, cut=lambda mid: mid):
    pairs, local = outs[0].shape[:2]
    for out, (k, which) in zip(outs, routes):
        dest = partner(k, which)
        for p in range(pairs):
            for h in range(local):
                j = dest * local + h
                mid = jnp.dot(
                    up_ref[p, j], leaf_ref[p, parent_ref[j]], preferred_element_type=F32
                )
                out[p, h] = cut(mid).astype(BF16)


def chunks(count):
    middle = (count + 1) // 2
    return [group for group in (range(middle), range(middle, count)) if group]


def leaf_stage(spreads, combine, count_ref, basis_ref, g_ref, leaf_ref, ready):
    boxes, dirs, rows, _ = basis_ref.shape
    rank = rows // 2
    width = leaf_ref.shape[3]
    first = lax.axis_index("rhs") * dirs
    even = pl.ds(0, rank, stride=2)
    odd = pl.ds(1, rank, stride=2)
    for b in range(boxes):
        ready(b)
        spread = spreads(b)
        for d in range(dirs):
            g = lax.dot_general(
                basis_ref[b, d], spread, (((1,), (1,)), ((), ())), preferred_element_type=F32
            )
            g_ref[b * dirs + d, 0] = g[:, :NRHS]
            g_ref[b * dirs + d, 1] = g[:, NRHS:]
        if b == 0:
            ready("count")
        for d in range(dirs):
            slot = b * dirs + d
            live = first + d < count_ref[b]
            pieces = combine(
                [g_ref[slot, i, even, :] for i in range(2)],
                [g_ref[slot, i, odd, :] for i in range(2)],
            )
            pieces = [jnp.where(live, x, jnp.zeros_like(x)).astype(BF16) for x in pieces]
            base = (b % 2) * 2 * rank
            top, bottom = slice(base, base + rank), slice(base + rank, base + 2 * rank)
            if width == NRHS:
                leaf_ref[b // 2, d, top, :] = pieces[0]
                leaf_ref[b // 2, d, bottom, :] = pieces[1]
            else:
                leaf_ref[b // 2, d, top, :NRHS] = pieces[0]
                leaf_ref[b // 2, d, top, NRHS:] = pieces[1]
                leaf_ref[b // 2, d, bottom, :NRHS] = -pieces[1]
                leaf_ref[b // 2, d, bottom, NRHS:] = pieces[0]


def half_columns(even, odd):
    return even[0] + odd[1], even[1] - odd[0]


def all_columns(even, odd):
    return even[0] - odd[1], even[1] + odd[0]


def own_kernel(routes, count_hbm, parent_hbm, x_hbm, basis_hbm, up_hbm, *refs):
    n = len(routes)
    outs, basis_ref, up_ref = refs[:n], refs[n], refs[n + 1]
    count_ref, parent_ref, x_ref, leaf_ref, g_ref, sems = refs[n + 2 :]
    boxes = basis_ref.shape[0]
    copies = {
        "x": pltpu.make_async_copy(x_hbm, x_ref, sems.at[0]),
        "count": pltpu.make_async_copy(count_hbm, count_ref, sems.at[1]),
        "parent": pltpu.make_async_copy(parent_hbm, parent_ref, sems.at[2]),
        "up": pltpu.make_async_copy(up_hbm, up_ref, sems.at[3]),
    }
    for b in range(boxes):
        copies[b] = pltpu.make_async_copy(basis_hbm.at[b], basis_ref.at[b], sems.at[4 + b])
    for name in ["x", 0, "count"] + list(range(1, boxes)) + ["up", "parent"]:
        copies[name].start()
    for name in ["x", "count", *range(boxes)]:
        copies[name].wait()

    def spreads(b):
        real, imag = x_ref[b, 0], x_ref[b, 1]
        return jnp.concatenate([real, imag, -imag, real], axis=0)

    leaf_stage(
        spreads, half_columns, count_ref, basis_ref, g_ref, leaf_ref, lambda name: None
    )
    copies["up"].wait()
    copies["parent"].wait()
    up_stage(outs, routes, parent_ref, up_ref, leaf_ref)


def own(routes, dests, count, parents, x, basis, up):
    boxes, dirs, rows, _ = basis.shape
    pairs, dirs_up, rank, _ = up.shape
    block = pltpu.VMEM((pairs, dirs_up // dests, rank, NRHS), BF16)
    args = [count, parents, x, basis, up]
    return pl.pallas_call(
        functools.partial(own_kernel, routes),
        out_shape=[block] * len(routes)
        + [pltpu.VMEM(basis.shape, BF16), pltpu.VMEM(up.shape, BF16)],
        in_specs=[pl.BlockSpec(memory_space=pltpu.HBM)] * 5,
        out_specs=[pl.BlockSpec(memory_space=pltpu.VMEM)] * (len(routes) + 2),
        scratch_shapes=[
            pltpu.SMEM(count.shape, jnp.int32),
            pltpu.SMEM(parents.shape, jnp.int32),
            pltpu.VMEM(x.shape, BF16),
            pltpu.VMEM((pairs, dirs, 4 * rank, NRHS), BF16),
            pltpu.VMEM((boxes * dirs, 2, rows, NRHS), F32),
            pltpu.SemaphoreType.DMA((4 + boxes,)),
        ],
        compiler_params=PARAMS,
        cost_estimate=COST,
        name="own",
    )(*[pltpu.with_memory_space_constraint(arg, pltpu.HBM) for arg in args])


def other_columns(mid):
    left = lax.broadcasted_iota(jnp.int32, (mid.shape[0], NRHS), 1) < HALF
    real, imag = mid[:, :NRHS], mid[:, NRHS:]
    low = jnp.where(left, real, pltpu.roll(imag, HALF, 1))
    high = jnp.where(left, pltpu.roll(real, HALF, 1), imag)
    return jnp.where(lax.axis_index("rhs") == 1, low, high)


def lower_kernel(full, halved, count_hbm, parent_hbm, *refs):
    n, m = len(full), len(halved)
    g_ref, leaf_ref, count_ref, parent_ref, sems = refs[-5:]
    outs = refs[-5 - n - m : -5]
    *xs, basis_ref, up_ref = refs[: -5 - n - m]
    copies = {
        "count": pltpu.make_async_copy(count_hbm, count_ref, sems.at[0]),
        "parent": pltpu.make_async_copy(parent_hbm, parent_ref, sems.at[1]),
    }
    for copy in copies.values():
        copy.start()

    def ready(name):
        if name in copies:
            copies[name].wait()

    def spreads(b):
        if len(xs) == 1:
            return jnp.concatenate([xs[0][b, 0], xs[0][b, 1]], axis=0)
        own, other = xs[0][b], xs[1][b]
        swap = lax.axis_index("rhs") == 1
        low, high = jnp.where(swap, other, own), jnp.where(swap, own, other)
        return jnp.concatenate([low[0], high[0], low[1], high[1]], axis=0)

    leaf_stage(spreads, all_columns, count_ref, basis_ref, g_ref, leaf_ref, ready)
    ready("parent")
    up_stage(outs[:n], full, parent_ref, up_ref, leaf_ref)
    if halved:
        up_stage(outs[n:], halved, parent_ref, up_ref, leaf_ref, other_columns)


def lower(full, halved, dests, count, parents, xs, basis, up):
    boxes, dirs, rows, _ = basis.shape
    pairs, dirs_up, rank, _ = up.shape
    shape = (pairs, dirs_up // dests, rank)
    hbm = pl.BlockSpec(memory_space=pltpu.HBM)
    vmem = pl.BlockSpec(memory_space=pltpu.VMEM)
    n = len(full) + len(halved)
    return pl.pallas_call(
        functools.partial(lower_kernel, full, halved),
        out_shape=[pltpu.VMEM(shape + (2 * NRHS,), BF16)] * len(full)
        + [pltpu.VMEM(shape + (NRHS,), BF16)] * len(halved),
        in_specs=[hbm, hbm] + [vmem] * (2 + len(xs)),
        out_specs=[vmem] * n,
        scratch_shapes=[
            pltpu.VMEM((boxes * dirs, 2, rows, NRHS), F32),
            pltpu.VMEM((pairs, dirs, 4 * rank, 2 * NRHS), BF16),
            pltpu.SMEM(count.shape, jnp.int32),
            pltpu.SMEM(parents.shape, jnp.int32),
            pltpu.SemaphoreType.DMA((2,)),
        ],
        compiler_params=PARAMS,
        cost_estimate=COST,
        name="lower",
    )(*[pltpu.with_memory_space_constraint(a, pltpu.HBM) for a in (count, parents)], *xs, basis, up)


def twist(top):
    return jnp.concatenate([-top[:, NRHS:], top[:, :NRHS]], axis=1)


def twisted_rows(tops):
    return jnp.concatenate([rows for top in tops for rows in (top, twist(top))], axis=0)


def late_groups(late, perm_ref, groups):
    found = []
    for route in late:
        source = partner(*route)
        group, child = 0, 0
        for i in range(2 * groups):
            hit = perm_ref[i] == source
            group = jnp.where(hit, i // 2, group)
            child = jnp.where(hit, i % 2, child)
        found.append((group, child))
    return found


def prep_kernel(late, perm_hbm, down_ref, row_ref, after_ref, down_out, row_out, perm_ref, sem):
    groups, local, rows = down_ref.shape[:3]
    width = row_ref.shape[4]
    fetch = pltpu.make_async_copy(perm_hbm, perm_ref, sem.at[0])
    fetch.start()
    fetch.wait()
    found = late_groups(late, perm_ref, groups)
    same = found[0][0] == found[1][0]
    for h in range(local):
        for i, (group, _) in enumerate(found):
            block = down_ref[group, h]
            for j, (_, child) in enumerate(found):
                part = jnp.where(child == 0, block[:, :width], block[:, width:])
                zeros = jnp.zeros_like(part)
                if i == 0 and j == 1:
                    part = jnp.where(same, part, zeros)
                elif i == 1:
                    part = zeros if j == 0 else jnp.where(same, zeros, part)
                down_out[h, i * rows : (i + 1) * rows, j * width : (j + 1) * width] = part
            for t in range(2):
                row_out[h, t, :, i * width : (i + 1) * width] = row_ref[h, t, group]


def prep(late, perm, down, row, after):
    local, rows = down.shape[1:3]
    leaf, width = row.shape[3:]
    vmem = pl.BlockSpec(memory_space=pltpu.VMEM)
    hbm = pl.BlockSpec(memory_space=pltpu.HBM)
    return pl.pallas_call(
        functools.partial(prep_kernel, late),
        out_shape=[
            pltpu.VMEM((local, 2 * rows, 2 * width), BF16),
            pltpu.VMEM((local, 2, leaf, 2 * width), BF16),
        ],
        in_specs=[hbm, vmem, vmem, pl.BlockSpec(memory_space=pl.ANY)],
        out_specs=[vmem] * 2,
        scratch_shapes=[pltpu.SMEM(perm.shape, jnp.int32), pltpu.SemaphoreType.DMA((1,))],
        compiler_params=PARAMS,
        cost_estimate=COST,
        name="prep",
    )(pltpu.with_memory_space_constraint(perm, pltpu.HBM), down, row, after)


def upper_kernel(full, halved, late, perm_hbm, down_ref, row_ref, *refs):
    n, m = len(full), len(halved)
    mids, own_mids, other_mids = refs[:n], refs[n : n + m], refs[n + m : n + 2 * m]
    field_ref, top_ref, spread_ref, perm_ref, sem = refs[n + 2 * m :]
    groups, local = down_ref.shape[:2]
    rank = spread_ref.shape[2] // 2
    fetch = pltpu.make_async_copy(perm_hbm, perm_ref, sem.at[0])
    fetch.start()

    def put(source, h, real, imag):
        spread_ref[source, h, :rank, :NRHS] = real
        spread_ref[source, h, :rank, NRHS:] = imag
        spread_ref[source, h, rank:, :NRHS] = -imag
        spread_ref[source, h, rank:, NRHS:] = real

    left = lax.broadcasted_iota(jnp.int32, (rank, NRHS), 1) < HALF
    for own_ref, other_ref, (k, which) in zip(own_mids, other_mids, halved):
        swap = lax.axis_index("rhs") == 1
        for h in range(local):
            low, high = own_ref[0, h].astype(F32), other_ref[0, h].astype(F32)
            low, high = jnp.where(swap, high, low), jnp.where(swap, low, high)
            real = jnp.where(left, low, pltpu.roll(high, HALF, 1)).astype(BF16)
            imag = jnp.where(left, pltpu.roll(low, HALF, 1), high).astype(BF16)
            put(partner(k, which), h, real, imag)
    for mid_ref, (k, which) in zip(mids, full):
        for h in range(local):
            mid = mid_ref[0, h]
            put(partner(k, which), h, mid[:, :NRHS], mid[:, NRHS:])
    for h in range(local):
        for route in late:
            spread_ref[partner(*route), h] = jnp.zeros(spread_ref.shape[2:], BF16)
        top_ref[1, h] = jnp.zeros(top_ref.shape[2:], F32)
    fetch.wait()
    (group_a, _), (group_b, _) = late_groups(late, perm_ref, groups)
    for h in range(local):
        tops = ([], [])
        for q in range(groups):
            parts = [spread_ref[perm_ref[2 * q + s], h] for s in range(2)]
            top = jnp.dot(
                down_ref[q, h], jnp.concatenate(parts, axis=0), preferred_element_type=F32
            )
            is_a, is_b = group_a == q, group_b == q
            top_ref[jnp.where(is_a, 0, jnp.where(is_b, 1, 2)), h] = top
            lacks = jnp.logical_or(is_a, is_b)
            top = jnp.where(lacks, jnp.zeros_like(top), top).astype(BF16)
            for t in range(2):
                tops[t].append(top[t * rank : (t + 1) * rank])
        for t in range(2):
            rows = jnp.concatenate([row_ref[h, t, q] for q in range(groups)], axis=1)
            field_ref[h, t] = jnp.dot(rows, twisted_rows(tops[t]), preferred_element_type=F32)


def upper(full, halved, late, perm, down, row, mids):
    groups, local, _, width = down.shape
    leaf = row.shape[3]
    rank = width // 4
    vmem = pl.BlockSpec(memory_space=pltpu.VMEM)
    hbm = pl.BlockSpec(memory_space=pltpu.HBM)
    return pl.pallas_call(
        functools.partial(upper_kernel, full, halved, late),
        out_shape=[
            pltpu.VMEM((local, 2, leaf, 2 * NRHS), F32),
            pltpu.VMEM((3, local, 2 * rank, 2 * NRHS), F32),
        ],
        in_specs=[hbm] + [vmem] * (2 + len(mids)),
        out_specs=[vmem] * 2,
        scratch_shapes=[
            pltpu.VMEM((2 * groups, local, 2 * rank, 2 * NRHS), BF16),
            pltpu.SMEM(perm.shape, jnp.int32),
            pltpu.SemaphoreType.DMA((1,)),
        ],
        compiler_params=PARAMS,
        cost_estimate=COST,
        name="upper",
    )(pltpu.with_memory_space_constraint(perm, pltpu.HBM), down, row, *mids)


def finish_kernel(down_ref, row_ref, field_ref, top_ref, mid_a, mid_b, out_hbm, mix_ref, out_ref, sems):
    local, _, leaf, _ = field_ref.shape
    rank = mid_a.shape[2]
    copies = []
    for i, group in enumerate(chunks(local)):
        for h in group:
            top = jnp.concatenate([top_ref[0, h], top_ref[1, h]], axis=0) + jnp.dot(
                down_ref[h], twisted_rows([mid_a[0, h], mid_b[0, h]]), preferred_element_type=F32
            )
            top = top.astype(BF16)
            for t in range(2):
                rows = twisted_rows([top[r : r + rank] for r in (t * rank, (2 + t) * rank)])
                field = field_ref[h, t] + jnp.dot(
                    row_ref[h, t], rows, preferred_element_type=F32
                )
                mix_ref[h, t, pl.ds(0, leaf, stride=2), :] = field[:, :NRHS]
                mix_ref[h, t, pl.ds(1, leaf, stride=2), :] = field[:, NRHS:]
                out_ref[h, t] = mix_ref[h, t].astype(BF16)
        at = pl.ds(group.start, len(group))
        copies.append(pltpu.make_async_copy(out_ref.at[at], out_hbm.at[at], sems.at[i]))
        copies[-1].start()
    for copy in copies:
        copy.wait()


def finish(down, row, field, top, mids):
    local, _, leaf, _ = field.shape
    shape = (local, 2, 2 * leaf, NRHS)
    vmem = pl.BlockSpec(memory_space=pltpu.VMEM)
    return pl.pallas_call(
        finish_kernel,
        out_shape=jax.ShapeDtypeStruct(shape, BF16),
        in_specs=[vmem] * 6,
        out_specs=pl.BlockSpec(memory_space=pltpu.HBM),
        scratch_shapes=[
            pltpu.VMEM(shape, F32),
            pltpu.VMEM(shape, BF16),
            pltpu.SemaphoreType.DMA((2,)),
        ],
        compiler_params=PARAMS,
        cost_estimate=COST,
        name="finish",
    )(down, row, field, top, *mids)


def send(block, route, dests):
    code = 2 * route[0] + route[1]
    if not code:
        return block
    return lax.ppermute(block, ("blk", "sub"), [(m, m ^ code) for m in range(dests)])


def on_device(
    columns, x_panels, leaf_basis, leaf_count, parent_map, up_transfer, mid_perm, down_transfer, row_basis
):
    boxes, directions, rank, _, leaf = leaf_basis.shape
    basis = leaf_basis.reshape(boxes, directions, rank * 2, leaf)
    groups, _, local = down_transfer.shape[:3]
    down = down_transfer.reshape(groups, local, 2 * rank, 4 * rank)
    row = row_basis.reshape(local, 2, groups, leaf, 2 * rank)
    x = jnp.transpose(x_panels, (0, 2, 3, 1))
    dests = 2 * columns
    two = both_cores((2,))
    full = both_cores(range(columns - 1, 3, -1)) + [(3, 0), (1, 0), (0, 1), (0, 0)]
    late = [(3, 1), (1, 1)]
    if 2 * x.shape[2] == NRHS:
        halved = two
        xs = [x, lax.ppermute(x, "rhs", [(0, 1), (1, 0)])]
        *own_mids, basis, up = own(halved, dests, leaf_count, parent_map, x, basis, up_transfer)
        own_mids = [send(mid, route, dests) for mid, route in zip(own_mids, halved)]
    else:
        full, halved, own_mids, up = two + full, [], [], up_transfer
        xs = [lax.all_gather(x, "rhs", axis=2, tiled=True)]
    n = len(full)
    routes = full + late + halved
    mids = lower(full + late, halved, dests, leaf_count, parent_map, xs, basis, up)
    mids = [send(mid, route, dests) for mid, route in zip(mids, routes)]
    down_late, row_late = prep(late, mid_perm, down, row, [*own_mids, mids[0]][0])
    field, top = upper(
        full, halved, late, mid_perm, down, row, [*mids[:n], *own_mids, *mids[n + 2 :]]
    )
    result = finish(down_late, row_late, field, top, mids[n : n + 2])
    return result.reshape(1, local, 2, leaf, 2, NRHS)


def solution(mesh):
    return jax.shard_map(
        functools.partial(on_device, mesh.shape["blk"]),
        mesh=mesh,
        in_specs=(
            P(("grp", "blk", "sub"), None, None, "rhs"),
            P(("blk", "sub"), "rhs", None, None, None),
            P(("blk", "sub")),
            P("rhs"),
            P(("blk", "sub"), "rhs", None, None),
            P(),
            P(None, "rhs", ("blk", "sub"), None, None, None),
            P("rhs", ("blk", "sub"), None, None, None, None),
        ),
        out_specs=P(("grp", "rhs"), ("blk", "sub"), None, None, None, None),
        check_vma=False,
    )
```

```python
import functools

import jax
import jax.numpy as jnp
from jax import lax
from jax.experimental import pallas as pl
from jax.experimental.pallas import tpu as pltpu
from jax.sharding import PartitionSpec as P

NRHS = 128
HALF = 64
F32 = jnp.float32
BF16 = jnp.bfloat16
PARAMS = pltpu.CompilerParams(vmem_limit_bytes=32 * 1024 * 1024)
COST = pl.CostEstimate(flops=1_000_000, bytes_accessed=10_000, transcendentals=0)


def both_cores(steps):
    return [(k, which) for k in steps for which in (0, 1)]


def partner(k, which):
    z = jnp.bitwise_xor(lax.axis_index("blk"), k)
    core = jnp.bitwise_xor(lax.axis_index("sub"), which)
    return z * 2 + core


def up_stage(outs, routes, parent_ref, up_ref, leaf_ref, cut=lambda mid: mid):
    pairs, local = outs[0].shape[:2]
    for out, (k, which) in zip(outs, routes):
        dest = partner(k, which)
        for p in range(pairs):
            for h in range(local):
                j = dest * local + h
                mid = jnp.dot(
                    up_ref[p, j], leaf_ref[p, parent_ref[j]], preferred_element_type=F32
                )
                out[p, h] = cut(mid).astype(BF16)


def chunks(count):
    middle = (count + 1) // 2
    return [group for group in (range(middle), range(middle, count)) if group]


def leaf_stage(spreads, combine, count_ref, basis_ref, g_ref, leaf_ref, ready):
    boxes, dirs, rows, _ = basis_ref.shape
    rank = rows // 2
    width = leaf_ref.shape[3]
    first = lax.axis_index("rhs") * dirs
    even = pl.ds(0, rank, stride=2)
    odd = pl.ds(1, rank, stride=2)
    for b in range(boxes):
        ready(b)
        spread = spreads(b)
        for d in range(dirs):
            g = lax.dot_general(
                basis_ref[b, d], spread, (((1,), (1,)), ((), ())), preferred_element_type=F32
            )
            g_ref[b * dirs + d, 0] = g[:, :NRHS]
            g_ref[b * dirs + d, 1] = g[:, NRHS:]
        if b == 0:
            ready("count")
        for d in range(dirs):
            slot = b * dirs + d
            live = first + d < count_ref[b]
            pieces = combine(
                [g_ref[slot, i, even, :] for i in range(2)],
                [g_ref[slot, i, odd, :] for i in range(2)],
            )
            pieces = [jnp.where(live, x, jnp.zeros_like(x)).astype(BF16) for x in pieces]
            base = (b % 2) * 2 * rank
            top, bottom = slice(base, base + rank), slice(base + rank, base + 2 * rank)
            if width == NRHS:
                leaf_ref[b // 2, d, top, :] = pieces[0]
                leaf_ref[b // 2, d, bottom, :] = pieces[1]
            else:
                leaf_ref[b // 2, d, top, :NRHS] = pieces[0]
                leaf_ref[b // 2, d, top, NRHS:] = pieces[1]
                leaf_ref[b // 2, d, bottom, :NRHS] = -pieces[1]
                leaf_ref[b // 2, d, bottom, NRHS:] = pieces[0]


def half_columns(even, odd):
    return even[0] + odd[1], even[1] - odd[0]


def all_columns(even, odd):
    return even[0] - odd[1], even[1] + odd[0]


def own_kernel(routes, count_hbm, parent_hbm, x_hbm, basis_hbm, up_hbm, *refs):
    n = len(routes)
    outs, basis_ref, up_ref = refs[:n], refs[n], refs[n + 1]
    count_ref, parent_ref, x_ref, leaf_ref, g_ref, sems = refs[n + 2 :]
    boxes = basis_ref.shape[0]
    copies = {
        "x": pltpu.make_async_copy(x_hbm, x_ref, sems.at[0]),
        "count": pltpu.make_async_copy(count_hbm, count_ref, sems.at[1]),
        "parent": pltpu.make_async_copy(parent_hbm, parent_ref, sems.at[2]),
        "up": pltpu.make_async_copy(up_hbm, up_ref, sems.at[3]),
    }
    for b in range(boxes):
        copies[b] = pltpu.make_async_copy(basis_hbm.at[b], basis_ref.at[b], sems.at[4 + b])
    for name in ["x", "count", "parent", *range(boxes), "up"]:
        copies[name].start()
    for name in ["x", "count", "parent", *range(boxes)]:
        copies[name].wait()
    spreads = []
    for b in range(boxes):
        real, imag = x_ref[b, 0], x_ref[b, 1]
        spreads.append(jnp.concatenate([real, imag, -imag, real], axis=0))
    pairs, local, rank = outs[0].shape[:3]
    first = lax.axis_index("rhs") * basis_ref.shape[1]
    even = pl.ds(0, rank, stride=2)
    odd = pl.ds(1, rank, stride=2)
    jobs = [
        (out, p, h, partner(k, which) * local + h)
        for out, (k, which) in zip(outs, routes)
        for p in range(pairs)
        for h in range(local)
    ]
    for i, (_, p, _, j) in enumerate(jobs):
        d = parent_ref[j]
        for child in range(2):
            b, slot = 2 * p + child, 2 * i + child
            g = lax.dot_general(
                basis_ref[b, d], spreads[b], (((1,), (1,)), ((), ())), preferred_element_type=F32
            )
            g_ref[slot, 0] = g[:, :NRHS]
            g_ref[slot, 1] = g[:, NRHS:]
            live = first + d < count_ref[b]
            pieces = half_columns(
                [g_ref[slot, c, even, :] for c in range(2)],
                [g_ref[slot, c, odd, :] for c in range(2)],
            )
            for c, piece in enumerate(pieces):
                piece = jnp.where(live, piece, jnp.zeros_like(piece)).astype(BF16)
                base = (2 * child + c) * rank
                leaf_ref[i, base : base + rank, :] = piece
    copies["up"].wait()
    for i, (out, p, h, j) in enumerate(jobs):
        mid = jnp.dot(up_ref[p, j], leaf_ref[i], preferred_element_type=F32)
        out[p, h] = mid.astype(BF16)


def own(routes, dests, count, parents, x, basis, up):
    boxes, dirs, rows, _ = basis.shape
    pairs, dirs_up, rank, _ = up.shape
    block = pltpu.VMEM((pairs, dirs_up // dests, rank, NRHS), BF16)
    args = [count, parents, x, basis, up]
    jobs = len(routes) * pairs * (dirs_up // dests)
    return pl.pallas_call(
        functools.partial(own_kernel, routes),
        out_shape=[block] * len(routes)
        + [pltpu.VMEM(basis.shape, BF16), pltpu.VMEM(up.shape, BF16)],
        in_specs=[pl.BlockSpec(memory_space=pltpu.HBM)] * 5,
        out_specs=[pl.BlockSpec(memory_space=pltpu.VMEM)] * (len(routes) + 2),
        scratch_shapes=[
            pltpu.SMEM(count.shape, jnp.int32),
            pltpu.SMEM(parents.shape, jnp.int32),
            pltpu.VMEM(x.shape, BF16),
            pltpu.VMEM((jobs, 4 * rank, NRHS), BF16),
            pltpu.VMEM((2 * jobs, 2, rows, NRHS), F32),
            pltpu.SemaphoreType.DMA((4 + boxes,)),
        ],
        compiler_params=PARAMS,
        cost_estimate=COST,
        name="own",
    )(*[pltpu.with_memory_space_constraint(arg, pltpu.HBM) for arg in args])


def other_columns(mid):
    left = lax.broadcasted_iota(jnp.int32, (mid.shape[0], NRHS), 1) < HALF
    real, imag = mid[:, :NRHS], mid[:, NRHS:]
    low = jnp.where(left, real, pltpu.roll(imag, HALF, 1))
    high = jnp.where(left, pltpu.roll(real, HALF, 1), imag)
    return jnp.where(lax.axis_index("rhs") == 1, low, high)


def lower_kernel(full, halved, count_hbm, parent_hbm, *refs):
    n, m = len(full), len(halved)
    g_ref, leaf_ref, count_ref, parent_ref, sems = refs[-5:]
    outs = refs[-5 - n - m : -5]
    *xs, basis_ref, up_ref = refs[: -5 - n - m]
    copies = {
        "count": pltpu.make_async_copy(count_hbm, count_ref, sems.at[0]),
        "parent": pltpu.make_async_copy(parent_hbm, parent_ref, sems.at[1]),
    }
    for copy in copies.values():
        copy.start()

    def ready(name):
        if name in copies:
            copies[name].wait()

    def spreads(b):
        if len(xs) == 1:
            return jnp.concatenate([xs[0][b, 0], xs[0][b, 1]], axis=0)
        own, other = xs[0][b], xs[1][b]
        swap = lax.axis_index("rhs") == 1
        low, high = jnp.where(swap, other, own), jnp.where(swap, own, other)
        return jnp.concatenate([low[0], high[0], low[1], high[1]], axis=0)

    leaf_stage(spreads, all_columns, count_ref, basis_ref, g_ref, leaf_ref, ready)
    ready("parent")
    up_stage(outs[:n], full, parent_ref, up_ref, leaf_ref)
    if halved:
        up_stage(outs[n:], halved, parent_ref, up_ref, leaf_ref, other_columns)


def lower(full, halved, dests, count, parents, xs, basis, up):
    boxes, dirs, rows, _ = basis.shape
    pairs, dirs_up, rank, _ = up.shape
    shape = (pairs, dirs_up // dests, rank)
    hbm = pl.BlockSpec(memory_space=pltpu.HBM)
    vmem = pl.BlockSpec(memory_space=pltpu.VMEM)
    n = len(full) + len(halved)
    return pl.pallas_call(
        functools.partial(lower_kernel, full, halved),
        out_shape=[pltpu.VMEM(shape + (2 * NRHS,), BF16)] * len(full)
        + [pltpu.VMEM(shape + (NRHS,), BF16)] * len(halved),
        in_specs=[hbm, hbm] + [vmem] * (2 + len(xs)),
        out_specs=[vmem] * n,
        scratch_shapes=[
            pltpu.VMEM((boxes * dirs, 2, rows, NRHS), F32),
            pltpu.VMEM((pairs, dirs, 4 * rank, 2 * NRHS), BF16),
            pltpu.SMEM(count.shape, jnp.int32),
            pltpu.SMEM(parents.shape, jnp.int32),
            pltpu.SemaphoreType.DMA((2,)),
        ],
        compiler_params=PARAMS,
        cost_estimate=COST,
        name="lower",
    )(*[pltpu.with_memory_space_constraint(a, pltpu.HBM) for a in (count, parents)], *xs, basis, up)


def twist(top):
    return jnp.concatenate([-top[:, NRHS:], top[:, :NRHS]], axis=1)


def twisted_rows(tops):
    return jnp.concatenate([rows for top in tops for rows in (top, twist(top))], axis=0)


def late_groups(late, perm_ref, groups):
    found = []
    for route in late:
        source = partner(*route)
        group, child = 0, 0
        for i in range(2 * groups):
            hit = perm_ref[i] == source
            group = jnp.where(hit, i // 2, group)
            child = jnp.where(hit, i % 2, child)
        found.append((group, child))
    return found


def prep_kernel(late, perm_hbm, down_ref, row_ref, after_ref, down_out, row_out, perm_ref, sem):
    groups, local, rows = down_ref.shape[:3]
    width = row_ref.shape[4]
    fetch = pltpu.make_async_copy(perm_hbm, perm_ref, sem.at[0])
    fetch.start()
    fetch.wait()
    found = late_groups(late, perm_ref, groups)
    same = found[0][0] == found[1][0]
    for h in range(local):
        for i, (group, _) in enumerate(found):
            block = down_ref[group, h]
            for j, (_, child) in enumerate(found):
                part = jnp.where(child == 0, block[:, :width], block[:, width:])
                zeros = jnp.zeros_like(part)
                if i == 0 and j == 1:
                    part = jnp.where(same, part, zeros)
                elif i == 1:
                    part = zeros if j == 0 else jnp.where(same, zeros, part)
                down_out[h, i * rows : (i + 1) * rows, j * width : (j + 1) * width] = part
            for t in range(2):
                row_out[h, t, :, i * width : (i + 1) * width] = row_ref[h, t, group]


def prep(late, perm, down, row, after):
    local, rows = down.shape[1:3]
    leaf, width = row.shape[3:]
    vmem = pl.BlockSpec(memory_space=pltpu.VMEM)
    hbm = pl.BlockSpec(memory_space=pltpu.HBM)
    return pl.pallas_call(
        functools.partial(prep_kernel, late),
        out_shape=[
            pltpu.VMEM((local, 2 * rows, 2 * width), BF16),
            pltpu.VMEM((local, 2, leaf, 2 * width), BF16),
        ],
        in_specs=[hbm, vmem, vmem, pl.BlockSpec(memory_space=pl.ANY)],
        out_specs=[vmem] * 2,
        scratch_shapes=[pltpu.SMEM(perm.shape, jnp.int32), pltpu.SemaphoreType.DMA((1,))],
        compiler_params=PARAMS,
        cost_estimate=COST,
        name="prep",
    )(pltpu.with_memory_space_constraint(perm, pltpu.HBM), down, row, after)


def upper_kernel(full, halved, late, perm_hbm, down_ref, row_ref, *refs):
    n, m = len(full), len(halved)
    mids, own_mids, other_mids = refs[:n], refs[n : n + m], refs[n + m : n + 2 * m]
    field_ref, top_ref, spread_ref, perm_ref, sem = refs[n + 2 * m :]
    groups, local = down_ref.shape[:2]
    rank = spread_ref.shape[2] // 2
    fetch = pltpu.make_async_copy(perm_hbm, perm_ref, sem.at[0])
    fetch.start()

    def put(source, h, real, imag):
        spread_ref[source, h, :rank, :NRHS] = real
        spread_ref[source, h, :rank, NRHS:] = imag
        spread_ref[source, h, rank:, :NRHS] = -imag
        spread_ref[source, h, rank:, NRHS:] = real

    left = lax.broadcasted_iota(jnp.int32, (rank, NRHS), 1) < HALF
    for own_ref, other_ref, (k, which) in zip(own_mids, other_mids, halved):
        swap = lax.axis_index("rhs") == 1
        for h in range(local):
            low, high = own_ref[0, h].astype(F32), other_ref[0, h].astype(F32)
            low, high = jnp.where(swap, high, low), jnp.where(swap, low, high)
            real = jnp.where(left, low, pltpu.roll(high, HALF, 1)).astype(BF16)
            imag = jnp.where(left, pltpu.roll(low, HALF, 1), high).astype(BF16)
            put(partner(k, which), h, real, imag)
    for mid_ref, (k, which) in zip(mids, full):
        for h in range(local):
            mid = mid_ref[0, h]
            put(partner(k, which), h, mid[:, :NRHS], mid[:, NRHS:])
    for h in range(local):
        for route in late:
            spread_ref[partner(*route), h] = jnp.zeros(spread_ref.shape[2:], BF16)
        top_ref[1, h] = jnp.zeros(top_ref.shape[2:], F32)
    fetch.wait()
    (group_a, _), (group_b, _) = late_groups(late, perm_ref, groups)
    for h in range(local):
        tops = ([], [])
        for q in range(groups):
            parts = [spread_ref[perm_ref[2 * q + s], h] for s in range(2)]
            top = jnp.dot(
                down_ref[q, h], jnp.concatenate(parts, axis=0), preferred_element_type=F32
            )
            is_a, is_b = group_a == q, group_b == q
            top_ref[jnp.where(is_a, 0, jnp.where(is_b, 1, 2)), h] = top
            lacks = jnp.logical_or(is_a, is_b)
            top = jnp.where(lacks, jnp.zeros_like(top), top).astype(BF16)
            for t in range(2):
                tops[t].append(top[t * rank : (t + 1) * rank])
        for t in range(2):
            rows = jnp.concatenate([row_ref[h, t, q] for q in range(groups)], axis=1)
            field_ref[h, t] = jnp.dot(rows, twisted_rows(tops[t]), preferred_element_type=F32)


def upper(full, halved, late, perm, down, row, mids):
    groups, local, _, width = down.shape
    leaf = row.shape[3]
    rank = width // 4
    vmem = pl.BlockSpec(memory_space=pltpu.VMEM)
    hbm = pl.BlockSpec(memory_space=pltpu.HBM)
    return pl.pallas_call(
        functools.partial(upper_kernel, full, halved, late),
        out_shape=[
            pltpu.VMEM((local, 2, leaf, 2 * NRHS), F32),
            pltpu.VMEM((3, local, 2 * rank, 2 * NRHS), F32),
        ],
        in_specs=[hbm] + [vmem] * (2 + len(mids)),
        out_specs=[vmem] * 2,
        scratch_shapes=[
            pltpu.VMEM((2 * groups, local, 2 * rank, 2 * NRHS), BF16),
            pltpu.SMEM(perm.shape, jnp.int32),
            pltpu.SemaphoreType.DMA((1,)),
        ],
        compiler_params=PARAMS,
        cost_estimate=COST,
        name="upper",
    )(pltpu.with_memory_space_constraint(perm, pltpu.HBM), down, row, *mids)


def finish_kernel(down_ref, row_ref, field_ref, top_ref, mid_a, mid_b, out_hbm, mix_ref, out_ref, sems):
    local, _, leaf, _ = field_ref.shape
    rank = mid_a.shape[2]
    copies = []
    for i, group in enumerate(chunks(local)):
        for h in group:
            top = jnp.concatenate([top_ref[0, h], top_ref[1, h]], axis=0) + jnp.dot(
                down_ref[h], twisted_rows([mid_a[0, h], mid_b[0, h]]), preferred_element_type=F32
            )
            top = top.astype(BF16)
            for t in range(2):
                rows = twisted_rows([top[r : r + rank] for r in (t * rank, (2 + t) * rank)])
                field = field_ref[h, t] + jnp.dot(
                    row_ref[h, t], rows, preferred_element_type=F32
                )
                mix_ref[h, t, pl.ds(0, leaf, stride=2), :] = field[:, :NRHS]
                mix_ref[h, t, pl.ds(1, leaf, stride=2), :] = field[:, NRHS:]
                out_ref[h, t] = mix_ref[h, t].astype(BF16)
        at = pl.ds(group.start, len(group))
        copies.append(pltpu.make_async_copy(out_ref.at[at], out_hbm.at[at], sems.at[i]))
        copies[-1].start()
    for copy in copies:
        copy.wait()


def finish(down, row, field, top, mids):
    local, _, leaf, _ = field.shape
    shape = (local, 2, 2 * leaf, NRHS)
    vmem = pl.BlockSpec(memory_space=pltpu.VMEM)
    return pl.pallas_call(
        finish_kernel,
        out_shape=jax.ShapeDtypeStruct(shape, BF16),
        in_specs=[vmem] * 6,
        out_specs=pl.BlockSpec(memory_space=pltpu.HBM),
        scratch_shapes=[
            pltpu.VMEM(shape, F32),
            pltpu.VMEM(shape, BF16),
            pltpu.SemaphoreType.DMA((2,)),
        ],
        compiler_params=PARAMS,
        cost_estimate=COST,
        name="finish",
    )(down, row, field, top, *mids)


def send(block, route, dests):
    code = 2 * route[0] + route[1]
    if not code:
        return block
    return lax.ppermute(block, ("blk", "sub"), [(m, m ^ code) for m in range(dests)])


def on_device(
    columns, x_panels, leaf_basis, leaf_count, parent_map, up_transfer, mid_perm, down_transfer, row_basis
):
    boxes, directions, rank, _, leaf = leaf_basis.shape
    basis = leaf_basis.reshape(boxes, directions, rank * 2, leaf)
    groups, _, local = down_transfer.shape[:3]
    down = down_transfer.reshape(groups, local, 2 * rank, 4 * rank)
    row = row_basis.reshape(local, 2, groups, leaf, 2 * rank)
    x = jnp.transpose(x_panels, (0, 2, 3, 1))
    dests = 2 * columns
    two = both_cores((2,))
    full = both_cores(range(columns - 1, 3, -1)) + [(3, 0), (1, 0), (0, 1), (0, 0)]
    late = [(1, 1), (3, 1)]
    if 2 * x.shape[2] == NRHS:
        halved = two
        xs = [x, lax.ppermute(x, "rhs", [(0, 1), (1, 0)])]
        *own_mids, basis, up = own(halved, dests, leaf_count, parent_map, x, basis, up_transfer)
        own_mids = [send(mid, route, dests) for mid, route in zip(own_mids, halved)]
    else:
        full, halved, own_mids, up = two + full, [], [], up_transfer
        xs = [lax.all_gather(x, "rhs", axis=2, tiled=True)]
    n = len(full)
    routes = full + late + halved
    mids = lower(full + late, halved, dests, leaf_count, parent_map, xs, basis, up)
    mids = [send(mid, route, dests) for mid, route in zip(mids, routes)]
    down_late, row_late = prep(late, mid_perm, down, row, [*own_mids, mids[0]][0])
    field, top = upper(
        full, halved, late, mid_perm, down, row, [*mids[:n], *own_mids, *mids[n + 2 :]]
    )
    result = finish(down_late, row_late, field, top, mids[n : n + 2])
    return result.reshape(1, local, 2, leaf, 2, NRHS)


def solution(mesh):
    return jax.shard_map(
        functools.partial(on_device, mesh.shape["blk"]),
        mesh=mesh,
        in_specs=(
            P(("grp", "blk", "sub"), None, None, "rhs"),
            P(("blk", "sub"), "rhs", None, None, None),
            P(("blk", "sub")),
            P("rhs"),
            P(("blk", "sub"), "rhs", None, None),
            P(),
            P(None, "rhs", ("blk", "sub"), None, None, None),
            P("rhs", ("blk", "sub"), None, None, None, None),
        ),
        out_specs=P(("grp", "rhs"), ("blk", "sub"), None, None, None, None),
        check_vma=False,
    )
```

```python
import functools

import jax
import jax.numpy as jnp
from jax import lax
from jax.experimental import pallas as pl
from jax.experimental.pallas import tpu as pltpu
from jax.sharding import PartitionSpec as P

NRHS = 128
HALF = 64
F32 = jnp.float32
BF16 = jnp.bfloat16
PARAMS = pltpu.CompilerParams(vmem_limit_bytes=32 * 1024 * 1024)
COST = pl.CostEstimate(flops=1_000_000, bytes_accessed=10_000, transcendentals=0)


def both_cores(steps):
    return [(k, which) for k in steps for which in (0, 1)]


def partner(k, which):
    z = jnp.bitwise_xor(lax.axis_index("blk"), k)
    core = jnp.bitwise_xor(lax.axis_index("sub"), which)
    return z * 2 + core


def up_stage(outs, routes, parent_ref, up_ref, leaf_ref, cut=lambda mid: mid):
    pairs, local = outs[0].shape[:2]
    for out, (k, which) in zip(outs, routes):
        dest = partner(k, which)
        for p in range(pairs):
            for h in range(local):
                j = dest * local + h
                mid = jnp.dot(
                    up_ref[p, j], leaf_ref[p, parent_ref[j]], preferred_element_type=F32
                )
                out[p, h] = cut(mid).astype(BF16)


def chunks(count):
    middle = (count + 1) // 2
    return [group for group in (range(middle), range(middle, count)) if group]


def leaf_stage(spreads, combine, count_ref, basis_ref, g_ref, leaf_ref, ready):
    boxes, dirs, rows, _ = basis_ref.shape
    rank = rows // 2
    width = leaf_ref.shape[3]
    first = lax.axis_index("rhs") * dirs
    even = pl.ds(0, rank, stride=2)
    odd = pl.ds(1, rank, stride=2)
    for b in range(boxes):
        ready(b)
        spread = spreads(b)
        for d in range(dirs):
            g = lax.dot_general(
                basis_ref[b, d], spread, (((1,), (1,)), ((), ())), preferred_element_type=F32
            )
            g_ref[b * dirs + d, 0] = g[:, :NRHS]
            g_ref[b * dirs + d, 1] = g[:, NRHS:]
        if b == 0:
            ready("count")
        for d in range(dirs):
            slot = b * dirs + d
            live = first + d < count_ref[b]
            pieces = combine(
                [g_ref[slot, i, even, :] for i in range(2)],
                [g_ref[slot, i, odd, :] for i in range(2)],
            )
            pieces = [jnp.where(live, x, jnp.zeros_like(x)).astype(BF16) for x in pieces]
            base = (b % 2) * 2 * rank
            top, bottom = slice(base, base + rank), slice(base + rank, base + 2 * rank)
            if width == NRHS:
                leaf_ref[b // 2, d, top, :] = pieces[0]
                leaf_ref[b // 2, d, bottom, :] = pieces[1]
            else:
                leaf_ref[b // 2, d, top, :NRHS] = pieces[0]
                leaf_ref[b // 2, d, top, NRHS:] = pieces[1]
                leaf_ref[b // 2, d, bottom, :NRHS] = -pieces[1]
                leaf_ref[b // 2, d, bottom, NRHS:] = pieces[0]


def half_columns(even, odd):
    return even[0] + odd[1], even[1] - odd[0]


def all_columns(even, odd):
    return even[0] - odd[1], even[1] + odd[0]


def own_kernel(routes, count_hbm, parent_hbm, x_hbm, basis_hbm, up_hbm, *refs):
    n = len(routes)
    outs, basis_ref, up_ref = refs[:n], refs[n], refs[n + 1]
    count_ref, parent_ref, x_ref, leaf_ref, g_ref, sems = refs[n + 2 :]
    boxes = basis_ref.shape[0]
    copies = {
        "x": pltpu.make_async_copy(x_hbm, x_ref, sems.at[0]),
        "count": pltpu.make_async_copy(count_hbm, count_ref, sems.at[1]),
        "parent": pltpu.make_async_copy(parent_hbm, parent_ref, sems.at[2]),
        "up": pltpu.make_async_copy(up_hbm, up_ref, sems.at[3]),
    }
    for b in range(boxes):
        copies[b] = pltpu.make_async_copy(basis_hbm.at[b], basis_ref.at[b], sems.at[4 + b])
    for name in ["x", "count", "parent", *range(boxes), "up"]:
        copies[name].start()
    for name in ["x", "count", "parent", *range(boxes)]:
        copies[name].wait()
    spreads = []
    for b in range(boxes):
        real, imag = x_ref[b, 0], x_ref[b, 1]
        spreads.append(jnp.concatenate([real, imag, -imag, real], axis=0))
    pairs, local, rank = outs[0].shape[:3]
    first = lax.axis_index("rhs") * basis_ref.shape[1]
    even = pl.ds(0, rank, stride=2)
    odd = pl.ds(1, rank, stride=2)
    jobs = [
        (out, p, h, partner(k, which) * local + h)
        for out, (k, which) in zip(outs, routes)
        for p in range(pairs)
        for h in range(local)
    ]
    for i, (_, p, _, j) in enumerate(jobs):
        d = parent_ref[j]
        for child in range(2):
            b, slot = 2 * p + child, 2 * i + child
            g = lax.dot_general(
                basis_ref[b, d], spreads[b], (((1,), (1,)), ((), ())), preferred_element_type=F32
            )
            g_ref[slot, 0] = g[:, :NRHS]
            g_ref[slot, 1] = g[:, NRHS:]
            live = first + d < count_ref[b]
            pieces = half_columns(
                [g_ref[slot, c, even, :] for c in range(2)],
                [g_ref[slot, c, odd, :] for c in range(2)],
            )
            for c, piece in enumerate(pieces):
                piece = jnp.where(live, piece, jnp.zeros_like(piece)).astype(BF16)
                base = (2 * child + c) * rank
                leaf_ref[i, base : base + rank, :] = piece
    copies["up"].wait()
    for i, (out, p, h, j) in enumerate(jobs):
        mid = jnp.dot(up_ref[p, j], leaf_ref[i], preferred_element_type=F32)
        out[p, h] = mid.astype(BF16)


def own(routes, dests, count, parents, x, basis, up):
    boxes, dirs, rows, _ = basis.shape
    pairs, dirs_up, rank, _ = up.shape
    block = pltpu.VMEM((pairs, dirs_up // dests, rank, NRHS), BF16)
    args = [count, parents, x, basis, up]
    jobs = len(routes) * pairs * (dirs_up // dests)
    return pl.pallas_call(
        functools.partial(own_kernel, routes),
        out_shape=[block] * len(routes)
        + [pltpu.VMEM(basis.shape, BF16), pltpu.VMEM(up.shape, BF16)],
        in_specs=[pl.BlockSpec(memory_space=pltpu.HBM)] * 5,
        out_specs=[pl.BlockSpec(memory_space=pltpu.VMEM)] * (len(routes) + 2),
        scratch_shapes=[
            pltpu.SMEM(count.shape, jnp.int32),
            pltpu.SMEM(parents.shape, jnp.int32),
            pltpu.VMEM(x.shape, BF16),
            pltpu.VMEM((jobs, 4 * rank, NRHS), BF16),
            pltpu.VMEM((2 * jobs, 2, rows, NRHS), F32),
            pltpu.SemaphoreType.DMA((4 + boxes,)),
        ],
        compiler_params=PARAMS,
        cost_estimate=COST,
        name="own",
    )(*[pltpu.with_memory_space_constraint(arg, pltpu.HBM) for arg in args])


def other_columns(mid):
    left = lax.broadcasted_iota(jnp.int32, (mid.shape[0], NRHS), 1) < HALF
    real, imag = mid[:, :NRHS], mid[:, NRHS:]
    low = jnp.where(left, real, pltpu.roll(imag, HALF, 1))
    high = jnp.where(left, pltpu.roll(real, HALF, 1), imag)
    return jnp.where(lax.axis_index("rhs") == 1, low, high)


def lower_kernel(full, halved, count_hbm, parent_hbm, *refs):
    n, m = len(full), len(halved)
    g_ref, leaf_ref, count_ref, parent_ref, sems = refs[-5:]
    outs = refs[-5 - n - m : -5]
    *xs, basis_ref, up_ref = refs[: -5 - n - m]
    copies = {
        "count": pltpu.make_async_copy(count_hbm, count_ref, sems.at[0]),
        "parent": pltpu.make_async_copy(parent_hbm, parent_ref, sems.at[1]),
    }
    for copy in copies.values():
        copy.start()

    def ready(name):
        if name in copies:
            copies[name].wait()

    def spreads(b):
        if len(xs) == 1:
            return jnp.concatenate([xs[0][b, 0], xs[0][b, 1]], axis=0)
        own, other = xs[0][b], xs[1][b]
        swap = lax.axis_index("rhs") == 1
        low, high = jnp.where(swap, other, own), jnp.where(swap, own, other)
        return jnp.concatenate([low[0], high[0], low[1], high[1]], axis=0)

    leaf_stage(spreads, all_columns, count_ref, basis_ref, g_ref, leaf_ref, ready)
    ready("parent")
    up_stage(outs[:n], full, parent_ref, up_ref, leaf_ref)
    if halved:
        up_stage(outs[n:], halved, parent_ref, up_ref, leaf_ref, other_columns)


def lower(full, halved, dests, count, parents, xs, basis, up):
    boxes, dirs, rows, _ = basis.shape
    pairs, dirs_up, rank, _ = up.shape
    shape = (pairs, dirs_up // dests, rank)
    hbm = pl.BlockSpec(memory_space=pltpu.HBM)
    vmem = pl.BlockSpec(memory_space=pltpu.VMEM)
    n = len(full) + len(halved)
    return pl.pallas_call(
        functools.partial(lower_kernel, full, halved),
        out_shape=[pltpu.VMEM(shape + (2 * NRHS,), BF16)] * len(full)
        + [pltpu.VMEM(shape + (NRHS,), BF16)] * len(halved),
        in_specs=[hbm, hbm] + [vmem] * (2 + len(xs)),
        out_specs=[vmem] * n,
        scratch_shapes=[
            pltpu.VMEM((boxes * dirs, 2, rows, NRHS), F32),
            pltpu.VMEM((pairs, dirs, 4 * rank, 2 * NRHS), BF16),
            pltpu.SMEM(count.shape, jnp.int32),
            pltpu.SMEM(parents.shape, jnp.int32),
            pltpu.SemaphoreType.DMA((2,)),
        ],
        compiler_params=PARAMS,
        cost_estimate=COST,
        name="lower",
    )(*[pltpu.with_memory_space_constraint(a, pltpu.HBM) for a in (count, parents)], *xs, basis, up)


def twist(top):
    return jnp.concatenate([-top[:, NRHS:], top[:, :NRHS]], axis=1)


def twisted_rows(tops):
    return jnp.concatenate([rows for top in tops for rows in (top, twist(top))], axis=0)


def late_groups(late, perm_ref, groups):
    found = []
    for route in late:
        source = partner(*route)
        group, child = 0, 0
        for i in range(2 * groups):
            hit = perm_ref[i] == source
            group = jnp.where(hit, i // 2, group)
            child = jnp.where(hit, i % 2, child)
        found.append((group, child))
    return found


def prep_kernel(late, perm_hbm, down_ref, row_ref, after_ref, down_out, row_out, perm_ref, sem):
    groups, local, rows = down_ref.shape[:3]
    width = row_ref.shape[4]
    fetch = pltpu.make_async_copy(perm_hbm, perm_ref, sem.at[0])
    fetch.start()
    fetch.wait()
    found = late_groups(late, perm_ref, groups)
    same = found[0][0] == found[1][0]
    for h in range(local):
        for i, (group, _) in enumerate(found):
            block = down_ref[group, h]
            for j, (_, child) in enumerate(found):
                part = jnp.where(child == 0, block[:, :width], block[:, width:])
                zeros = jnp.zeros_like(part)
                if i == 0 and j == 1:
                    part = jnp.where(same, part, zeros)
                elif i == 1:
                    part = zeros if j == 0 else jnp.where(same, zeros, part)
                down_out[h, i * rows : (i + 1) * rows, j * width : (j + 1) * width] = part
            for t in range(2):
                row_out[h, t, :, i * width : (i + 1) * width] = row_ref[h, t, group]


def prep(late, perm, down, row, after):
    local, rows = down.shape[1:3]
    leaf, width = row.shape[3:]
    vmem = pl.BlockSpec(memory_space=pltpu.VMEM)
    hbm = pl.BlockSpec(memory_space=pltpu.HBM)
    return pl.pallas_call(
        functools.partial(prep_kernel, late),
        out_shape=[
            pltpu.VMEM((local, 2 * rows, 2 * width), BF16),
            pltpu.VMEM((local, 2, leaf, 2 * width), BF16),
        ],
        in_specs=[hbm, vmem, vmem, pl.BlockSpec(memory_space=pl.ANY)],
        out_specs=[vmem] * 2,
        scratch_shapes=[pltpu.SMEM(perm.shape, jnp.int32), pltpu.SemaphoreType.DMA((1,))],
        compiler_params=PARAMS,
        cost_estimate=COST,
        name="prep",
    )(pltpu.with_memory_space_constraint(perm, pltpu.HBM), down, row, after)


def upper_kernel(full, halved, late, perm_hbm, down_ref, row_ref, *refs):
    n, m = len(full), len(halved)
    mids, own_mids, other_mids = refs[:n], refs[n : n + m], refs[n + m : n + 2 * m]
    field_ref, top_ref, spread_ref, perm_ref, sem = refs[n + 2 * m :]
    groups, local = down_ref.shape[:2]
    rank = spread_ref.shape[2] // 2
    fetch = pltpu.make_async_copy(perm_hbm, perm_ref, sem.at[0])
    fetch.start()

    def put(source, h, real, imag):
        spread_ref[source, h, :rank, :NRHS] = real
        spread_ref[source, h, :rank, NRHS:] = imag
        spread_ref[source, h, rank:, :NRHS] = -imag
        spread_ref[source, h, rank:, NRHS:] = real

    left = lax.broadcasted_iota(jnp.int32, (rank, NRHS), 1) < HALF
    for own_ref, other_ref, (k, which) in zip(own_mids, other_mids, halved):
        swap = lax.axis_index("rhs") == 1
        for h in range(local):
            low, high = own_ref[0, h].astype(F32), other_ref[0, h].astype(F32)
            low, high = jnp.where(swap, high, low), jnp.where(swap, low, high)
            real = jnp.where(left, low, pltpu.roll(high, HALF, 1)).astype(BF16)
            imag = jnp.where(left, pltpu.roll(low, HALF, 1), high).astype(BF16)
            put(partner(k, which), h, real, imag)
    for mid_ref, (k, which) in zip(mids, full):
        for h in range(local):
            mid = mid_ref[0, h]
            put(partner(k, which), h, mid[:, :NRHS], mid[:, NRHS:])
    for h in range(local):
        for route in late:
            spread_ref[partner(*route), h] = jnp.zeros(spread_ref.shape[2:], BF16)
        top_ref[1, h] = jnp.zeros(top_ref.shape[2:], F32)
    fetch.wait()
    (group_a, _), (group_b, _) = late_groups(late, perm_ref, groups)
    for h in range(local):
        tops = ([], [])
        for q in range(groups):
            parts = [spread_ref[perm_ref[2 * q + s], h] for s in range(2)]
            top = jnp.dot(
                down_ref[q, h], jnp.concatenate(parts, axis=0), preferred_element_type=F32
            )
            is_a, is_b = group_a == q, group_b == q
            top_ref[jnp.where(is_a, 0, jnp.where(is_b, 1, 2)), h] = top
            lacks = jnp.logical_or(is_a, is_b)
            top = jnp.where(lacks, jnp.zeros_like(top), top).astype(BF16)
            for t in range(2):
                tops[t].append(top[t * rank : (t + 1) * rank])
        for t in range(2):
            rows = jnp.concatenate([row_ref[h, t, q] for q in range(groups)], axis=1)
            field_ref[h, t] = jnp.dot(rows, twisted_rows(tops[t]), preferred_element_type=F32)


def upper(full, halved, late, perm, down, row, mids):
    groups, local, _, width = down.shape
    leaf = row.shape[3]
    rank = width // 4
    vmem = pl.BlockSpec(memory_space=pltpu.VMEM)
    hbm = pl.BlockSpec(memory_space=pltpu.HBM)
    return pl.pallas_call(
        functools.partial(upper_kernel, full, halved, late),
        out_shape=[
            pltpu.VMEM((local, 2, leaf, 2 * NRHS), F32),
            pltpu.VMEM((3, local, 2 * rank, 2 * NRHS), F32),
        ],
        in_specs=[hbm] + [vmem] * (2 + len(mids)),
        out_specs=[vmem] * 2,
        scratch_shapes=[
            pltpu.VMEM((2 * groups, local, 2 * rank, 2 * NRHS), BF16),
            pltpu.SMEM(perm.shape, jnp.int32),
            pltpu.SemaphoreType.DMA((1,)),
        ],
        compiler_params=PARAMS,
        cost_estimate=COST,
        name="upper",
    )(pltpu.with_memory_space_constraint(perm, pltpu.HBM), down, row, *mids)


def finish_kernel(down_ref, row_ref, field_ref, top_ref, mid_a, mid_b, out_hbm, mix_ref, out_ref, sems):
    local, _, leaf, _ = field_ref.shape
    rank = mid_a.shape[2]
    for h in range(local):
        top = jnp.concatenate([top_ref[0, h], top_ref[1, h]], axis=0) + jnp.dot(
            down_ref[h], twisted_rows([mid_a[0, h], mid_b[0, h]]), preferred_element_type=F32
        )
        top = top.astype(BF16)
        for t in range(2):
            rows = twisted_rows([top[r : r + rank] for r in (t * rank, (2 + t) * rank)])
            field = field_ref[h, t] + jnp.dot(
                row_ref[h, t], rows, preferred_element_type=F32
            )
            mix_ref[h, t, pl.ds(0, leaf, stride=2), :] = field[:, :NRHS]
            mix_ref[h, t, pl.ds(1, leaf, stride=2), :] = field[:, NRHS:]
            out_ref[h, t] = mix_ref[h, t].astype(BF16)
    copies = []
    for i, group in enumerate(chunks(local)):
        at = pl.ds(group.start, len(group))
        copies.append(pltpu.make_async_copy(out_ref.at[at], out_hbm.at[at], sems.at[i]))
        copies[-1].start()
    for copy in copies:
        copy.wait()


def finish(down, row, field, top, mids):
    local, _, leaf, _ = field.shape
    shape = (local, 2, 2 * leaf, NRHS)
    vmem = pl.BlockSpec(memory_space=pltpu.VMEM)
    return pl.pallas_call(
        finish_kernel,
        out_shape=jax.ShapeDtypeStruct(shape, BF16),
        in_specs=[vmem] * 6,
        out_specs=pl.BlockSpec(memory_space=pltpu.HBM),
        scratch_shapes=[
            pltpu.VMEM(shape, F32),
            pltpu.VMEM(shape, BF16),
            pltpu.SemaphoreType.DMA((2,)),
        ],
        compiler_params=PARAMS,
        cost_estimate=COST,
        name="finish",
    )(down, row, field, top, *mids)


def send(block, route, dests):
    code = 2 * route[0] + route[1]
    if not code:
        return block
    return lax.ppermute(block, ("blk", "sub"), [(m, m ^ code) for m in range(dests)])


def on_device(
    columns, x_panels, leaf_basis, leaf_count, parent_map, up_transfer, mid_perm, down_transfer, row_basis
):
    boxes, directions, rank, _, leaf = leaf_basis.shape
    basis = leaf_basis.reshape(boxes, directions, rank * 2, leaf)
    groups, _, local = down_transfer.shape[:3]
    down = down_transfer.reshape(groups, local, 2 * rank, 4 * rank)
    row = row_basis.reshape(local, 2, groups, leaf, 2 * rank)
    x = jnp.transpose(x_panels, (0, 2, 3, 1))
    dests = 2 * columns
    two = both_cores((2,))
    full = both_cores(range(columns - 1, 3, -1)) + [(3, 0), (1, 0), (0, 1), (0, 0)]
    late = [(1, 1), (3, 1)]
    if 2 * x.shape[2] == NRHS:
        halved = two
        xs = [x, lax.ppermute(x, "rhs", [(0, 1), (1, 0)])]
        *own_mids, basis, up = own(halved, dests, leaf_count, parent_map, x, basis, up_transfer)
        own_mids = [send(mid, route, dests) for mid, route in zip(own_mids, halved)]
    else:
        full, halved, own_mids, up = two + full, [], [], up_transfer
        xs = [lax.all_gather(x, "rhs", axis=2, tiled=True)]
    n = len(full)
    routes = full + late + halved
    mids = lower(full + late, halved, dests, leaf_count, parent_map, xs, basis, up)
    mids = [send(mid, route, dests) for mid, route in zip(mids, routes)]
    down_late, row_late = prep(late, mid_perm, down, row, [*own_mids, mids[0]][0])
    field, top = upper(
        full, halved, late, mid_perm, down, row, [*mids[:n], *own_mids, *mids[n + 2 :]]
    )
    result = finish(down_late, row_late, field, top, mids[n : n + 2])
    return result.reshape(1, local, 2, leaf, 2, NRHS)


def solution(mesh):
    return jax.shard_map(
        functools.partial(on_device, mesh.shape["blk"]),
        mesh=mesh,
        in_specs=(
            P(("grp", "blk", "sub"), None, None, "rhs"),
            P(("blk", "sub"), "rhs", None, None, None),
            P(("blk", "sub")),
            P("rhs"),
            P(("blk", "sub"), "rhs", None, None),
            P(),
            P(None, "rhs", ("blk", "sub"), None, None, None),
            P("rhs", ("blk", "sub"), None, None, None, None),
        ),
        out_specs=P(("grp", "rhs"), ("blk", "sub"), None, None, None, None),
        check_vma=False,
    )
```

```python
import functools

import jax
import jax.numpy as jnp
from jax import lax
from jax.experimental import pallas as pl
from jax.experimental.pallas import tpu as pltpu
from jax.sharding import PartitionSpec as P

NRHS = 128
HALF = 64
F32 = jnp.float32
BF16 = jnp.bfloat16
PARAMS = pltpu.CompilerParams(vmem_limit_bytes=32 * 1024 * 1024)
COST = pl.CostEstimate(flops=1_000_000, bytes_accessed=10_000, transcendentals=0)


def both_cores(steps):
    return [(k, which) for k in steps for which in (0, 1)]


def partner(k, which):
    z = jnp.bitwise_xor(lax.axis_index("blk"), k)
    core = jnp.bitwise_xor(lax.axis_index("sub"), which)
    return z * 2 + core


def up_stage(outs, routes, parent_ref, up_ref, leaf_ref, cut=lambda mid: mid):
    pairs, local = outs[0].shape[:2]
    for out, (k, which) in zip(outs, routes):
        dest = partner(k, which)
        for p in range(pairs):
            for h in range(local):
                j = dest * local + h
                mid = jnp.dot(
                    up_ref[p, j], leaf_ref[p, parent_ref[j]], preferred_element_type=F32
                )
                out[p, h] = cut(mid).astype(BF16)


def chunks(count):
    middle = (count + 1) // 2
    return [group for group in (range(middle), range(middle, count)) if group]


def leaf_stage(spreads, combine, count_ref, basis_ref, g_ref, leaf_ref, ready):
    boxes, dirs, rows, _ = basis_ref.shape
    rank = rows // 2
    width = leaf_ref.shape[3]
    first = lax.axis_index("rhs") * dirs
    even = pl.ds(0, rank, stride=2)
    odd = pl.ds(1, rank, stride=2)
    for b in range(boxes):
        ready(b)
        spread = spreads(b)
        for d in range(dirs):
            g = lax.dot_general(
                basis_ref[b, d], spread, (((1,), (1,)), ((), ())), preferred_element_type=F32
            )
            g_ref[b * dirs + d, 0] = g[:, :NRHS]
            g_ref[b * dirs + d, 1] = g[:, NRHS:]
        if b == 0:
            ready("count")
        for d in range(dirs):
            slot = b * dirs + d
            live = first + d < count_ref[b]
            pieces = combine(
                [g_ref[slot, i, even, :] for i in range(2)],
                [g_ref[slot, i, odd, :] for i in range(2)],
            )
            pieces = [jnp.where(live, x, jnp.zeros_like(x)).astype(BF16) for x in pieces]
            base = (b % 2) * 2 * rank
            top, bottom = slice(base, base + rank), slice(base + rank, base + 2 * rank)
            if width == NRHS:
                leaf_ref[b // 2, d, top, :] = pieces[0]
                leaf_ref[b // 2, d, bottom, :] = pieces[1]
            else:
                leaf_ref[b // 2, d, top, :NRHS] = pieces[0]
                leaf_ref[b // 2, d, top, NRHS:] = pieces[1]
                leaf_ref[b // 2, d, bottom, :NRHS] = -pieces[1]
                leaf_ref[b // 2, d, bottom, NRHS:] = pieces[0]


def half_columns(even, odd):
    return even[0] + odd[1], even[1] - odd[0]


def all_columns(even, odd):
    return even[0] - odd[1], even[1] + odd[0]


def own_kernel(routes, count_hbm, parent_hbm, x_hbm, basis_hbm, up_hbm, *refs):
    n = len(routes)
    outs, basis_ref, up_ref = refs[:n], refs[n], refs[n + 1]
    count_ref, parent_ref, x_ref, leaf_ref, g_ref, sems = refs[n + 2 :]
    boxes = basis_ref.shape[0]
    copies = {
        "x": pltpu.make_async_copy(x_hbm, x_ref, sems.at[0]),
        "count": pltpu.make_async_copy(count_hbm, count_ref, sems.at[1]),
        "parent": pltpu.make_async_copy(parent_hbm, parent_ref, sems.at[2]),
        "up": pltpu.make_async_copy(up_hbm, up_ref, sems.at[3]),
    }
    for b in range(boxes):
        for i, group in enumerate(chunks(basis_ref.shape[1])):
            at = (b, pl.ds(group.start, len(group)))
            sem = sems.at[4 + 2 * b + i]
            copies[b, i] = pltpu.make_async_copy(basis_hbm.at[at], basis_ref.at[at], sem)
    first_ones = [name for name in copies if name != "up"]
    for name in first_ones + ["up"]:
        copies[name].start()
    for name in first_ones:
        copies[name].wait()
    spreads = []
    for b in range(boxes):
        real, imag = x_ref[b, 0], x_ref[b, 1]
        spreads.append(jnp.concatenate([real, imag, -imag, real], axis=0))
    pairs, local, rank = outs[0].shape[:3]
    first = lax.axis_index("rhs") * basis_ref.shape[1]
    even = pl.ds(0, rank, stride=2)
    odd = pl.ds(1, rank, stride=2)
    jobs = [
        (out, p, h, partner(k, which) * local + h)
        for out, (k, which) in zip(outs, routes)
        for p in range(pairs)
        for h in range(local)
    ]
    for i, (_, p, _, j) in enumerate(jobs):
        d = parent_ref[j]
        for child in range(2):
            b, slot = 2 * p + child, 2 * i + child
            g = lax.dot_general(
                basis_ref[b, d], spreads[b], (((1,), (1,)), ((), ())), preferred_element_type=F32
            )
            g_ref[slot, 0] = g[:, :NRHS]
            g_ref[slot, 1] = g[:, NRHS:]
            live = first + d < count_ref[b]
            pieces = half_columns(
                [g_ref[slot, c, even, :] for c in range(2)],
                [g_ref[slot, c, odd, :] for c in range(2)],
            )
            for c, piece in enumerate(pieces):
                piece = jnp.where(live, piece, jnp.zeros_like(piece)).astype(BF16)
                base = (2 * child + c) * rank
                leaf_ref[i, base : base + rank, :] = piece
    copies["up"].wait()
    for i, (out, p, h, j) in enumerate(jobs):
        mid = jnp.dot(up_ref[p, j], leaf_ref[i], preferred_element_type=F32)
        out[p, h] = mid.astype(BF16)


def own(routes, dests, count, parents, x, basis, up):
    boxes, dirs, rows, _ = basis.shape
    pairs, dirs_up, rank, _ = up.shape
    block = pltpu.VMEM((pairs, dirs_up // dests, rank, NRHS), BF16)
    args = [count, parents, x, basis, up]
    jobs = len(routes) * pairs * (dirs_up // dests)
    return pl.pallas_call(
        functools.partial(own_kernel, routes),
        out_shape=[block] * len(routes)
        + [pltpu.VMEM(basis.shape, BF16), pltpu.VMEM(up.shape, BF16)],
        in_specs=[pl.BlockSpec(memory_space=pltpu.HBM)] * 5,
        out_specs=[pl.BlockSpec(memory_space=pltpu.VMEM)] * (len(routes) + 2),
        scratch_shapes=[
            pltpu.SMEM(count.shape, jnp.int32),
            pltpu.SMEM(parents.shape, jnp.int32),
            pltpu.VMEM(x.shape, BF16),
            pltpu.VMEM((jobs, 4 * rank, NRHS), BF16),
            pltpu.VMEM((2 * jobs, 2, rows, NRHS), F32),
            pltpu.SemaphoreType.DMA((4 + 2 * boxes,)),
        ],
        compiler_params=PARAMS,
        cost_estimate=COST,
        name="own",
    )(*[pltpu.with_memory_space_constraint(arg, pltpu.HBM) for arg in args])


def other_columns(mid):
    left = lax.broadcasted_iota(jnp.int32, (mid.shape[0], NRHS), 1) < HALF
    real, imag = mid[:, :NRHS], mid[:, NRHS:]
    low = jnp.where(left, real, pltpu.roll(imag, HALF, 1))
    high = jnp.where(left, pltpu.roll(real, HALF, 1), imag)
    return jnp.where(lax.axis_index("rhs") == 1, low, high)


def lower_kernel(full, halved, count_hbm, parent_hbm, *refs):
    n, m = len(full), len(halved)
    g_ref, leaf_ref, count_ref, parent_ref, sems = refs[-5:]
    outs = refs[-5 - n - m : -5]
    *xs, basis_ref, up_ref = refs[: -5 - n - m]
    copies = {
        "count": pltpu.make_async_copy(count_hbm, count_ref, sems.at[0]),
        "parent": pltpu.make_async_copy(parent_hbm, parent_ref, sems.at[1]),
    }
    for copy in copies.values():
        copy.start()

    def ready(name):
        if name in copies:
            copies[name].wait()

    def spreads(b):
        if len(xs) == 1:
            return jnp.concatenate([xs[0][b, 0], xs[0][b, 1]], axis=0)
        own, other = xs[0][b], xs[1][b]
        swap = lax.axis_index("rhs") == 1
        low, high = jnp.where(swap, other, own), jnp.where(swap, own, other)
        return jnp.concatenate([low[0], high[0], low[1], high[1]], axis=0)

    leaf_stage(spreads, all_columns, count_ref, basis_ref, g_ref, leaf_ref, ready)
    ready("parent")
    up_stage(outs[:n], full, parent_ref, up_ref, leaf_ref)
    if halved:
        up_stage(outs[n:], halved, parent_ref, up_ref, leaf_ref, other_columns)


def lower(full, halved, dests, count, parents, xs, basis, up):
    boxes, dirs, rows, _ = basis.shape
    pairs, dirs_up, rank, _ = up.shape
    shape = (pairs, dirs_up // dests, rank)
    hbm = pl.BlockSpec(memory_space=pltpu.HBM)
    vmem = pl.BlockSpec(memory_space=pltpu.VMEM)
    n = len(full) + len(halved)
    return pl.pallas_call(
        functools.partial(lower_kernel, full, halved),
        out_shape=[pltpu.VMEM(shape + (2 * NRHS,), BF16)] * len(full)
        + [pltpu.VMEM(shape + (NRHS,), BF16)] * len(halved),
        in_specs=[hbm, hbm] + [vmem] * (2 + len(xs)),
        out_specs=[vmem] * n,
        scratch_shapes=[
            pltpu.VMEM((boxes * dirs, 2, rows, NRHS), F32),
            pltpu.VMEM((pairs, dirs, 4 * rank, 2 * NRHS), BF16),
            pltpu.SMEM(count.shape, jnp.int32),
            pltpu.SMEM(parents.shape, jnp.int32),
            pltpu.SemaphoreType.DMA((2,)),
        ],
        compiler_params=PARAMS,
        cost_estimate=COST,
        name="lower",
    )(*[pltpu.with_memory_space_constraint(a, pltpu.HBM) for a in (count, parents)], *xs, basis, up)


def twist(top):
    return jnp.concatenate([-top[:, NRHS:], top[:, :NRHS]], axis=1)


def twisted_rows(tops):
    return jnp.concatenate([rows for top in tops for rows in (top, twist(top))], axis=0)


def late_groups(late, perm_ref, groups):
    found = []
    for route in late:
        source = partner(*route)
        group, child = 0, 0
        for i in range(2 * groups):
            hit = perm_ref[i] == source
            group = jnp.where(hit, i // 2, group)
            child = jnp.where(hit, i % 2, child)
        found.append((group, child))
    return found


def prep_kernel(late, perm_hbm, down_ref, row_ref, after_ref, down_out, row_out, perm_ref, sem):
    groups, local, rows = down_ref.shape[:3]
    width = row_ref.shape[4]
    fetch = pltpu.make_async_copy(perm_hbm, perm_ref, sem.at[0])
    fetch.start()
    fetch.wait()
    found = late_groups(late, perm_ref, groups)
    same = found[0][0] == found[1][0]
    for h in range(local):
        for i, (group, _) in enumerate(found):
            block = down_ref[group, h]
            for j, (_, child) in enumerate(found):
                part = jnp.where(child == 0, block[:, :width], block[:, width:])
                zeros = jnp.zeros_like(part)
                if i == 0 and j == 1:
                    part = jnp.where(same, part, zeros)
                elif i == 1:
                    part = zeros if j == 0 else jnp.where(same, zeros, part)
                down_out[h, i * rows : (i + 1) * rows, j * width : (j + 1) * width] = part
            for t in range(2):
                row_out[h, t, :, i * width : (i + 1) * width] = row_ref[h, t, group]


def prep(late, perm, down, row, after):
    local, rows = down.shape[1:3]
    leaf, width = row.shape[3:]
    vmem = pl.BlockSpec(memory_space=pltpu.VMEM)
    hbm = pl.BlockSpec(memory_space=pltpu.HBM)
    return pl.pallas_call(
        functools.partial(prep_kernel, late),
        out_shape=[
            pltpu.VMEM((local, 2 * rows, 2 * width), BF16),
            pltpu.VMEM((local, 2, leaf, 2 * width), BF16),
        ],
        in_specs=[hbm, vmem, vmem, pl.BlockSpec(memory_space=pl.ANY)],
        out_specs=[vmem] * 2,
        scratch_shapes=[pltpu.SMEM(perm.shape, jnp.int32), pltpu.SemaphoreType.DMA((1,))],
        compiler_params=PARAMS,
        cost_estimate=COST,
        name="prep",
    )(pltpu.with_memory_space_constraint(perm, pltpu.HBM), down, row, after)


def upper_kernel(full, halved, late, perm_hbm, down_ref, row_ref, *refs):
    n, m = len(full), len(halved)
    mids, own_mids, other_mids = refs[:n], refs[n : n + m], refs[n + m : n + 2 * m]
    field_ref, top_ref, spread_ref, perm_ref, sem = refs[n + 2 * m :]
    groups, local = down_ref.shape[:2]
    rank = spread_ref.shape[2] // 2
    fetch = pltpu.make_async_copy(perm_hbm, perm_ref, sem.at[0])
    fetch.start()

    def put(source, h, real, imag):
        spread_ref[source, h, :rank, :NRHS] = real
        spread_ref[source, h, :rank, NRHS:] = imag
        spread_ref[source, h, rank:, :NRHS] = -imag
        spread_ref[source, h, rank:, NRHS:] = real

    left = lax.broadcasted_iota(jnp.int32, (rank, NRHS), 1) < HALF
    for own_ref, other_ref, (k, which) in zip(own_mids, other_mids, halved):
        swap = lax.axis_index("rhs") == 1
        for h in range(local):
            low, high = own_ref[0, h].astype(F32), other_ref[0, h].astype(F32)
            low, high = jnp.where(swap, high, low), jnp.where(swap, low, high)
            real = jnp.where(left, low, pltpu.roll(high, HALF, 1)).astype(BF16)
            imag = jnp.where(left, pltpu.roll(low, HALF, 1), high).astype(BF16)
            put(partner(k, which), h, real, imag)
    for mid_ref, (k, which) in zip(mids, full):
        for h in range(local):
            mid = mid_ref[0, h]
            put(partner(k, which), h, mid[:, :NRHS], mid[:, NRHS:])
    for h in range(local):
        for route in late:
            spread_ref[partner(*route), h] = jnp.zeros(spread_ref.shape[2:], BF16)
        top_ref[1, h] = jnp.zeros(top_ref.shape[2:], F32)
    fetch.wait()
    (group_a, _), (group_b, _) = late_groups(late, perm_ref, groups)
    for h in range(local):
        tops = ([], [])
        for q in range(groups):
            parts = [spread_ref[perm_ref[2 * q + s], h] for s in range(2)]
            top = jnp.dot(
                down_ref[q, h], jnp.concatenate(parts, axis=0), preferred_element_type=F32
            )
            is_a, is_b = group_a == q, group_b == q
            top_ref[jnp.where(is_a, 0, jnp.where(is_b, 1, 2)), h] = top
            lacks = jnp.logical_or(is_a, is_b)
            top = jnp.where(lacks, jnp.zeros_like(top), top).astype(BF16)
            for t in range(2):
                tops[t].append(top[t * rank : (t + 1) * rank])
        for t in range(2):
            rows = jnp.concatenate([row_ref[h, t, q] for q in range(groups)], axis=1)
            field_ref[h, t] = jnp.dot(rows, twisted_rows(tops[t]), preferred_element_type=F32)


def upper(full, halved, late, perm, down, row, mids):
    groups, local, _, width = down.shape
    leaf = row.shape[3]
    rank = width // 4
    vmem = pl.BlockSpec(memory_space=pltpu.VMEM)
    hbm = pl.BlockSpec(memory_space=pltpu.HBM)
    return pl.pallas_call(
        functools.partial(upper_kernel, full, halved, late),
        out_shape=[
            pltpu.VMEM((local, 2, leaf, 2 * NRHS), F32),
            pltpu.VMEM((3, local, 2 * rank, 2 * NRHS), F32),
        ],
        in_specs=[hbm] + [vmem] * (2 + len(mids)),
        out_specs=[vmem] * 2,
        scratch_shapes=[
            pltpu.VMEM((2 * groups, local, 2 * rank, 2 * NRHS), BF16),
            pltpu.SMEM(perm.shape, jnp.int32),
            pltpu.SemaphoreType.DMA((1,)),
        ],
        compiler_params=PARAMS,
        cost_estimate=COST,
        name="upper",
    )(pltpu.with_memory_space_constraint(perm, pltpu.HBM), down, row, *mids)


def finish_kernel(down_ref, row_ref, field_ref, top_ref, mid_a, mid_b, out_hbm, mix_ref, out_ref, sems):
    local, _, leaf, _ = field_ref.shape
    rank = mid_a.shape[2]
    for h in range(local):
        top = jnp.concatenate([top_ref[0, h], top_ref[1, h]], axis=0) + jnp.dot(
            down_ref[h], twisted_rows([mid_a[0, h], mid_b[0, h]]), preferred_element_type=F32
        )
        top = top.astype(BF16)
        for t in range(2):
            rows = twisted_rows([top[r : r + rank] for r in (t * rank, (2 + t) * rank)])
            field = field_ref[h, t] + jnp.dot(
                row_ref[h, t], rows, preferred_element_type=F32
            )
            mix_ref[h, t, pl.ds(0, leaf, stride=2), :] = field[:, :NRHS]
            mix_ref[h, t, pl.ds(1, leaf, stride=2), :] = field[:, NRHS:]
            out_ref[h, t] = mix_ref[h, t].astype(BF16)
    copies = []
    for i, group in enumerate(chunks(local)):
        at = pl.ds(group.start, len(group))
        copies.append(pltpu.make_async_copy(out_ref.at[at], out_hbm.at[at], sems.at[i]))
        copies[-1].start()
    for copy in copies:
        copy.wait()


def finish(down, row, field, top, mids):
    local, _, leaf, _ = field.shape
    shape = (local, 2, 2 * leaf, NRHS)
    vmem = pl.BlockSpec(memory_space=pltpu.VMEM)
    return pl.pallas_call(
        finish_kernel,
        out_shape=jax.ShapeDtypeStruct(shape, BF16),
        in_specs=[vmem] * 6,
        out_specs=pl.BlockSpec(memory_space=pltpu.HBM),
        scratch_shapes=[
            pltpu.VMEM(shape, F32),
            pltpu.VMEM(shape, BF16),
            pltpu.SemaphoreType.DMA((2,)),
        ],
        compiler_params=PARAMS,
        cost_estimate=COST,
        name="finish",
    )(down, row, field, top, *mids)


def send(block, route, dests):
    code = 2 * route[0] + route[1]
    if not code:
        return block
    return lax.ppermute(block, ("blk", "sub"), [(m, m ^ code) for m in range(dests)])


def on_device(
    columns, x_panels, leaf_basis, leaf_count, parent_map, up_transfer, mid_perm, down_transfer, row_basis
):
    boxes, directions, rank, _, leaf = leaf_basis.shape
    basis = leaf_basis.reshape(boxes, directions, rank * 2, leaf)
    groups, _, local = down_transfer.shape[:3]
    down = down_transfer.reshape(groups, local, 2 * rank, 4 * rank)
    row = row_basis.reshape(local, 2, groups, leaf, 2 * rank)
    x = jnp.transpose(x_panels, (0, 2, 3, 1))
    dests = 2 * columns
    two = both_cores((2,))
    full = both_cores(range(columns - 1, 3, -1)) + [(3, 0), (1, 0), (0, 1), (0, 0)]
    late = [(1, 1), (3, 1)]
    if 2 * x.shape[2] == NRHS:
        halved = two
        xs = [x, lax.ppermute(x, "rhs", [(0, 1), (1, 0)])]
        *own_mids, basis, up = own(halved, dests, leaf_count, parent_map, x, basis, up_transfer)
        own_mids = [send(mid, route, dests) for mid, route in zip(own_mids, halved)]
    else:
        full, halved, own_mids, up = two + full, [], [], up_transfer
        xs = [lax.all_gather(x, "rhs", axis=2, tiled=True)]
    n = len(full)
    routes = full + late + halved
    mids = lower(full + late, halved, dests, leaf_count, parent_map, xs, basis, up)
    mids = [send(mid, route, dests) for mid, route in zip(mids, routes)]
    down_late, row_late = prep(late, mid_perm, down, row, [*own_mids, mids[0]][0])
    field, top = upper(
        full, halved, late, mid_perm, down, row, [*mids[:n], *own_mids, *mids[n + 2 :]]
    )
    result = finish(down_late, row_late, field, top, mids[n : n + 2])
    return result.reshape(1, local, 2, leaf, 2, NRHS)


def solution(mesh):
    return jax.shard_map(
        functools.partial(on_device, mesh.shape["blk"]),
        mesh=mesh,
        in_specs=(
            P(("grp", "blk", "sub"), None, None, "rhs"),
            P(("blk", "sub"), "rhs", None, None, None),
            P(("blk", "sub")),
            P("rhs"),
            P(("blk", "sub"), "rhs", None, None),
            P(),
            P(None, "rhs", ("blk", "sub"), None, None, None),
            P("rhs", ("blk", "sub"), None, None, None, None),
        ),
        out_specs=P(("grp", "rhs"), ("blk", "sub"), None, None, None, None),
        check_vma=False,
    )
```

```python
import functools

import jax
import jax.numpy as jnp
from jax import lax
from jax.experimental import pallas as pl
from jax.experimental.pallas import tpu as pltpu
from jax.sharding import PartitionSpec as P

NRHS = 128
HALF = 64
F32 = jnp.float32
BF16 = jnp.bfloat16
PARAMS = pltpu.CompilerParams(vmem_limit_bytes=32 * 1024 * 1024)
COST = pl.CostEstimate(flops=1_000_000, bytes_accessed=10_000, transcendentals=0)


def both_cores(steps):
    return [(k, which) for k in steps for which in (0, 1)]


def partner(k, which):
    z = jnp.bitwise_xor(lax.axis_index("blk"), k)
    core = jnp.bitwise_xor(lax.axis_index("sub"), which)
    return z * 2 + core


def up_stage(outs, routes, parent_ref, up_ref, leaf_ref, cut=lambda mid: mid):
    pairs, local = outs[0].shape[:2]
    for out, (k, which) in zip(outs, routes):
        dest = partner(k, which)
        for p in range(pairs):
            for h in range(local):
                j = dest * local + h
                mid = jnp.dot(
                    up_ref[p, j], leaf_ref[p, parent_ref[j]], preferred_element_type=F32
                )
                out[p, h] = cut(mid).astype(BF16)


def chunks(count):
    middle = (count + 1) // 2
    return [group for group in (range(middle), range(middle, count)) if group]


def leaf_stage(spreads, combine, count_ref, basis_ref, g_ref, leaf_ref, ready):
    boxes, dirs, rows, _ = basis_ref.shape
    rank = rows // 2
    width = leaf_ref.shape[3]
    first = lax.axis_index("rhs") * dirs
    even = pl.ds(0, rank, stride=2)
    odd = pl.ds(1, rank, stride=2)
    for b in range(boxes):
        ready(b)
        spread = spreads(b)
        for d in range(dirs):
            g = lax.dot_general(
                basis_ref[b, d], spread, (((1,), (1,)), ((), ())), preferred_element_type=F32
            )
            g_ref[b * dirs + d, 0] = g[:, :NRHS]
            g_ref[b * dirs + d, 1] = g[:, NRHS:]
        if b == 0:
            ready("count")
        for d in range(dirs):
            slot = b * dirs + d
            live = first + d < count_ref[b]
            pieces = combine(
                [g_ref[slot, i, even, :] for i in range(2)],
                [g_ref[slot, i, odd, :] for i in range(2)],
            )
            pieces = [jnp.where(live, x, jnp.zeros_like(x)).astype(BF16) for x in pieces]
            base = (b % 2) * 2 * rank
            top, bottom = slice(base, base + rank), slice(base + rank, base + 2 * rank)
            if width == NRHS:
                leaf_ref[b // 2, d, top, :] = pieces[0]
                leaf_ref[b // 2, d, bottom, :] = pieces[1]
            else:
                leaf_ref[b // 2, d, top, :NRHS] = pieces[0]
                leaf_ref[b // 2, d, top, NRHS:] = pieces[1]
                leaf_ref[b // 2, d, bottom, :NRHS] = -pieces[1]
                leaf_ref[b // 2, d, bottom, NRHS:] = pieces[0]


def half_columns(even, odd):
    return even[0] + odd[1], even[1] - odd[0]


def all_columns(even, odd):
    return even[0] - odd[1], even[1] + odd[0]


def own_kernel(routes, count_hbm, parent_hbm, x_hbm, basis_hbm, up_hbm, *refs):
    n = len(routes)
    outs, basis_ref, up_ref = refs[:n], refs[n], refs[n + 1]
    count_ref, parent_ref, x_ref, leaf_ref, g_ref, sems = refs[n + 2 :]
    boxes = basis_ref.shape[0]
    copies = {
        "x": pltpu.make_async_copy(x_hbm, x_ref, sems.at[0]),
        "count": pltpu.make_async_copy(count_hbm, count_ref, sems.at[1]),
        "parent": pltpu.make_async_copy(parent_hbm, parent_ref, sems.at[2]),
        "up": pltpu.make_async_copy(up_hbm, up_ref, sems.at[3]),
    }
    for b in range(boxes):
        copies[b] = pltpu.make_async_copy(basis_hbm.at[b], basis_ref.at[b], sems.at[4 + b])
    for name in ["parent", "count", "x", *range(boxes), "up"]:
        copies[name].start()
    for name in ["x", "count", "parent", *range(boxes)]:
        copies[name].wait()
    spreads = []
    for b in range(boxes):
        real, imag = x_ref[b, 0], x_ref[b, 1]
        spreads.append(jnp.concatenate([real, imag, -imag, real], axis=0))
    pairs, local, rank = outs[0].shape[:3]
    first = lax.axis_index("rhs") * basis_ref.shape[1]
    even = pl.ds(0, rank, stride=2)
    odd = pl.ds(1, rank, stride=2)
    jobs = [
        (out, p, h, partner(k, which) * local + h)
        for out, (k, which) in zip(outs, routes)
        for p in range(pairs)
        for h in range(local)
    ]
    for i, (_, p, _, j) in enumerate(jobs):
        d = parent_ref[j]
        for child in range(2):
            b, slot = 2 * p + child, 2 * i + child
            g = lax.dot_general(
                basis_ref[b, d], spreads[b], (((1,), (1,)), ((), ())), preferred_element_type=F32
            )
            g_ref[slot, 0] = g[:, :NRHS]
            g_ref[slot, 1] = g[:, NRHS:]
            live = first + d < count_ref[b]
            pieces = half_columns(
                [g_ref[slot, c, even, :] for c in range(2)],
                [g_ref[slot, c, odd, :] for c in range(2)],
            )
            for c, piece in enumerate(pieces):
                piece = jnp.where(live, piece, jnp.zeros_like(piece)).astype(BF16)
                base = (2 * child + c) * rank
                leaf_ref[i, base : base + rank, :] = piece
    copies["up"].wait()
    for i, (out, p, h, j) in enumerate(jobs):
        mid = jnp.dot(up_ref[p, j], leaf_ref[i], preferred_element_type=F32)
        out[p, h] = mid.astype(BF16)


def own(routes, dests, count, parents, x, basis, up):
    boxes, dirs, rows, _ = basis.shape
    pairs, dirs_up, rank, _ = up.shape
    block = pltpu.VMEM((pairs, dirs_up // dests, rank, NRHS), BF16)
    args = [count, parents, x, basis, up]
    jobs = len(routes) * pairs * (dirs_up // dests)
    return pl.pallas_call(
        functools.partial(own_kernel, routes),
        out_shape=[block] * len(routes)
        + [pltpu.VMEM(basis.shape, BF16), pltpu.VMEM(up.shape, BF16)],
        in_specs=[pl.BlockSpec(memory_space=pltpu.HBM)] * 5,
        out_specs=[pl.BlockSpec(memory_space=pltpu.VMEM)] * (len(routes) + 2),
        scratch_shapes=[
            pltpu.SMEM(count.shape, jnp.int32),
            pltpu.SMEM(parents.shape, jnp.int32),
            pltpu.VMEM(x.shape, BF16),
            pltpu.VMEM((jobs, 4 * rank, NRHS), BF16),
            pltpu.VMEM((2 * jobs, 2, rows, NRHS), F32),
            pltpu.SemaphoreType.DMA((4 + boxes,)),
        ],
        compiler_params=PARAMS,
        cost_estimate=COST,
        name="own",
    )(*[pltpu.with_memory_space_constraint(arg, pltpu.HBM) for arg in args])


def other_columns(mid):
    left = lax.broadcasted_iota(jnp.int32, (mid.shape[0], NRHS), 1) < HALF
    real, imag = mid[:, :NRHS], mid[:, NRHS:]
    low = jnp.where(left, real, pltpu.roll(imag, HALF, 1))
    high = jnp.where(left, pltpu.roll(real, HALF, 1), imag)
    return jnp.where(lax.axis_index("rhs") == 1, low, high)


def lower_kernel(full, halved, count_hbm, parent_hbm, *refs):
    n, m = len(full), len(halved)
    g_ref, leaf_ref, count_ref, parent_ref, sems = refs[-5:]
    outs = refs[-5 - n - m : -5]
    *xs, basis_ref, up_ref = refs[: -5 - n - m]
    copies = {
        "count": pltpu.make_async_copy(count_hbm, count_ref, sems.at[0]),
        "parent": pltpu.make_async_copy(parent_hbm, parent_ref, sems.at[1]),
    }
    for copy in copies.values():
        copy.start()

    def ready(name):
        if name in copies:
            copies[name].wait()

    def spreads(b):
        if len(xs) == 1:
            return jnp.concatenate([xs[0][b, 0], xs[0][b, 1]], axis=0)
        own, other = xs[0][b], xs[1][b]
        swap = lax.axis_index("rhs") == 1
        low, high = jnp.where(swap, other, own), jnp.where(swap, own, other)
        return jnp.concatenate([low[0], high[0], low[1], high[1]], axis=0)

    leaf_stage(spreads, all_columns, count_ref, basis_ref, g_ref, leaf_ref, ready)
    ready("parent")
    up_stage(outs[:n], full, parent_ref, up_ref, leaf_ref)
    if halved:
        up_stage(outs[n:], halved, parent_ref, up_ref, leaf_ref, other_columns)


def lower(full, halved, dests, count, parents, xs, basis, up):
    boxes, dirs, rows, _ = basis.shape
    pairs, dirs_up, rank, _ = up.shape
    shape = (pairs, dirs_up // dests, rank)
    hbm = pl.BlockSpec(memory_space=pltpu.HBM)
    vmem = pl.BlockSpec(memory_space=pltpu.VMEM)
    n = len(full) + len(halved)
    return pl.pallas_call(
        functools.partial(lower_kernel, full, halved),
        out_shape=[pltpu.VMEM(shape + (2 * NRHS,), BF16)] * len(full)
        + [pltpu.VMEM(shape + (NRHS,), BF16)] * len(halved),
        in_specs=[hbm, hbm] + [vmem] * (2 + len(xs)),
        out_specs=[vmem] * n,
        scratch_shapes=[
            pltpu.VMEM((boxes * dirs, 2, rows, NRHS), F32),
            pltpu.VMEM((pairs, dirs, 4 * rank, 2 * NRHS), BF16),
            pltpu.SMEM(count.shape, jnp.int32),
            pltpu.SMEM(parents.shape, jnp.int32),
            pltpu.SemaphoreType.DMA((2,)),
        ],
        compiler_params=PARAMS,
        cost_estimate=COST,
        name="lower",
    )(*[pltpu.with_memory_space_constraint(a, pltpu.HBM) for a in (count, parents)], *xs, basis, up)


def twist(top):
    return jnp.concatenate([-top[:, NRHS:], top[:, :NRHS]], axis=1)


def twisted_rows(tops):
    return jnp.concatenate([rows for top in tops for rows in (top, twist(top))], axis=0)


def late_groups(late, perm_ref, groups):
    found = []
    for route in late:
        source = partner(*route)
        group, child = 0, 0
        for i in range(2 * groups):
            hit = perm_ref[i] == source
            group = jnp.where(hit, i // 2, group)
            child = jnp.where(hit, i % 2, child)
        found.append((group, child))
    return found


def prep_kernel(late, perm_hbm, down_ref, row_ref, after_ref, down_out, row_out, perm_ref, sem):
    groups, local, rows = down_ref.shape[:3]
    width = row_ref.shape[4]
    fetch = pltpu.make_async_copy(perm_hbm, perm_ref, sem.at[0])
    fetch.start()
    fetch.wait()
    found = late_groups(late, perm_ref, groups)
    same = found[0][0] == found[1][0]
    for h in range(local):
        for i, (group, _) in enumerate(found):
            block = down_ref[group, h]
            for j, (_, child) in enumerate(found):
                part = jnp.where(child == 0, block[:, :width], block[:, width:])
                zeros = jnp.zeros_like(part)
                if i == 0 and j == 1:
                    part = jnp.where(same, part, zeros)
                elif i == 1:
                    part = zeros if j == 0 else jnp.where(same, zeros, part)
                down_out[h, i * rows : (i + 1) * rows, j * width : (j + 1) * width] = part
            for t in range(2):
                row_out[h, t, :, i * width : (i + 1) * width] = row_ref[h, t, group]


def prep(late, perm, down, row, after):
    local, rows = down.shape[1:3]
    leaf, width = row.shape[3:]
    vmem = pl.BlockSpec(memory_space=pltpu.VMEM)
    hbm = pl.BlockSpec(memory_space=pltpu.HBM)
    return pl.pallas_call(
        functools.partial(prep_kernel, late),
        out_shape=[
            pltpu.VMEM((local, 2 * rows, 2 * width), BF16),
            pltpu.VMEM((local, 2, leaf, 2 * width), BF16),
        ],
        in_specs=[hbm, vmem, vmem, pl.BlockSpec(memory_space=pl.ANY)],
        out_specs=[vmem] * 2,
        scratch_shapes=[pltpu.SMEM(perm.shape, jnp.int32), pltpu.SemaphoreType.DMA((1,))],
        compiler_params=PARAMS,
        cost_estimate=COST,
        name="prep",
    )(pltpu.with_memory_space_constraint(perm, pltpu.HBM), down, row, after)


def upper_kernel(full, halved, late, perm_hbm, down_ref, row_ref, *refs):
    n, m = len(full), len(halved)
    mids, own_mids, other_mids = refs[:n], refs[n : n + m], refs[n + m : n + 2 * m]
    field_ref, top_ref, spread_ref, perm_ref, sem = refs[n + 2 * m :]
    groups, local = down_ref.shape[:2]
    rank = spread_ref.shape[2] // 2
    fetch = pltpu.make_async_copy(perm_hbm, perm_ref, sem.at[0])
    fetch.start()

    def put(source, h, real, imag):
        spread_ref[source, h, :rank, :NRHS] = real
        spread_ref[source, h, :rank, NRHS:] = imag
        spread_ref[source, h, rank:, :NRHS] = -imag
        spread_ref[source, h, rank:, NRHS:] = real

    left = lax.broadcasted_iota(jnp.int32, (rank, NRHS), 1) < HALF
    for own_ref, other_ref, (k, which) in zip(own_mids, other_mids, halved):
        swap = lax.axis_index("rhs") == 1
        for h in range(local):
            low, high = own_ref[0, h].astype(F32), other_ref[0, h].astype(F32)
            low, high = jnp.where(swap, high, low), jnp.where(swap, low, high)
            real = jnp.where(left, low, pltpu.roll(high, HALF, 1)).astype(BF16)
            imag = jnp.where(left, pltpu.roll(low, HALF, 1), high).astype(BF16)
            put(partner(k, which), h, real, imag)
    for mid_ref, (k, which) in zip(mids, full):
        for h in range(local):
            mid = mid_ref[0, h]
            put(partner(k, which), h, mid[:, :NRHS], mid[:, NRHS:])
    for h in range(local):
        for route in late:
            spread_ref[partner(*route), h] = jnp.zeros(spread_ref.shape[2:], BF16)
        top_ref[1, h] = jnp.zeros(top_ref.shape[2:], F32)
    fetch.wait()
    (group_a, _), (group_b, _) = late_groups(late, perm_ref, groups)
    for h in range(local):
        tops = ([], [])
        for q in range(groups):
            parts = [spread_ref[perm_ref[2 * q + s], h] for s in range(2)]
            top = jnp.dot(
                down_ref[q, h], jnp.concatenate(parts, axis=0), preferred_element_type=F32
            )
            is_a, is_b = group_a == q, group_b == q
            top_ref[jnp.where(is_a, 0, jnp.where(is_b, 1, 2)), h] = top
            lacks = jnp.logical_or(is_a, is_b)
            top = jnp.where(lacks, jnp.zeros_like(top), top).astype(BF16)
            for t in range(2):
                tops[t].append(top[t * rank : (t + 1) * rank])
        for t in range(2):
            rows = jnp.concatenate([row_ref[h, t, q] for q in range(groups)], axis=1)
            field_ref[h, t] = jnp.dot(rows, twisted_rows(tops[t]), preferred_element_type=F32)


def upper(full, halved, late, perm, down, row, mids):
    groups, local, _, width = down.shape
    leaf = row.shape[3]
    rank = width // 4
    vmem = pl.BlockSpec(memory_space=pltpu.VMEM)
    hbm = pl.BlockSpec(memory_space=pltpu.HBM)
    return pl.pallas_call(
        functools.partial(upper_kernel, full, halved, late),
        out_shape=[
            pltpu.VMEM((local, 2, leaf, 2 * NRHS), F32),
            pltpu.VMEM((3, local, 2 * rank, 2 * NRHS), F32),
        ],
        in_specs=[hbm] + [vmem] * (2 + len(mids)),
        out_specs=[vmem] * 2,
        scratch_shapes=[
            pltpu.VMEM((2 * groups, local, 2 * rank, 2 * NRHS), BF16),
            pltpu.SMEM(perm.shape, jnp.int32),
            pltpu.SemaphoreType.DMA((1,)),
        ],
        compiler_params=PARAMS,
        cost_estimate=COST,
        name="upper",
    )(pltpu.with_memory_space_constraint(perm, pltpu.HBM), down, row, *mids)


def finish_kernel(down_ref, row_ref, field_ref, top_ref, mid_a, mid_b, out_hbm, mix_ref, out_ref, sems):
    local, _, leaf, _ = field_ref.shape
    rank = mid_a.shape[2]
    for h in range(local):
        top = jnp.concatenate([top_ref[0, h], top_ref[1, h]], axis=0) + jnp.dot(
            down_ref[h], twisted_rows([mid_a[0, h], mid_b[0, h]]), preferred_element_type=F32
        )
        top = top.astype(BF16)
        for t in range(2):
            rows = twisted_rows([top[r : r + rank] for r in (t * rank, (2 + t) * rank)])
            field = field_ref[h, t] + jnp.dot(
                row_ref[h, t], rows, preferred_element_type=F32
            )
            mix_ref[h, t, pl.ds(0, leaf, stride=2), :] = field[:, :NRHS]
            mix_ref[h, t, pl.ds(1, leaf, stride=2), :] = field[:, NRHS:]
            out_ref[h, t] = mix_ref[h, t].astype(BF16)
    copies = []
    for i, group in enumerate(chunks(local)):
        at = pl.ds(group.start, len(group))
        copies.append(pltpu.make_async_copy(out_ref.at[at], out_hbm.at[at], sems.at[i]))
        copies[-1].start()
    for copy in copies:
        copy.wait()


def finish(down, row, field, top, mids):
    local, _, leaf, _ = field.shape
    shape = (local, 2, 2 * leaf, NRHS)
    vmem = pl.BlockSpec(memory_space=pltpu.VMEM)
    return pl.pallas_call(
        finish_kernel,
        out_shape=jax.ShapeDtypeStruct(shape, BF16),
        in_specs=[vmem] * 6,
        out_specs=pl.BlockSpec(memory_space=pltpu.HBM),
        scratch_shapes=[
            pltpu.VMEM(shape, F32),
            pltpu.VMEM(shape, BF16),
            pltpu.SemaphoreType.DMA((2,)),
        ],
        compiler_params=PARAMS,
        cost_estimate=COST,
        name="finish",
    )(down, row, field, top, *mids)


def send(block, route, dests):
    code = 2 * route[0] + route[1]
    if not code:
        return block
    return lax.ppermute(block, ("blk", "sub"), [(m, m ^ code) for m in range(dests)])


def on_device(
    columns, x_panels, leaf_basis, leaf_count, parent_map, up_transfer, mid_perm, down_transfer, row_basis
):
    boxes, directions, rank, _, leaf = leaf_basis.shape
    basis = leaf_basis.reshape(boxes, directions, rank * 2, leaf)
    groups, _, local = down_transfer.shape[:3]
    down = down_transfer.reshape(groups, local, 2 * rank, 4 * rank)
    row = row_basis.reshape(local, 2, groups, leaf, 2 * rank)
    x = jnp.transpose(x_panels, (0, 2, 3, 1))
    dests = 2 * columns
    two = both_cores((2,))
    full = both_cores(range(columns - 1, 3, -1)) + [(3, 0), (1, 0), (0, 1), (0, 0)]
    late = [(1, 1), (3, 1)]
    if 2 * x.shape[2] == NRHS:
        halved = two
        xs = [x, lax.ppermute(x, "rhs", [(0, 1), (1, 0)])]
        *own_mids, basis, up = own(halved, dests, leaf_count, parent_map, x, basis, up_transfer)
        own_mids = [send(mid, route, dests) for mid, route in zip(own_mids, halved)]
    else:
        full, halved, own_mids, up = two + full, [], [], up_transfer
        xs = [lax.all_gather(x, "rhs", axis=2, tiled=True)]
    n = len(full)
    routes = full + late + halved
    mids = lower(full + late, halved, dests, leaf_count, parent_map, xs, basis, up)
    mids = [send(mid, route, dests) for mid, route in zip(mids, routes)]
    down_late, row_late = prep(late, mid_perm, down, row, [*own_mids, mids[0]][0])
    field, top = upper(
        full, halved, late, mid_perm, down, row, [*mids[:n], *own_mids, *mids[n + 2 :]]
    )
    result = finish(down_late, row_late, field, top, mids[n : n + 2])
    return result.reshape(1, local, 2, leaf, 2, NRHS)


def solution(mesh):
    return jax.shard_map(
        functools.partial(on_device, mesh.shape["blk"]),
        mesh=mesh,
        in_specs=(
            P(("grp", "blk", "sub"), None, None, "rhs"),
            P(("blk", "sub"), "rhs", None, None, None),
            P(("blk", "sub")),
            P("rhs"),
            P(("blk", "sub"), "rhs", None, None),
            P(),
            P(None, "rhs", ("blk", "sub"), None, None, None),
            P("rhs", ("blk", "sub"), None, None, None, None),
        ),
        out_specs=P(("grp", "rhs"), ("blk", "sub"), None, None, None, None),
        check_vma=False,
    )
```

```python
import functools

import jax
import jax.numpy as jnp
from jax import lax
from jax.experimental import pallas as pl
from jax.experimental.pallas import tpu as pltpu
from jax.sharding import PartitionSpec as P

NRHS = 128
HALF = 64
F32 = jnp.float32
BF16 = jnp.bfloat16
PARAMS = pltpu.CompilerParams(vmem_limit_bytes=32 * 1024 * 1024)
COST = pl.CostEstimate(flops=1_000_000, bytes_accessed=10_000, transcendentals=0)


def both_cores(steps):
    return [(k, which) for k in steps for which in (0, 1)]


def partner(k, which):
    z = jnp.bitwise_xor(lax.axis_index("blk"), k)
    core = jnp.bitwise_xor(lax.axis_index("sub"), which)
    return z * 2 + core


def up_stage(outs, routes, parent_ref, up_ref, leaf_ref, cut=lambda mid: mid):
    pairs, local = outs[0].shape[:2]
    for out, (k, which) in zip(outs, routes):
        dest = partner(k, which)
        for p in range(pairs):
            for h in range(local):
                j = dest * local + h
                mid = jnp.dot(
                    up_ref[p, j], leaf_ref[p, parent_ref[j]], preferred_element_type=F32
                )
                out[p, h] = cut(mid).astype(BF16)


def chunks(count):
    middle = (count + 1) // 2
    return [group for group in (range(middle), range(middle, count)) if group]


def leaf_stage(spreads, combine, count_ref, basis_ref, g_ref, leaf_ref, ready):
    boxes, dirs, rows, _ = basis_ref.shape
    rank = rows // 2
    width = leaf_ref.shape[3]
    first = lax.axis_index("rhs") * dirs
    even = pl.ds(0, rank, stride=2)
    odd = pl.ds(1, rank, stride=2)
    for b in range(boxes):
        ready(b)
        spread = spreads(b)
        for d in range(dirs):
            g = lax.dot_general(
                basis_ref[b, d], spread, (((1,), (1,)), ((), ())), preferred_element_type=F32
            )
            g_ref[b * dirs + d, 0] = g[:, :NRHS]
            g_ref[b * dirs + d, 1] = g[:, NRHS:]
        if b == 0:
            ready("count")
        for d in range(dirs):
            slot = b * dirs + d
            live = first + d < count_ref[b]
            pieces = combine(
                [g_ref[slot, i, even, :] for i in range(2)],
                [g_ref[slot, i, odd, :] for i in range(2)],
            )
            pieces = [jnp.where(live, x, jnp.zeros_like(x)).astype(BF16) for x in pieces]
            base = (b % 2) * 2 * rank
            top, bottom = slice(base, base + rank), slice(base + rank, base + 2 * rank)
            if width == NRHS:
                leaf_ref[b // 2, d, top, :] = pieces[0]
                leaf_ref[b // 2, d, bottom, :] = pieces[1]
            else:
                leaf_ref[b // 2, d, top, :NRHS] = pieces[0]
                leaf_ref[b // 2, d, top, NRHS:] = pieces[1]
                leaf_ref[b // 2, d, bottom, :NRHS] = -pieces[1]
                leaf_ref[b // 2, d, bottom, NRHS:] = pieces[0]


def half_columns(even, odd):
    return even[0] + odd[1], even[1] - odd[0]


def all_columns(even, odd):
    return even[0] - odd[1], even[1] + odd[0]


def own_kernel(routes, count_hbm, parent_hbm, x_hbm, basis_hbm, up_hbm, *refs):
    n = len(routes)
    outs, basis_ref, up_ref = refs[:n], refs[n], refs[n + 1]
    count_ref, parent_ref, x_ref, leaf_ref, g_ref, sems = refs[n + 2 :]
    boxes = basis_ref.shape[0]
    copies = {
        "x": pltpu.make_async_copy(x_hbm, x_ref, sems.at[0]),
        "count": pltpu.make_async_copy(count_hbm, count_ref, sems.at[1]),
        "parent": pltpu.make_async_copy(parent_hbm, parent_ref, sems.at[2]),
        "up": pltpu.make_async_copy(up_hbm, up_ref, sems.at[3]),
    }
    for b in range(boxes):
        copies[b] = pltpu.make_async_copy(basis_hbm.at[b], basis_ref.at[b], sems.at[4 + b])
    for name in ["x", "count", "parent", *range(boxes), "up"]:
        copies[name].start()
    for name in ["x", "count", "parent", *range(boxes)]:
        copies[name].wait()
    spreads = []
    for b in range(boxes):
        real, imag = x_ref[b, 0], x_ref[b, 1]
        spreads.append(jnp.concatenate([real, imag, -imag, real], axis=0))
    pairs, local, rank = outs[0].shape[:3]
    first = lax.axis_index("rhs") * basis_ref.shape[1]
    even = pl.ds(0, rank, stride=2)
    odd = pl.ds(1, rank, stride=2)
    jobs = [
        (out, p, h, partner(k, which) * local + h)
        for out, (k, which) in zip(outs, routes)
        for p in range(pairs)
        for h in range(local)
    ]
    for i, (_, p, _, j) in enumerate(jobs):
        d = parent_ref[j]
        for child in range(2):
            b, slot = 2 * p + child, 2 * i + child
            g = lax.dot_general(
                basis_ref[b, d], spreads[b], (((1,), (1,)), ((), ())), preferred_element_type=F32
            )
            g_ref[slot, 0] = g[:, :NRHS]
            g_ref[slot, 1] = g[:, NRHS:]
            live = first + d < count_ref[b]
            pieces = half_columns(
                [g_ref[slot, c, even, :] for c in range(2)],
                [g_ref[slot, c, odd, :] for c in range(2)],
            )
            for c, piece in enumerate(pieces):
                piece = jnp.where(live, piece, jnp.zeros_like(piece)).astype(BF16)
                base = (2 * child + c) * rank
                leaf_ref[i, base : base + rank, :] = piece
    copies["up"].wait()
    for i, (out, p, h, j) in enumerate(jobs):
        mid = jnp.dot(up_ref[p, j], leaf_ref[i], preferred_element_type=F32)
        out[p, h] = mid.astype(BF16)


def own(routes, dests, count, parents, x, basis, up):
    boxes, dirs, rows, _ = basis.shape
    pairs, dirs_up, rank, _ = up.shape
    block = pltpu.VMEM((pairs, dirs_up // dests, rank, NRHS), BF16)
    args = [count, parents, x, basis, up]
    jobs = len(routes) * pairs * (dirs_up // dests)
    return pl.pallas_call(
        functools.partial(own_kernel, routes),
        out_shape=[block] * len(routes)
        + [pltpu.VMEM(basis.shape, BF16), pltpu.VMEM(up.shape, BF16)],
        in_specs=[pl.BlockSpec(memory_space=pltpu.HBM)] * 5,
        out_specs=[pl.BlockSpec(memory_space=pltpu.VMEM)] * (len(routes) + 2),
        scratch_shapes=[
            pltpu.SMEM(count.shape, jnp.int32),
            pltpu.SMEM(parents.shape, jnp.int32),
            pltpu.VMEM(x.shape, BF16),
            pltpu.VMEM((jobs, 4 * rank, NRHS), BF16),
            pltpu.VMEM((2 * jobs, 2, rows, NRHS), F32),
            pltpu.SemaphoreType.DMA((4 + boxes,)),
        ],
        compiler_params=PARAMS,
        cost_estimate=COST,
        name="own",
    )(*[pltpu.with_memory_space_constraint(arg, pltpu.HBM) for arg in args])


def other_columns(mid):
    left = lax.broadcasted_iota(jnp.int32, (mid.shape[0], NRHS), 1) < HALF
    real, imag = mid[:, :NRHS], mid[:, NRHS:]
    low = jnp.where(left, real, pltpu.roll(imag, HALF, 1))
    high = jnp.where(left, pltpu.roll(real, HALF, 1), imag)
    return jnp.where(lax.axis_index("rhs") == 1, low, high)


def lower_kernel(full, halved, count_hbm, parent_hbm, *refs):
    n, m = len(full), len(halved)
    g_ref, leaf_ref, count_ref, parent_ref, sems = refs[-5:]
    outs = refs[-5 - n - m : -5]
    *xs, basis_ref, up_ref = refs[: -5 - n - m]
    copies = {
        "count": pltpu.make_async_copy(count_hbm, count_ref, sems.at[0]),
        "parent": pltpu.make_async_copy(parent_hbm, parent_ref, sems.at[1]),
    }
    for copy in copies.values():
        copy.start()

    def ready(name):
        if name in copies:
            copies[name].wait()

    def spreads(b):
        if len(xs) == 1:
            return jnp.concatenate([xs[0][b, 0], xs[0][b, 1]], axis=0)
        own, other = xs[0][b], xs[1][b]
        swap = lax.axis_index("rhs") == 1
        low, high = jnp.where(swap, other, own), jnp.where(swap, own, other)
        return jnp.concatenate([low[0], high[0], low[1], high[1]], axis=0)

    leaf_stage(spreads, all_columns, count_ref, basis_ref, g_ref, leaf_ref, ready)
    ready("parent")
    up_stage(outs[:n], full, parent_ref, up_ref, leaf_ref)
    if halved:
        up_stage(outs[n:], halved, parent_ref, up_ref, leaf_ref, other_columns)


def lower(full, halved, dests, count, parents, xs, basis, up):
    boxes, dirs, rows, _ = basis.shape
    pairs, dirs_up, rank, _ = up.shape
    shape = (pairs, dirs_up // dests, rank)
    hbm = pl.BlockSpec(memory_space=pltpu.HBM)
    vmem = pl.BlockSpec(memory_space=pltpu.VMEM)
    n = len(full) + len(halved)
    return pl.pallas_call(
        functools.partial(lower_kernel, full, halved),
        out_shape=[pltpu.VMEM(shape + (2 * NRHS,), BF16)] * len(full)
        + [pltpu.VMEM(shape + (NRHS,), BF16)] * len(halved),
        in_specs=[hbm, hbm] + [vmem] * (2 + len(xs)),
        out_specs=[vmem] * n,
        scratch_shapes=[
            pltpu.VMEM((boxes * dirs, 2, rows, NRHS), F32),
            pltpu.VMEM((pairs, dirs, 4 * rank, 2 * NRHS), BF16),
            pltpu.SMEM(count.shape, jnp.int32),
            pltpu.SMEM(parents.shape, jnp.int32),
            pltpu.SemaphoreType.DMA((2,)),
        ],
        compiler_params=PARAMS,
        cost_estimate=COST,
        name="lower",
    )(*[pltpu.with_memory_space_constraint(a, pltpu.HBM) for a in (count, parents)], *xs, basis, up)


def twist(top):
    return jnp.concatenate([-top[:, NRHS:], top[:, :NRHS]], axis=1)


def twisted_rows(tops):
    return jnp.concatenate([rows for top in tops for rows in (top, twist(top))], axis=0)


def late_groups(late, perm_ref, groups):
    found = []
    for route in late:
        source = partner(*route)
        group, child = 0, 0
        for i in range(2 * groups):
            hit = perm_ref[i] == source
            group = jnp.where(hit, i // 2, group)
            child = jnp.where(hit, i % 2, child)
        found.append((group, child))
    return found


def prep_kernel(late, perm_hbm, down_ref, row_ref, after_ref, down_out, row_out, perm_ref, sem):
    groups, local, rows = down_ref.shape[:3]
    width = row_ref.shape[4]
    fetch = pltpu.make_async_copy(perm_hbm, perm_ref, sem.at[0])
    fetch.start()
    fetch.wait()
    found = late_groups(late, perm_ref, groups)
    same = found[0][0] == found[1][0]
    for h in range(local):
        for i, (group, _) in enumerate(found):
            block = down_ref[group, h]
            for j, (_, child) in enumerate(found):
                part = jnp.where(child == 0, block[:, :width], block[:, width:])
                zeros = jnp.zeros_like(part)
                if i == 0 and j == 1:
                    part = jnp.where(same, part, zeros)
                elif i == 1:
                    part = zeros if j == 0 else jnp.where(same, zeros, part)
                down_out[h, i * rows : (i + 1) * rows, j * width : (j + 1) * width] = part
            for t in range(2):
                row_out[h, t, :, i * width : (i + 1) * width] = row_ref[h, t, group]


def prep(late, perm, down, row, after):
    local, rows = down.shape[1:3]
    leaf, width = row.shape[3:]
    vmem = pl.BlockSpec(memory_space=pltpu.VMEM)
    hbm = pl.BlockSpec(memory_space=pltpu.HBM)
    return pl.pallas_call(
        functools.partial(prep_kernel, late),
        out_shape=[
            pltpu.VMEM((local, 2 * rows, 2 * width), BF16),
            pltpu.VMEM((local, 2, leaf, 2 * width), BF16),
        ],
        in_specs=[hbm, vmem, vmem, pl.BlockSpec(memory_space=pl.ANY)],
        out_specs=[vmem] * 2,
        scratch_shapes=[pltpu.SMEM(perm.shape, jnp.int32), pltpu.SemaphoreType.DMA((1,))],
        compiler_params=PARAMS,
        cost_estimate=COST,
        name="prep",
    )(pltpu.with_memory_space_constraint(perm, pltpu.HBM), down, row, after)


def upper_kernel(full, halved, late, perm_hbm, down_ref, row_ref, *refs):
    n, m = len(full), len(halved)
    mids, own_mids, other_mids = refs[:n], refs[n : n + m], refs[n + m : n + 2 * m]
    field_ref, top_ref, spread_ref, perm_ref, sem = refs[n + 2 * m :]
    groups, local = down_ref.shape[:2]
    rank = spread_ref.shape[2] // 2
    fetch = pltpu.make_async_copy(perm_hbm, perm_ref, sem.at[0])
    fetch.start()

    def put(source, h, real, imag):
        spread_ref[source, h, :rank, :NRHS] = real
        spread_ref[source, h, :rank, NRHS:] = imag
        spread_ref[source, h, rank:, :NRHS] = -imag
        spread_ref[source, h, rank:, NRHS:] = real

    left = lax.broadcasted_iota(jnp.int32, (rank, NRHS), 1) < HALF
    for own_ref, other_ref, (k, which) in zip(own_mids, other_mids, halved):
        swap = lax.axis_index("rhs") == 1
        for h in range(local):
            low, high = own_ref[0, h].astype(F32), other_ref[0, h].astype(F32)
            low, high = jnp.where(swap, high, low), jnp.where(swap, low, high)
            real = jnp.where(left, low, pltpu.roll(high, HALF, 1)).astype(BF16)
            imag = jnp.where(left, pltpu.roll(low, HALF, 1), high).astype(BF16)
            put(partner(k, which), h, real, imag)
    for mid_ref, (k, which) in zip(mids, full):
        for h in range(local):
            mid = mid_ref[0, h]
            put(partner(k, which), h, mid[:, :NRHS], mid[:, NRHS:])
    for h in range(local):
        for route in late:
            spread_ref[partner(*route), h] = jnp.zeros(spread_ref.shape[2:], BF16)
        top_ref[1, h] = jnp.zeros(top_ref.shape[2:], F32)
    fetch.wait()
    (group_a, _), (group_b, _) = late_groups(late, perm_ref, groups)
    for h in range(local):
        tops = ([], [])
        for q in range(groups):
            parts = [spread_ref[perm_ref[2 * q + s], h] for s in range(2)]
            top = jnp.dot(
                down_ref[q, h], jnp.concatenate(parts, axis=0), preferred_element_type=F32
            )
            is_a, is_b = group_a == q, group_b == q
            top_ref[jnp.where(is_a, 0, jnp.where(is_b, 1, 2)), h] = top
            lacks = jnp.logical_or(is_a, is_b)
            top = jnp.where(lacks, jnp.zeros_like(top), top).astype(BF16)
            for t in range(2):
                tops[t].append(top[t * rank : (t + 1) * rank])
        for t in range(2):
            rows = jnp.concatenate([row_ref[h, t, q] for q in range(groups)], axis=1)
            field_ref[h, t] = jnp.dot(rows, twisted_rows(tops[t]), preferred_element_type=F32)


def upper(full, halved, late, perm, down, row, mids):
    groups, local, _, width = down.shape
    leaf = row.shape[3]
    rank = width // 4
    vmem = pl.BlockSpec(memory_space=pltpu.VMEM)
    hbm = pl.BlockSpec(memory_space=pltpu.HBM)
    return pl.pallas_call(
        functools.partial(upper_kernel, full, halved, late),
        out_shape=[
            pltpu.VMEM((local, 2, leaf, 2 * NRHS), F32),
            pltpu.VMEM((3, local, 2 * rank, 2 * NRHS), F32),
        ],
        in_specs=[hbm] + [vmem] * (2 + len(mids)),
        out_specs=[vmem] * 2,
        scratch_shapes=[
            pltpu.VMEM((2 * groups, local, 2 * rank, 2 * NRHS), BF16),
            pltpu.SMEM(perm.shape, jnp.int32),
            pltpu.SemaphoreType.DMA((1,)),
        ],
        compiler_params=PARAMS,
        cost_estimate=COST,
        name="upper",
    )(pltpu.with_memory_space_constraint(perm, pltpu.HBM), down, row, *mids)


def finish_kernel(down_ref, row_ref, field_ref, top_ref, mid_a, mid_b, out_hbm, mix_ref, out_ref, sems):
    local, _, leaf, _ = field_ref.shape
    rank = mid_a.shape[2]
    copies = []
    stretches = [group for group in (range(local - 1), range(local - 1, local)) if group]
    for i, group in enumerate(stretches):
        for h in group:
            top = jnp.concatenate([top_ref[0, h], top_ref[1, h]], axis=0) + jnp.dot(
                down_ref[h], twisted_rows([mid_a[0, h], mid_b[0, h]]), preferred_element_type=F32
            )
            top = top.astype(BF16)
            for t in range(2):
                rows = twisted_rows([top[r : r + rank] for r in (t * rank, (2 + t) * rank)])
                field = field_ref[h, t] + jnp.dot(
                    row_ref[h, t], rows, preferred_element_type=F32
                )
                mix_ref[h, t, pl.ds(0, leaf, stride=2), :] = field[:, :NRHS]
                mix_ref[h, t, pl.ds(1, leaf, stride=2), :] = field[:, NRHS:]
                out_ref[h, t] = mix_ref[h, t].astype(BF16)
        at = pl.ds(group.start, len(group))
        copies.append(pltpu.make_async_copy(out_ref.at[at], out_hbm.at[at], sems.at[i]))
        copies[-1].start()
    for copy in copies:
        copy.wait()


def finish(down, row, field, top, mids):
    local, _, leaf, _ = field.shape
    shape = (local, 2, 2 * leaf, NRHS)
    vmem = pl.BlockSpec(memory_space=pltpu.VMEM)
    return pl.pallas_call(
        finish_kernel,
        out_shape=jax.ShapeDtypeStruct(shape, BF16),
        in_specs=[vmem] * 6,
        out_specs=pl.BlockSpec(memory_space=pltpu.HBM),
        scratch_shapes=[
            pltpu.VMEM(shape, F32),
            pltpu.VMEM(shape, BF16),
            pltpu.SemaphoreType.DMA((2,)),
        ],
        compiler_params=PARAMS,
        cost_estimate=COST,
        name="finish",
    )(down, row, field, top, *mids)


def send(block, route, dests):
    code = 2 * route[0] + route[1]
    if not code:
        return block
    return lax.ppermute(block, ("blk", "sub"), [(m, m ^ code) for m in range(dests)])


def on_device(
    columns, x_panels, leaf_basis, leaf_count, parent_map, up_transfer, mid_perm, down_transfer, row_basis
):
    boxes, directions, rank, _, leaf = leaf_basis.shape
    basis = leaf_basis.reshape(boxes, directions, rank * 2, leaf)
    groups, _, local = down_transfer.shape[:3]
    down = down_transfer.reshape(groups, local, 2 * rank, 4 * rank)
    row = row_basis.reshape(local, 2, groups, leaf, 2 * rank)
    x = jnp.transpose(x_panels, (0, 2, 3, 1))
    dests = 2 * columns
    two = both_cores((2,))
    full = both_cores(range(columns - 1, 3, -1)) + [(3, 0), (1, 0), (0, 1), (0, 0)]
    late = [(1, 1), (3, 1)]
    if 2 * x.shape[2] == NRHS:
        halved = two
        xs = [x, lax.ppermute(x, "rhs", [(0, 1), (1, 0)])]
        *own_mids, basis, up = own(halved, dests, leaf_count, parent_map, x, basis, up_transfer)
        own_mids = [send(mid, route, dests) for mid, route in zip(own_mids, halved)]
    else:
        full, halved, own_mids, up = two + full, [], [], up_transfer
        xs = [lax.all_gather(x, "rhs", axis=2, tiled=True)]
    n = len(full)
    routes = full + late + halved
    mids = lower(full + late, halved, dests, leaf_count, parent_map, xs, basis, up)
    mids = [send(mid, route, dests) for mid, route in zip(mids, routes)]
    down_late, row_late = prep(late, mid_perm, down, row, [*own_mids, mids[0]][0])
    field, top = upper(
        full, halved, late, mid_perm, down, row, [*mids[:n], *own_mids, *mids[n + 2 :]]
    )
    result = finish(down_late, row_late, field, top, mids[n : n + 2])
    return result.reshape(1, local, 2, leaf, 2, NRHS)


def solution(mesh):
    return jax.shard_map(
        functools.partial(on_device, mesh.shape["blk"]),
        mesh=mesh,
        in_specs=(
            P(("grp", "blk", "sub"), None, None, "rhs"),
            P(("blk", "sub"), "rhs", None, None, None),
            P(("blk", "sub")),
            P("rhs"),
            P(("blk", "sub"), "rhs", None, None),
            P(),
            P(None, "rhs", ("blk", "sub"), None, None, None),
            P("rhs", ("blk", "sub"), None, None, None, None),
        ),
        out_specs=P(("grp", "rhs"), ("blk", "sub"), None, None, None, None),
        check_vma=False,
    )
```
